32 devices in a mesh: node: 8 (over z, y), mp: 4 (over x, core).
Axes of the slice: x: 2, y: 2, z: 4, core: 2. Of those that a mesh axis runs over, the one named last changes fastest.
Arguments:
- features: bfloat16 [49152, 2048], P('node', 'mp'), may hold values from -6 to 6
- weight: float32 [2048, 2048], P(None, 'mp'), may hold values from -0.125 to 0.125
- scale: float32 [2048], P('mp'), may hold values from 0.5 to 1.5
- shift: float32 [2048], P('mp'), may hold values from -3 to 3
- cotangent: bfloat16 [49152, 2048], P('node', 'mp'), may hold values from -6 to 6
- neighbours: int32 [49152, 16], P('node'), may hold values from 0 to 128, as said below
- halo_links: int32 [49152, 4], P('node'), may hold values from 0 to 256, as said below
- valid_rows: int32 [49152], P('node'), may hold values from 0 to 1, as said below
- send_rows: int32 [1024, 2], P('node'), may hold values from 0 to 6143
Outputs:
- activations: float32 [49152, 2048], P('node', 'mp')
- input_grad: float32 [49152, 2048], P('node', 'mp')
- weight_grad: float32 [2048, 2048], P(None, 'mp')
- scale_grad: float32 [2048], P('mp')
- shift_grad: float32 [2048], P('mp')
The draws below stay inside these ranges and needn't reach their ends.
Inputs may be any that keep to these rules, and one draw needn't show every extreme that they name: `neighbours`: values below 128 name a row of the node's own slot; the value 128 marks an empty entry. `halo_links`: values below 128 name a row received from the lower node block, values from 128 to 255 one from the upper block; 256 marks an empty entry. `valid_rows`: the valid rows of each slot are a prefix of it, at least half of the slot.
All inputs are finite; a program needn't handle non-finite values.
Results may differ from the reference program's by a relative error of at most 0.0059.
Values may be sent and summed in bfloat16 or wider, within the bound.
A program may use at most 320 MiB of HBM per device.

```python
import jax
import jax.numpy as jnp
from jax import lax

F = 2048
SLOT = 128
HB = 128
KI = 16
KH = 4
ROWS_DEV = 6144
NODES = 49152
N_NODE = 8


def draw_neighbours(key, part):
    key = jax.random.fold_in(key, 11)
    picked = jax.random.randint(key, (NODES, KI), 0, SLOT + SLOT // 4, dtype=jnp.int32)
    return jnp.minimum(picked, SLOT)


def draw_halo_links(key, part):
    key = jax.random.fold_in(key, 12)
    picked = jax.random.randint(key, (NODES, KH), 0, 4 * HB, dtype=jnp.int32)
    return jnp.minimum(picked, 2 * HB)


def draw_valid_rows(key, part):
    key = jax.random.fold_in(key, 13)
    lengths = jax.random.randint(key, (NODES // SLOT, 1), SLOT // 2, SLOT + 1, dtype=jnp.int32)
    places = jnp.arange(SLOT, dtype=jnp.int32)[None, :]
    return (places < lengths).astype(jnp.int32).reshape(NODES)


def set_ends(drawn, own_key, smallest, top_value):
    longest = drawn.shape.index(max(drawn.shape))
    spots = []
    for shift in (0, 1):
        where = [jax.random.randint(jax.random.fold_in(own_key, axis), (), 0, length) for axis, length in enumerate(drawn.shape)]
        where[longest] = (where[longest] + shift) % drawn.shape[longest]
        spots.append(tuple(where))
    return drawn.at[spots[0]].set(smallest).at[spots[1]].set(top_value)


def block_scale(own_key, shape, cuts, smallest, high):
    factor_of, own = 1.0, jax.random.fold_in(own_key, 6)
    for position, shards_of in cuts:
        steps = jnp.exp(jax.random.uniform(jax.random.fold_in(own, position), (shards_of,), jnp.float32, smallest / len(cuts), high / len(cuts)))
        factor_of = factor_of * jnp.repeat(steps, shape[position] // shards_of).reshape([-1 if axis == position else 1 for axis in range(len(shape))])
    return factor_of


def bell_draw(rng, extent, spread, reach, split=(), kind=jnp.bfloat16):
    drawn = jax.random.normal(rng, extent, jnp.float32) * spread
    if len(split) > 0:
        drawn = block_scale(rng, extent, split, -0.22, 0.18) * drawn
    return jnp.clip(drawn, min=-reach, max=reach).astype(kind)


def setup_inputs(seed: int = 0) -> dict:
    seeds = jax.random.split(jax.random.key(seed), 10)
    return {
        "features": bell_draw(seeds[0], (NODES, F), 1.0, 6.0, ((0, 8), (1, 4))),
        "weight": bell_draw(seeds[1], (F, F), F ** -0.5, 0.125, ((1, 4),), jnp.float32),
        "scale": jnp.clip(1.0 + 0.1 * jax.random.normal(seeds[2], (F,), jnp.float32), 0.5, 1.5),
        "shift": bell_draw(seeds[3], (F,), 0.5, 3.0, ((0, 4),), jnp.float32),
        "cotangent": bell_draw(seeds[4], (NODES, F), 1.0, 6.0, ((0, 8), (1, 4))),
        "neighbours": draw_neighbours(jax.random.fold_in(seeds[9], 71), 0),
        "halo_links": draw_halo_links(jax.random.fold_in(seeds[9], 71), 0),
        "valid_rows": draw_valid_rows(jax.random.fold_in(seeds[9], 71), 0),
        "send_rows": set_ends(jax.random.randint(seeds[8], (HB * N_NODE, 2), 0, ROWS_DEV), jax.random.fold_in(seeds[8], 1), 0, ROWS_DEV - 1).astype(jnp.int32),
    }


epsilon = 1e-05

@jax.custom_vjp
def low(v):
    return lax.optimization_barrier(v.astype(jnp.bfloat16)).astype(jnp.float32)

@jax.custom_vjp
def low_back(v):
    return v

def low_keep(v):
    return (low(v), None)

def low_pass(kept, grad):
    return (grad,)

def back_keep(v):
    return (v, None)

def back_low(kept, grad):
    return (low(grad),)
low.defvjp(low_keep, low_pass)
low_back.defvjp(back_keep, back_low)

def adjacency(neighbours, halo_links, slot_size, link_width):
    row_count = neighbours.shape[0]
    columns = jnp.arange(slot_size, dtype=jnp.int32)
    link_cols = jnp.arange(link_width, dtype=jnp.int32)
    counted = jnp.zeros((row_count, slot_size), jnp.float32)
    for entry in range(neighbours.shape[1]):
        counted = counted + (neighbours[:, entry:entry + 1] == columns[None, :]).astype(jnp.float32)
    linked = jnp.zeros((row_count, link_width), jnp.float32)
    for entry in range(halo_links.shape[1]):
        linked = linked + (halo_links[:, entry:entry + 1] == link_cols[None, :]).astype(jnp.float32)
    present = lax.optimization_barrier(jnp.sum((neighbours < slot_size).astype(jnp.float32), 1)) + lax.optimization_barrier(jnp.sum((halo_links < link_width).astype(jnp.float32), 1))
    degree = 1.0 + present
    places = jnp.arange(row_count, dtype=jnp.int32) % slot_size
    own_col = (places[:, None] == columns[None, :]).astype(jnp.float32)
    self_count = lax.optimization_barrier(jnp.sum(counted * own_col, 1))
    tiles = (counted + (self_count + 2.0)[:, None] * own_col) / degree[:, None]
    return (tiles.reshape(row_count // slot_size, slot_size, slot_size), linked / degree[:, None])

def reference(features, weight, scale, shift, cotangent, neighbours, halo_links, valid_rows, send_rows):
    mask_col = valid_rows.astype(jnp.float32)[:, None]
    tiles, hlink = adjacency(neighbours, halo_links, SLOT, 2 * HB)
    hlink = hlink.reshape(N_NODE, ROWS_DEV, 2 * HB)
    sends = send_rows.reshape(N_NODE, HB, 2)
    highest = lax.Precision.HIGHEST

    def forward(inputs, matrix, gain, bias):
        masked = inputs * mask_col
        blocks = masked.reshape(N_NODE, ROWS_DEV, F)
        picker = jax.vmap(lambda block, index: block[index])
        to_lower = picker(blocks, sends[:, :, 0])
        to_upper = picker(blocks, sends[:, :, 1])
        empty = jnp.zeros((1, HB, F), jnp.float32)
        below = jnp.concatenate([empty, to_upper[:-1]], 0)
        above = jnp.concatenate([to_lower[1:], empty], 0)
        received = jnp.concatenate([below, above], 1)
        inner = jnp.einsum('sij,sjf->sif', tiles, masked.reshape(-1, SLOT, F), precision=highest).reshape(NODES, F)
        outer = jnp.einsum('prh,phf->prf', hlink, received, precision=highest).reshape(NODES, F)
        aggregated = low(low_back(inner + outer))
        linear = low_back(jnp.dot(aggregated, low(matrix), precision=highest))
        total = jnp.sum(mask_col)
        mean_val = lax.optimization_barrier(jnp.sum(linear * mask_col, 0)) / total
        centred = linear - mean_val
        variance = lax.optimization_barrier(jnp.sum(centred * centred * mask_col, 0)) / total
        normed = centred * lax.rsqrt(variance + epsilon)
        return jax.nn.gelu(gain * normed + bias) * mask_col
    outputs, pullback = jax.vjp(forward, features.astype(jnp.float32), weight, scale, shift)
    input_grad, weight_grad, scale_grad, shift_grad = pullback(cotangent.astype(jnp.float32))
    return (outputs, input_grad, weight_grad, scale_grad, shift_grad)
```

```python
import functools

import jax
import jax.numpy as jnp
from jax import lax
from jax.experimental import pallas as pl
from jax.experimental.pallas import tpu as pltpu
from jax.sharding import PartitionSpec as P

SLOT = 128
LANE = 128
GROUP = 4
epsilon = 1e-05
VMEM_BYTES = 56 * 1024 * 1024
MESH = pl.DeviceIdType.MESH
f32, bf16, i32 = jnp.float32, jnp.bfloat16, jnp.int32


def params(**extra):
    return pltpu.CompilerParams(vmem_limit_bytes=VMEM_BYTES, **extra)


def whole():
    return pl.BlockSpec(memory_space=pltpu.VMEM)


def smem():
    return pl.BlockSpec(memory_space=pltpu.SMEM)


def fixed(shape):
    return pl.BlockSpec(shape, lambda i: (0,) * len(shape), pipeline_mode=pl.Buffered(1))


def cost(flops, moved, trans=0):
    return pl.CostEstimate(flops=int(flops), bytes_accessed=int(moved), transcendentals=int(trans))


def dot(a, b, ca=1, cb=0):
    return lax.dot_general(a, b, (((ca,), (cb,)), ((), ())), preferred_element_type=f32)


def row_tile(rows, most):
    tile = most - most % 16
    while rows % tile:
        tile -= 16
    return tile


def chosen(rows_ref, base, count, valid):
    width = rows_ref.shape[1]
    place = lax.broadcasted_iota(i32, (count, width), 0)
    hit = (rows_ref[...] == place + base) & (place < valid)
    return jnp.where(hit, 1.0, 0.0).astype(bf16)


def pick_rows(features, send_row, counts):
    rows, width = features.shape
    sends = send_row.shape[1]
    steps = rows // (GROUP * SLOT)

    def kernel(counts_ref, feat_ref, send_ref, out_ref, total):
        step = pl.program_id(0)

        @pl.when(step == 0)
        def _():
            total[...] = jnp.zeros_like(total)

        for part in range(GROUP):
            slot = step * GROUP + part
            hot = chosen(send_ref, slot * SLOT, SLOT, counts_ref[slot])
            total[...] += dot(hot, feat_ref[part * SLOT : (part + 1) * SLOT, :], 0, 0)

        @pl.when(step == steps - 1)
        def _():
            out_ref[...] = total[...].astype(bf16)

    return pl.pallas_call(
        kernel,
        grid=(steps,),
        out_shape=jax.ShapeDtypeStruct((sends, width), bf16),
        in_specs=[
            smem(),
            pl.BlockSpec((GROUP * SLOT, width), lambda i: (i, 0)),
            fixed((1, sends)),
        ],
        out_specs=fixed((sends, width)),
        scratch_shapes=[pltpu.VMEM((sends, width), f32)],
        compiler_params=params(),
        cost_estimate=cost(2 * rows * sends * width, 2 * rows * width),
        name="pick_rows",
    )(counts, features, send_row)


def count_tiles(near, links, counts):
    entries, rows = near.shape
    link_entries = links.shape[0]
    slots = rows // SLOT

    def kernel(counts_ref, near_ref, link_ref, tile_ref, inv_ref):
        step = pl.program_id(0)
        row = lax.broadcasted_iota(i32, (SLOT, SLOT), 0)
        column = lax.broadcasted_iota(i32, (SLOT, SLOT), 1)
        link_row = lax.broadcasted_iota(i32, (2 * SLOT, SLOT), 0)
        for part in range(GROUP):
            lanes = slice(part * SLOT, (part + 1) * SLOT)
            counted = jnp.zeros((SLOT, SLOT), f32)
            for entry in range(entries):
                counted += jnp.where(near_ref[entry : entry + 1, lanes] == row, 1.0, 0.0)
            linked = jnp.zeros((2 * SLOT, SLOT), f32)
            for entry in range(link_entries):
                linked += jnp.where(link_ref[entry : entry + 1, lanes] == link_row, 1.0, 0.0)
            degree = (
                1.0
                + jnp.sum(counted, 0, keepdims=True)
                + jnp.sum(linked, 0, keepdims=True)
            )
            tile = counted + jnp.where(row == column, counted + 2.0, 0.0)
            tile = jnp.where(row < counts_ref[step * GROUP + part], tile, 0.0)
            tile_ref[part, :SLOT, :] = tile.astype(bf16)
            tile_ref[part, SLOT:, :] = linked.astype(bf16)
            inv_ref[part] = jnp.broadcast_to(1.0 / degree, (8, SLOT))

    return pl.pallas_call(
        kernel,
        grid=(slots // GROUP,),
        out_shape=[
            jax.ShapeDtypeStruct((slots, 3 * SLOT, SLOT), bf16),
            jax.ShapeDtypeStruct((slots, 8, SLOT), f32),
        ],
        in_specs=[
            smem(),
            pl.BlockSpec((entries, GROUP * SLOT), lambda i: (0, i)),
            pl.BlockSpec((link_entries, GROUP * SLOT), lambda i: (0, i)),
        ],
        out_specs=[
            pl.BlockSpec((GROUP, 3 * SLOT, SLOT), lambda i: (i, 0, 0)),
            pl.BlockSpec((GROUP, 8, SLOT), lambda i: (i, 0, 0)),
        ],
        compiler_params=params(),
        cost_estimate=cost(rows * 12000, 6 * rows * SLOT),
        name="count_tiles",
    )(counts, near, links)


def column_of(inv_ref, slot):
    return jnp.transpose(jnp.broadcast_to(inv_ref[slot, 0:1, :], (SLOT, SLOT)))


def aggregate(tiles, inv, features, halo, offsets, counts, first, rows):
    slots = tiles.shape[0]
    width = features.shape[1]
    quarter = width // LANE

    def kernel(off_ref, counts_ref, tile_ref, inv_ref, feat_ref, halo_ref, out_ref, held):
        def step(slot, carry):
            start = off_ref[slot]

            @pl.when((start < first + rows) & (start + counts_ref[slot] > first))
            def _():
                source = pl.ds(pl.multiple_of(slot * SLOT, SLOT), SLOT)
                tile = tile_ref[slot]
                total = dot(tile[:SLOT], feat_ref[source, :], 0, 0)
                total += dot(tile[SLOT:], halo_ref[...], 0, 0)
                scale = column_of(inv_ref, slot)
                for q in range(quarter):
                    held[q, pl.ds(start - first + SLOT, SLOT), :] = (
                        total[:, q * LANE : (q + 1) * LANE] * scale
                    )

            return carry

        lax.fori_loop(0, slots, step, 0)
        total_rows = off_ref[slots]
        for part in range(rows // row_tile(rows, 256)):
            size = row_tile(rows, 256)
            live = (
                lax.broadcasted_iota(i32, (size, LANE), 0) + (first + part * size) < total_rows
            )
            for q in range(quarter):
                out_ref[part * size : (part + 1) * size, q * LANE : (q + 1) * LANE] = jnp.where(
                    live, held[q, SLOT + part * size : SLOT + (part + 1) * size, :], 0.0
                ).astype(bf16)

    return pl.pallas_call(
        kernel,
        out_shape=jax.ShapeDtypeStruct((rows, width), bf16),
        in_specs=[smem(), smem(), whole(), whole(), whole(), whole()],
        out_specs=whole(),
        scratch_shapes=[pltpu.VMEM((quarter, rows + 2 * SLOT, LANE), f32)],
        compiler_params=params(),
        cost_estimate=cost(2 * rows * 3 * SLOT * width, 2 * features.size + tiles.size * 2),
        name="aggregate",
    )(offsets, counts, tiles, inv, features, halo)


def partial_product(own, sib, w_own, w_sib, block, width):
    rows, depth = own.shape
    tile = row_tile(rows, 512)

    def kernel(a_ref, b_ref, wa_ref, wb_ref, out_ref):
        out_ref[...] = (dot(a_ref[...], wa_ref[...]) + dot(b_ref[...], wb_ref[...])).astype(bf16)

    return pl.pallas_call(
        kernel,
        grid=(rows // tile,),
        out_shape=jax.ShapeDtypeStruct((rows, width), bf16),
        in_specs=[pl.BlockSpec((tile, depth), lambda i: (i, 0))] * 2
        + [pl.BlockSpec((depth, width), lambda i: (0, block))] * 2,
        out_specs=pl.BlockSpec((tile, width), lambda i: (i, 0)),
        compiler_params=params(),
        cost_estimate=cost(4 * rows * depth * width, 4 * rows * depth + 2 * rows * width),
        name="partial_product",
    )(own, sib, w_own, w_sib)


def linear_stats(own, sib, w_own, w_sib, received, offsets, slots, block, width):
    rows, depth = own.shape
    tile = row_tile(rows, 512)
    parts = width // LANE
    others = len(received)

    def kernel(off_ref, a_ref, b_ref, wa_ref, wb_ref, *rest):
        recv_refs, (lin_ref, stat_ref) = rest[:others], rest[others:]
        step = pl.program_id(0)

        @pl.when(step == 0)
        def _():
            stat_ref[...] = jnp.zeros_like(stat_ref)

        value = dot(a_ref[...], wa_ref[...]) + dot(b_ref[...], wb_ref[...])
        for ref in recv_refs:
            value += ref[...].astype(f32)
        for part in range(parts):
            lin_ref[part] = value[:, part * LANE : (part + 1) * LANE]
        total = off_ref[slots]
        before = jnp.minimum(step * tile, total)
        here = jnp.minimum(step * tile + tile, total) - before
        seen, new = before.astype(f32), here.astype(f32)
        both = jnp.full((1, width), jnp.maximum(seen + new, 1.0), f32)
        live = lax.broadcasted_iota(i32, (tile, width), 0) < here
        mean_here = jnp.sum(jnp.where(live, value, 0.0), 0, keepdims=True) / jnp.full(
            (1, width), jnp.maximum(new, 1.0), f32
        )
        centred = jnp.where(live, value - mean_here, 0.0)
        squares = jnp.sum(centred * centred, 0, keepdims=True)
        mean, held = stat_ref[0:1, :], stat_ref[1:2, :]
        gap = mean_here - mean
        ratio = new / both
        stat_ref[0:1, :] = mean + gap * ratio
        stat_ref[1:2, :] = held + squares + gap * gap * (seen * ratio)
        stat_ref[2:3, :] = jnp.full((1, width), total.astype(f32), f32)

    return pl.pallas_call(
        kernel,
        grid=(rows // tile,),
        out_shape=[
            jax.ShapeDtypeStruct((parts, rows + SLOT, LANE), f32),
            jax.ShapeDtypeStruct((8, width), f32),
        ],
        in_specs=[smem()]
        + [pl.BlockSpec((tile, depth), lambda i: (i, 0))] * 2
        + [pl.BlockSpec((depth, width), lambda i: (0, block))] * 2
        + [pl.BlockSpec((tile, width), lambda i: (i, 0))] * others,
        out_specs=[
            pl.BlockSpec((parts, tile, LANE), lambda i: (0, i, 0)),
            pl.BlockSpec((8, width), lambda i: (0, 0)),
        ],
        compiler_params=params(),
        cost_estimate=cost(4 * rows * depth * width, 4 * rows * depth + 6 * rows * width),
        name="linear_stats",
    )(offsets, own, sib, w_own, w_sib, *received)


def exchange(block, nodes):
    def kernel(in_ref, out_ref, held, send_sem, recv_sem):
        me = lax.axis_index("node")
        barrier = pltpu.get_barrier_semaphore()
        for step in range(1, nodes):
            pl.semaphore_signal(
                barrier,
                inc=1,
                device_id={"node": lax.rem(me + step, nodes)},
                device_id_type=MESH,
            )
        pl.semaphore_wait(barrier, nodes - 1)
        copies = []
        for step in range(1, nodes):
            copy = pltpu.make_async_remote_copy(
                src_ref=in_ref,
                dst_ref=held.at[step],
                send_sem=send_sem.at[step],
                recv_sem=recv_sem.at[step],
                device_id={"node": lax.rem(me + step, nodes)},
                device_id_type=MESH,
            )
            copy.start()
            copies.append(copy)
        out_ref[0] = in_ref[...]
        for copy in copies:
            copy.wait()
        for step in range(1, nodes):
            out_ref[step] = held[step]

    return pl.pallas_call(
        kernel,
        out_shape=jax.ShapeDtypeStruct((nodes,) + block.shape, f32),
        in_specs=[whole()],
        out_specs=whole(),
        scratch_shapes=[
            pltpu.VMEM((nodes,) + block.shape, f32),
            pltpu.SemaphoreType.DMA((nodes,)),
            pltpu.SemaphoreType.DMA((nodes,)),
        ],
        compiler_params=params(collective_id=1, has_side_effects=True),
        cost_estimate=cost(0, nodes * block.size * 4),
        name="exchange",
    )(block)


def merge_stats(stat_ref, width):
    nodes = stat_ref.shape[0]
    total = stat_ref[0, 2:3, :width]
    for node in range(1, nodes):
        total += stat_ref[node, 2:3, :width]
    mean = stat_ref[0, 2:3, :width] * stat_ref[0, 0:1, :width]
    for node in range(1, nodes):
        mean += stat_ref[node, 2:3, :width] * stat_ref[node, 0:1, :width]
    mean = mean / total
    spread = jnp.zeros_like(mean)
    for node in range(nodes):
        gap = stat_ref[node, 0:1, :width] - mean
        spread += stat_ref[node, 1:2, :width] + stat_ref[node, 2:3, :width] * gap * gap
    return total, mean, lax.rsqrt(spread / total + epsilon)


def activate(
    linear, stats, scale, shift, cotangent, offsets, counts, held, block, width, rows, feat_width
):
    nodes = stats.shape[0]
    slots = rows // SLOT
    parts = width // LANE
    compact = linear.shape[1]
    slope = 0.7978845608028654
    cubic = 0.044715

    def kernel(off_ref, counts_ref, lin_ref, stat_ref, scale_ref, shift_ref, cot_ref, *rest):
        act_ref, grad_ref, sum_ref, norm = rest[-4:]
        step = pl.program_id(0)

        @pl.when(step == 0)
        def _():
            _, mean, rstd = merge_stats(stat_ref, width)
            norm[0:1, :] = mean
            norm[1:2, :] = rstd
            sum_ref[...] = jnp.zeros_like(sum_ref)

        for part in range(parts):
            lanes = slice(part * LANE, (part + 1) * LANE)
            mean, rstd = norm[0:1, lanes], norm[1:2, lanes]
            gain, bias = scale_ref[:, lanes], shift_ref[:, lanes]
            first = jnp.zeros((8, LANE), f32)
            second = jnp.zeros((8, LANE), f32)
            for member in range(GROUP):
                slot = step * GROUP + member
                start = off_ref[slot]
                rows_here = slice(member * SLOT, (member + 1) * SLOT)
                live = lax.broadcasted_iota(i32, (SLOT, LANE), 0) < counts_ref[slot]
                value = jnp.where(live, lin_ref[part, pl.ds(start, SLOT), :], 0.0)
                normed = (value - mean) * rstd
                z = gain * normed + bias
                square = z * z
                bent = jnp.tanh(slope * z * (1.0 + cubic * square))
                half = 0.5 + 0.5 * bent
                act_ref[rows_here, lanes] = jnp.where(live, z * half, 0.0)
                back = half + (0.5 * slope) * z * (1.0 - bent * bent) * (
                    1.0 + (3.0 * cubic) * square
                )
                grad = jnp.where(live, cot_ref[rows_here, lanes].astype(f32) * back, 0.0)
                grad_ref[part, pl.ds(start, SLOT), :] = grad
                first += jnp.sum((grad * normed).reshape(SLOT // 8, 8, LANE), 0)
                second += jnp.sum(grad.reshape(SLOT // 8, 8, LANE), 0)
            sum_ref[0:1, lanes] += jnp.sum(first, 0, keepdims=True)
            sum_ref[1:2, lanes] += jnp.sum(second, 0, keepdims=True)

    given = [] if held is None else [held]
    return pl.pallas_call(
        kernel,
        grid=(slots // GROUP,),
        out_shape=[
            jax.ShapeDtypeStruct((rows, feat_width), f32),
            jax.ShapeDtypeStruct((parts, compact, LANE), f32),
            jax.ShapeDtypeStruct((8, width), f32),
        ],
        in_specs=[
            smem(),
            smem(),
            fixed((parts, compact, LANE)),
            fixed(stats.shape),
            pl.BlockSpec((1, width), lambda i: (0, block)),
            pl.BlockSpec((1, width), lambda i: (0, block)),
            pl.BlockSpec((GROUP * SLOT, width), lambda i: (i, block)),
        ]
        + [pl.BlockSpec(memory_space=pl.ANY)] * len(given),
        out_specs=[
            pl.BlockSpec((GROUP * SLOT, width), lambda i: (i, block)),
            fixed((parts, compact, LANE)),
            pl.BlockSpec((8, width), lambda i: (0, 0)),
        ],
        scratch_shapes=[pltpu.VMEM((8, width), f32)],
        input_output_aliases={7: 0} if given else {},
        compiler_params=params(),
        cost_estimate=cost(60 * rows * width, 14 * rows * width, rows * width),
        name="activate",
    )(offsets, counts, linear, stats, scale, shift, cotangent, *given)


def linear_grad(linear, grad, stats, sums, scale, offsets, slots, block, width):
    parts, padded, _ = linear.shape
    rows = padded - SLOT
    tile = row_tile(rows, 512)
    nodes = stats.shape[0]

    def kernel(off_ref, lin_ref, grad_ref, stat_ref, sums_ref, scale_ref, out_ref, total_ref, norm):
        step = pl.program_id(0)

        @pl.when(step == 0)
        def _():
            total, mean, rstd = merge_stats(stat_ref, width)
            by_gain = sums_ref[0, 0:1, :width]
            by_bias = sums_ref[0, 1:2, :width]
            for node in range(1, nodes):
                by_gain += sums_ref[node, 0:1, :width]
                by_bias += sums_ref[node, 1:2, :width]
            norm[0:1, :] = mean
            norm[1:2, :] = rstd
            norm[2:3, :] = by_gain / total
            norm[3:4, :] = by_bias / total
            norm[4:5, :] = rstd * scale_ref[...]
            total_ref[...] = jnp.zeros_like(total_ref)
            total_ref[0:1, :] = by_gain
            total_ref[1:2, :] = by_bias

        live = lax.broadcasted_iota(i32, (tile, LANE), 0) + step * tile < off_ref[slots]
        for part in range(parts):
            lanes = slice(part * LANE, (part + 1) * LANE)
            normed = (lin_ref[part] - norm[0:1, lanes]) * norm[1:2, lanes]
            value = norm[4:5, lanes] * (
                grad_ref[part] - norm[3:4, lanes] - normed * norm[2:3, lanes]
            )
            out_ref[:, lanes] = jnp.where(live, value, 0.0).astype(bf16)

    return pl.pallas_call(
        kernel,
        grid=(rows // tile,),
        out_shape=[
            jax.ShapeDtypeStruct((rows, width), bf16),
            jax.ShapeDtypeStruct((8, width), f32),
        ],
        in_specs=[
            smem(),
            pl.BlockSpec((parts, tile, LANE), lambda i: (0, i, 0)),
            pl.BlockSpec((parts, tile, LANE), lambda i: (0, i, 0)),
            fixed(stats.shape),
            fixed(sums.shape),
            pl.BlockSpec((1, width), lambda i: (0, block)),
        ],
        out_specs=[
            pl.BlockSpec((tile, width), lambda i: (i, 0)),
            pl.BlockSpec((8, width), lambda i: (0, 0)),
        ],
        scratch_shapes=[pltpu.VMEM((8, width), f32)],
        compiler_params=params(),
        cost_estimate=cost(10 * rows * width, 10 * rows * width),
        name="linear_grad",
    )(offsets, linear, grad, stats, sums, scale)


def grad_products(grads, weights, held, block, width):
    rows = grads[0].shape[0]
    feat_width = weights[0].shape[0]
    parts = feat_width // LANE
    tile = row_tile(rows, 512)
    count = len(grads)
    given = [] if held is None else [held]

    def kernel(*refs):
        out_ref = refs[-1]
        left = jnp.concatenate([ref[...] for ref in refs[:count]], 1)
        right = jnp.concatenate([ref[...] for ref in refs[count : 2 * count]], 1)
        value = dot(left, right, 1, 1)
        for part in range(parts):
            piece = value[:, part * LANE : (part + 1) * LANE]
            if given:
                piece = piece + refs[2 * count][part]
            out_ref[part] = piece

    def stripe():
        return pl.BlockSpec((parts, tile, LANE), lambda i: (0, i, 0))

    return pl.pallas_call(
        kernel,
        grid=(rows // tile,),
        out_shape=jax.ShapeDtypeStruct((parts, rows + SLOT, LANE), f32),
        in_specs=[pl.BlockSpec((tile, width), lambda i: (i, 0))] * count
        + [pl.BlockSpec((feat_width, width), lambda i: (0, block))] * count
        + [stripe()] * len(given),
        out_specs=stripe(),
        input_output_aliases={2 * count: 0} if given else {},
        compiler_params=params(),
        cost_estimate=cost(
            2 * rows * feat_width * width * count, rows * (8 * feat_width + 2 * count * width)
        ),
        name="grad_products",
    )(*grads, *weights, *given)


def slot_grads(grad, tiles, inv, offsets, counts):
    slots = tiles.shape[0]
    parts, padded, _ = grad.shape
    width = parts * LANE
    steps = slots // GROUP

    def kernel(off_ref, counts_ref, grad_ref, tile_ref, inv_ref, out_ref, halo_ref, total):
        step = pl.program_id(0)

        @pl.when(step == 0)
        def _():
            total[...] = jnp.zeros_like(total)

        pieces = []
        for member in range(GROUP):
            slot = step * GROUP + member
            start = off_ref[slot]
            live = lax.broadcasted_iota(i32, (SLOT, LANE), 0) < counts_ref[slot]
            scale = column_of(inv_ref, member)
            row = []
            for part in range(parts):
                value = grad_ref[part, pl.ds(start, SLOT), :].astype(bf16).astype(f32)
                row.append(jnp.where(live, value * scale, 0.0).astype(bf16))
            piece = jnp.concatenate(row, 1)
            out_ref[member * SLOT : (member + 1) * SLOT, :] = piece
            pieces.append(piece)
        link = jnp.concatenate([tile_ref[member, SLOT:, :] for member in range(GROUP)], 1)
        total[...] += dot(link, jnp.concatenate(pieces, 0))

        @pl.when(step == steps - 1)
        def _():
            halo_ref[...] = total[...].astype(bf16)

    return pl.pallas_call(
        kernel,
        grid=(steps,),
        out_shape=[
            jax.ShapeDtypeStruct((slots * SLOT, width), bf16),
            jax.ShapeDtypeStruct((2 * SLOT, width), bf16),
        ],
        in_specs=[
            smem(),
            smem(),
            fixed((parts, padded, LANE)),
            pl.BlockSpec((GROUP, 3 * SLOT, SLOT), lambda i: (i, 0, 0)),
            pl.BlockSpec((GROUP, 8, SLOT), lambda i: (i, 0, 0)),
        ],
        out_specs=[
            pl.BlockSpec((GROUP * SLOT, width), lambda i: (i, 0)),
            fixed((2 * SLOT, width)),
        ],
        scratch_shapes=[pltpu.VMEM((2 * SLOT, width), f32)],
        compiler_params=params(),
        cost_estimate=cost(4 * slots * SLOT * SLOT * width, 6 * slots * SLOT * width),
        name="slot_grads",
    )(offsets, counts, grad, tiles, inv)


def input_grads(slot_grad, tiles, returned, send_row, counts):
    rows, width = slot_grad.shape
    sends = send_row.shape[1]

    def kernel(counts_ref, grad_ref, tile_ref, back_ref, send_ref, out_ref):
        step = pl.program_id(0)
        for member in range(GROUP):
            slot = step * GROUP + member
            here = slice(member * SLOT, (member + 1) * SLOT)
            hot = chosen(send_ref, slot * SLOT, SLOT, counts_ref[slot])
            value = dot(tile_ref[member, :SLOT, :], grad_ref[here, :])
            out_ref[here, :] = value + dot(hot, back_ref[...])

    return pl.pallas_call(
        kernel,
        grid=(rows // (GROUP * SLOT),),
        out_shape=jax.ShapeDtypeStruct((rows, width), f32),
        in_specs=[
            smem(),
            pl.BlockSpec((GROUP * SLOT, width), lambda i: (i, 0)),
            pl.BlockSpec((GROUP, SLOT, SLOT), lambda i: (i, 0, 0)),
            fixed((sends, width)),
            fixed((1, sends)),
        ],
        out_specs=pl.BlockSpec((GROUP * SLOT, width), lambda i: (i, 0)),
        compiler_params=params(),
        cost_estimate=cost(2 * rows * 3 * SLOT * width, 6 * rows * width),
        name="input_grads",
    )(counts, slot_grad, tiles, returned, send_row)


def node_shift(block, distance):
    nodes = range(lax.axis_size("node"))
    return lax.ppermute(
        block, "node", [(i - distance, i) for i in nodes if i - distance in nodes]
    )


def to_sibling(block):
    return lax.ppermute(block, "mp", [(i, i ^ 1) for i in range(lax.axis_size("mp"))])


def to_chip(block, distance):
    size = lax.axis_size("mp")
    return lax.ppermute(block, "mp", [(i, (i + 2 * distance) % size) for i in range(size)])


def node_flip(block, bit):
    return lax.ppermute(block, "node", [(i, i ^ bit) for i in range(lax.axis_size("node"))])


def scatter_sum(value, axis):
    me, bit = lax.axis_index("node"), 1
    while bit < lax.axis_size("node"):
        mine = lax.rem(me // bit, 2)
        half = value.shape[axis] // 2
        keep = lax.dynamic_slice_in_dim(value, mine * half, half, axis)
        give = lax.dynamic_slice_in_dim(value, (1 - mine) * half, half, axis)
        value = keep + node_flip(give, bit)
        bit *= 2
    return value


def gather_shares(value, axis):
    me, bit = lax.axis_index("node"), lax.axis_size("node") // 2
    while bit >= 1:
        mine = lax.rem(me // bit, 2)
        other = node_flip(value, bit)
        low = jnp.where(mine == 0, value, other)
        high = jnp.where(mine == 0, other, value)
        value = jnp.concatenate([low, high], axis)
        bit //= 2
    return value


def blocks_of(width):
    if width % 512 == 0:
        sizes = [width // 2, width // 4, width // 4]
    else:
        sizes = [width // 2, width // 2]
    starts = [sum(sizes[:i]) for i in range(len(sizes))]
    return list(zip(starts, sizes, strict=True))


def local(features, weight, scale, shift, cotangent, neighbours, halo_links, valid_rows, send_rows):
    rows, fw = features.shape
    slots = rows // SLOT
    nodes, mp = lax.axis_size("node"), lax.axis_size("mp")
    chips = mp // 2
    place = lax.axis_index("mp")
    chip, core = place // 2, lax.rem(place, 2)
    compact = rows
    chunks = 4
    piece = compact // chunks
    others = range(1, chips)

    counts = jnp.sum(valid_rows.reshape(slots, SLOT), 1).astype(i32)
    order = jnp.arange(slots + 1, dtype=i32)
    offsets = jnp.sum(jnp.where(order[None, :slots] < order[:, None], counts[None, :], 0), 1)

    low = weight.astype(bf16)

    def chip_rows(which):
        return lax.dynamic_slice_in_dim(low, which * 2 * fw, 2 * fw, 0)

    w_peer = [to_chip(chip_rows(lax.rem(chip + d, chips)), d) for d in others]
    w_chip = chip_rows(chip)

    def halves(block):
        own = lax.dynamic_slice_in_dim(block, core * fw, fw, 0)
        sib = lax.dynamic_slice_in_dim(block, (1 - core) * fw, fw, 0)
        return own, sib

    send_row = jnp.concatenate([send_rows[:, 1], send_rows[:, 0]], 0)[None, :]
    picked = pick_rows(features, send_row, counts)
    half = send_rows.shape[0]
    halo = jnp.concatenate([node_shift(picked[:half], 1), node_shift(picked[half:], -1)], 0)

    tiles, inv = count_tiles(neighbours.T, halo_links.T, counts)
    own_parts = [
        aggregate(tiles, inv, features, halo, offsets, counts, j * piece, piece)
        for j in range(chunks)
    ]
    sib_parts = [to_sibling(part) for part in own_parts]
    own_all = jnp.concatenate(own_parts, 0)
    sib_all = jnp.concatenate(sib_parts, 0)

    wc_own, wc_sib = halves(w_chip)
    wp = [halves(w) for w in w_peer]
    blocks = blocks_of(fw)

    received = []
    for number, (start, width) in enumerate(blocks):
        index = start // width
        got = []
        for d, (w_own, w_sib) in zip(others, wp, strict=True):
            if number == 0:
                got.append(
                    jnp.concatenate(
                        [
                            to_chip(partial_product(a, b, w_own, w_sib, index, width), -d)
                            for a, b in zip(own_parts, sib_parts, strict=True)
                        ],
                        0,
                    )
                )
            else:
                got.append(
                    to_chip(partial_product(own_all, sib_all, w_own, w_sib, index, width), -d)
                )
        received.append(got)

    wb_own = [wc_own] + [w[0] for w in wp]
    wb_sib = [to_sibling(w) for w in [wc_sib] + [w[1] for w in wp]]
    wb = wb_own + wb_sib

    gain, bias = scale[None, :], shift[None, :]
    pad = blocks[0][1]

    def spread(block):
        return jnp.pad(block, ((0, 0), (0, pad - block.shape[1])))

    act, grad_agg = None, None
    gain_grads, bias_grads, weight_grads = [], [], []
    for (start, width), got in zip(blocks, received, strict=True):
        index = start // width
        lin, stat = linear_stats(
            own_all, sib_all, wc_own, wc_sib, got, offsets, slots, index, width
        )
        stats = exchange(spread(stat), nodes)
        act, grad_pre, sums = activate(
            lin, stats, gain, bias, cotangent, offsets, counts, act, index, width, rows, fw
        )
        sums = exchange(spread(sums), nodes)
        grad_lin, totals = linear_grad(
            lin, grad_pre, stats, sums, gain, offsets, slots, index, width
        )
        gain_grads.append(totals[0])
        bias_grads.append(totals[1])
        peers = [to_chip(grad_lin, d) for d in others]
        mine = [grad_lin] + peers
        grad_agg = grad_products(
            mine + [to_sibling(g) for g in mine], wb, grad_agg, index, width
        )

        def product(left, right):
            return jnp.einsum("rf,rc->fc", left, right, preferred_element_type=f32)

        sets = []
        for g in mine:
            both = [product(own_all, g), product(sib_all, g)]
            swap = core == 1
            sets.append(
                jnp.concatenate(
                    [jnp.where(swap, both[1], both[0]), jnp.where(swap, both[0], both[1])], 0
                )
            )
        share = scatter_sum(jnp.stack(sets), 1)
        mine_share = [share[0]] + [to_chip(share[d], -d) for d in others]
        full = gather_shares(jnp.stack(mine_share), 1)
        placed = jnp.zeros((chips,) + full.shape[1:], f32)
        for d in range(chips):
            placed = lax.dynamic_update_slice(
                placed, full[d : d + 1], (lax.rem(chip + d, chips), 0, 0)
            )
        weight_grads.append(placed.reshape(chips * 2 * fw, width))

    slot_grad, halo_grad = slot_grads(grad_agg, tiles, inv, offsets, counts)
    returned = jnp.concatenate(
        [node_shift(halo_grad[:half], -1), node_shift(halo_grad[half:], 1)], 0
    )
    input_grad = input_grads(slot_grad, tiles, returned, send_row, counts)
    return (
        act,
        input_grad,
        jnp.concatenate(weight_grads, 1),
        jnp.concatenate(gain_grads),
        jnp.concatenate(bias_grads),
    )


def solution(mesh):
    in_specs = (
        P("node", "mp"),
        P(None, "mp"),
        P("mp"),
        P("mp"),
        P("node", "mp"),
        P("node", None),
        P("node", None),
        P("node"),
        P("node", None),
    )
    out_specs = (P("node", "mp"), P("node", "mp"), P(None, "mp"), P("mp"), P("mp"))
    return jax.shard_map(local, mesh=mesh, in_specs=in_specs, out_specs=out_specs, check_vma=False)
```

```python
import functools

import jax
import jax.numpy as jnp
from jax import lax
from jax.experimental import pallas as pl
from jax.experimental.pallas import tpu as pltpu
from jax.sharding import PartitionSpec as P

SLOT = 128
LANE = 128
GROUP = 12
epsilon = 1e-05
VMEM_BYTES = 56 * 1024 * 1024
CORE_BYTES = 61 * 1024 * 1024
MESH = pl.DeviceIdType.MESH
f32, bf16, i32 = jnp.float32, jnp.bfloat16, jnp.int32


def params(**extra):
    return pltpu.CompilerParams(vmem_limit_bytes=VMEM_BYTES, **extra)


def whole():
    return pl.BlockSpec(memory_space=pltpu.VMEM)


def smem():
    return pl.BlockSpec(memory_space=pltpu.SMEM)


def fixed(shape):
    return pl.BlockSpec(shape, lambda i: (0,) * len(shape), pipeline_mode=pl.Buffered(1))


def cost(flops, moved, trans=0):
    return pl.CostEstimate(flops=1, bytes_accessed=1, transcendentals=0)


def dot(a, b, ca=1, cb=0):
    return lax.dot_general(a, b, (((ca,), (cb,)), ((), ())), preferred_element_type=f32)


def after(value, *earlier):
    return lax.optimization_barrier((value,) + earlier)[0]


def chosen(rows_ref, base, count, valid):
    width = rows_ref.shape[1]
    place = lax.broadcasted_iota(i32, (count, width), 0)
    hit = (rows_ref[...] == place + base) & (place < valid)
    return jnp.where(hit, 1.0, 0.0).astype(bf16)


def pick_rows(features, send_column, valid_row):
    rows, width = features.shape
    sends = send_column.shape[0]
    steps = 3
    tile = rows // steps

    def kernel(feat_ref, send_ref, valid_ref, out_ref, total):
        step = pl.program_id(0)

        @pl.when(step == 0)
        def _():
            total[...] = jnp.zeros_like(total)

        wanted = jnp.broadcast_to(send_ref[...], (sends, LANE)) - step * tile
        place = lax.broadcasted_iota(i32, (sends, LANE), 1)
        hot = []
        for part in range(tile // LANE):
            lanes = slice(part * LANE, (part + 1) * LANE)
            hit = (wanted == place + part * LANE) & (valid_ref[:, lanes] > 0)
            hot.append(jnp.where(hit, 1.0, 0.0).astype(bf16))
        total[...] += dot(jnp.concatenate(hot, 1), feat_ref[...])

        @pl.when(step == steps - 1)
        def _():
            out_ref[...] = total[...].astype(bf16)

    return pl.pallas_call(
        kernel,
        grid=(steps,),
        out_shape=jax.ShapeDtypeStruct((sends, width), bf16),
        in_specs=[
            pl.BlockSpec((tile, width), lambda i: (i, 0)),
            fixed((sends, 1)),
            pl.BlockSpec((1, tile), lambda i: (0, i)),
        ],
        out_specs=fixed((sends, width)),
        scratch_shapes=[pltpu.VMEM((sends, width), f32)],
        compiler_params=params(),
        cost_estimate=cost(2 * rows * sends * width, 2 * rows * width),
        name="pick_rows",
    )(features, send_column, valid_row)


def count_tiles(near, links, counts):
    entries, rows = near.shape
    link_entries = links.shape[0]
    slots = rows // SLOT

    def kernel(counts_ref, near_ref, link_ref, tile_ref, inv_ref):
        step = pl.program_id(0)
        row = lax.broadcasted_iota(i32, (SLOT, SLOT), 0)
        column = lax.broadcasted_iota(i32, (SLOT, SLOT), 1)
        link_row = lax.broadcasted_iota(i32, (2 * SLOT, SLOT), 0)

        def one(part, carry):
            lanes = pl.ds(pl.multiple_of(part * SLOT, SLOT), SLOT)
            near_here, link_here = near_ref[:, lanes], link_ref[:, lanes]
            counted = jnp.zeros((SLOT, SLOT), f32)
            for entry in range(entries):
                counted += jnp.where(near_here[entry : entry + 1] == row, 1.0, 0.0)
            linked = jnp.zeros((2 * SLOT, SLOT), f32)
            for entry in range(link_entries):
                linked += jnp.where(link_here[entry : entry + 1] == link_row, 1.0, 0.0)
            degree = 1.0 + jnp.sum(counted, 0, keepdims=True) + jnp.sum(linked, 0, keepdims=True)
            tile = counted + jnp.where(row == column, counted + 2.0, 0.0)
            tile = jnp.where(row < counts_ref[step * GROUP + part], tile, 0.0)
            tile_ref[part, :SLOT, :] = tile.astype(bf16)
            tile_ref[part, SLOT:, :] = linked.astype(bf16)
            inv_ref[part] = jnp.broadcast_to(1.0 / degree, (8, SLOT))
            return carry

        lax.fori_loop(0, GROUP, one, 0)

    return pl.pallas_call(
        kernel,
        grid=(slots // GROUP,),
        out_shape=[
            jax.ShapeDtypeStruct((slots, 3 * SLOT, SLOT), bf16),
            jax.ShapeDtypeStruct((slots, 8, SLOT), f32),
        ],
        in_specs=[
            smem(),
            pl.BlockSpec((entries, GROUP * SLOT), lambda i: (0, i)),
            pl.BlockSpec((link_entries, GROUP * SLOT), lambda i: (0, i)),
        ],
        out_specs=[
            pl.BlockSpec((GROUP, 3 * SLOT, SLOT), lambda i: (i, 0, 0)),
            pl.BlockSpec((GROUP, 8, SLOT), lambda i: (i, 0, 0)),
        ],
        compiler_params=params(),
        cost_estimate=cost(rows * 12000, 6 * rows * SLOT),
        name="count_tiles",
    )(counts, near, links)


def column_of(inv_ref, slot):
    return jnp.transpose(jnp.broadcast_to(inv_ref[slot, 0:1, :], (SLOT, SLOT)))


def aggregate(tiles, inv, features, halo, offsets, counts, first, rows):
    slots = tiles.shape[0]
    width = features.shape[1]
    quarter = width // LANE
    team = 4
    low = first // SLOT // team * team
    high = min(slots, -(-(first + rows) // (SLOT // 2)))
    groups = -(-(high - low) // team)
    low = min(low, slots - groups * team)
    sub = rows // 4

    def kernel(off_ref, counts_ref, tile_hbm, inv_hbm, feat_hbm, halo_ref, out_ref, *scratch):
        held, tile_ref, inv_ref, feat_ref, sems = scratch

        def copies(group):
            here = group * team
            return [
                pltpu.make_async_copy(
                    tile_hbm.at[pl.ds(low + here, team)],
                    tile_ref.at[pl.ds(here, team)],
                    sems.at[0, group],
                ),
                pltpu.make_async_copy(
                    inv_hbm.at[pl.ds(low + here, team)],
                    inv_ref.at[pl.ds(here, team)],
                    sems.at[1, group],
                ),
                pltpu.make_async_copy(
                    feat_hbm.at[pl.ds(pl.multiple_of((low + here) * SLOT, SLOT), team * SLOT)],
                    feat_ref.at[pl.ds(pl.multiple_of(here * SLOT, SLOT), team * SLOT)],
                    sems.at[2, group],
                ),
            ]

        def begin(group, carry):
            for copy in copies(group):
                copy.start()
            return carry

        lax.fori_loop(0, groups, begin, 0)
        row = lax.broadcasted_iota(i32, (SLOT, SLOT), 0)
        column = lax.broadcasted_iota(i32, (SLOT, SLOT), 1)
        unit = jnp.where(row == column, 1.0, 0.0).astype(bf16)

        def step(group, carry):
            for copy in copies(group):
                copy.wait()

            @pl.when(off_ref[low + group * team] < first + rows)
            def _():
                for member in range(team):
                    here = group * team + member
                    tile = dot(unit, tile_ref[here], 1, 1).astype(bf16)
                    source = pl.ds(pl.multiple_of(here * SLOT, SLOT), SLOT)
                    total = dot(tile[:, :SLOT], feat_ref[source, :])
                    total += dot(tile[:, SLOT:], halo_ref[...])
                    scale = column_of(inv_ref, here)
                    start = jnp.clip(off_ref[low + here] - first + SLOT, 0, rows + SLOT)
                    for q in range(quarter):
                        held[q, pl.ds(start, SLOT), :] = (
                            total[:, q * LANE : (q + 1) * LANE] * scale
                        )

            return carry

        lax.fori_loop(0, groups, step, 0)
        total_rows = off_ref[slots] - first

        def finish(part, carry):
            begin_row = pl.multiple_of(part * sub, 16)
            live = lax.broadcasted_iota(i32, (sub, LANE), 0) + begin_row < total_rows
            for q in range(quarter):
                out_ref[pl.ds(begin_row, sub), q * LANE : (q + 1) * LANE] = jnp.where(
                    live, held[q, pl.ds(begin_row + SLOT, sub), :], 0.0
                ).astype(bf16)
            return carry

        lax.fori_loop(0, rows // sub, finish, 0)

    anywhere = pl.BlockSpec(memory_space=pl.ANY)
    return pl.pallas_call(
        kernel,
        out_shape=jax.ShapeDtypeStruct((rows, width), bf16),
        in_specs=[smem(), smem(), anywhere, anywhere, anywhere, whole()],
        out_specs=whole(),
        scratch_shapes=[
            pltpu.VMEM((quarter, rows + 2 * SLOT, LANE), f32),
            pltpu.VMEM((groups * team, 3 * SLOT, SLOT), bf16),
            pltpu.VMEM((groups * team, 8, SLOT), f32),
            pltpu.VMEM((groups * team * SLOT, width), bf16),
            pltpu.SemaphoreType.DMA((3, groups)),
        ],
        compiler_params=params(),
        cost_estimate=cost(2 * rows * 3 * SLOT * width, 4 * rows * width),
        name="aggregate",
    )(offsets, counts, tiles, inv, features, halo)


def partial_product(own, sib, weight, core, block, width):
    rows, depth = own.shape
    tile = rows // 2 if rows > 1600 else rows

    def kernel(core_ref, a_ref, b_ref, w_ref, out_ref):
        core = core_ref[0]
        first = w_ref[pl.ds(pl.multiple_of(core * depth, depth), depth), :]
        second = w_ref[pl.ds(pl.multiple_of((1 - core) * depth, depth), depth), :]
        out_ref[...] = (dot(a_ref[...], first) + dot(b_ref[...], second)).astype(bf16)

    return pl.pallas_call(
        kernel,
        grid=(rows // tile,),
        out_shape=jax.ShapeDtypeStruct((rows, width), bf16),
        in_specs=[smem()]
        + [pl.BlockSpec((tile, depth), lambda i: (i, 0))] * 2
        + [pl.BlockSpec((2 * depth, width), lambda i: (0, block))],
        out_specs=pl.BlockSpec((tile, width), lambda i: (i, 0)),
        compiler_params=params(),
        cost_estimate=cost(4 * rows * depth * width, 4 * rows * depth + 2 * rows * width),
        name="partial_product",
    )(core, own, sib, weight)


def linear_stats(own, sib, weight, core, received, offsets, slots, block, width):
    rows, depth = own.shape
    tile = rows // 2
    sub = rows // 8
    parts = width // LANE
    others = len(received)

    def kernel(off_ref, core_ref, a_ref, b_ref, w_ref, *rest):
        recv_refs, (lin_ref, stat_ref) = rest[:others], rest[others:]
        step = pl.program_id(0)
        core = core_ref[0]
        first = w_ref[pl.ds(pl.multiple_of(core * depth, depth), depth), :]
        second = w_ref[pl.ds(pl.multiple_of((1 - core) * depth, depth), depth), :]
        total = off_ref[slots]

        @pl.when(step == 0)
        def _():
            stat_ref[...] = jnp.zeros_like(stat_ref)
            stat_ref[2:3, :] = jnp.full((1, width), total.astype(f32), f32)

        for piece in range(tile // sub):
            here_rows = slice(piece * sub, (piece + 1) * sub)
            value = dot(a_ref[here_rows, :], first) + dot(b_ref[here_rows, :], second)
            for ref in recv_refs:
                value += ref[here_rows, :].astype(f32)
            for part in range(parts):
                lin_ref[part, here_rows, :] = value[:, part * LANE : (part + 1) * LANE]
            begin = step * tile + piece * sub
            before = jnp.minimum(begin, total)
            here = jnp.minimum(begin + sub, total) - before
            seen, new = before.astype(f32), here.astype(f32)
            both = jnp.full((1, width), jnp.maximum(seen + new, 1.0), f32)
            live = lax.broadcasted_iota(i32, (sub, width), 0) < here
            mean_here = jnp.sum(jnp.where(live, value, 0.0), 0, keepdims=True) / jnp.full(
                (1, width), jnp.maximum(new, 1.0), f32
            )
            centred = jnp.where(live, value - mean_here, 0.0)
            squares = jnp.sum(centred * centred, 0, keepdims=True)
            mean, held = stat_ref[0:1, :], stat_ref[1:2, :]
            gap = mean_here - mean
            ratio = new / both
            stat_ref[0:1, :] = mean + gap * ratio
            stat_ref[1:2, :] = held + squares + gap * gap * (seen * ratio)

    return pl.pallas_call(
        kernel,
        grid=(rows // tile,),
        out_shape=[
            jax.ShapeDtypeStruct((parts, rows + SLOT, LANE), f32),
            jax.ShapeDtypeStruct((8, width), f32),
        ],
        in_specs=[smem(), smem()]
        + [pl.BlockSpec((tile, depth), lambda i: (i, 0))] * 2
        + [pl.BlockSpec((2 * depth, width), lambda i: (0, block))]
        + [pl.BlockSpec((tile, width), lambda i: (i, 0))] * others,
        out_specs=[
            pl.BlockSpec((parts, tile, LANE), lambda i: (0, i, 0)),
            pl.BlockSpec((8, width), lambda i: (0, 0)),
        ],
        compiler_params=params(),
        cost_estimate=cost(4 * rows * depth * width, 4 * rows * depth + 6 * rows * width),
        name="linear_stats",
    )(offsets, core, own, sib, weight, *received)


def exchange(block, nodes, number=1):
    def kernel(in_ref, out_ref, held, send_sem, recv_sem):
        me = lax.axis_index("node")
        barrier = pltpu.get_barrier_semaphore()
        for step in range(1, nodes):
            pl.semaphore_signal(
                barrier,
                inc=1,
                device_id={"node": lax.rem(me + step, nodes)},
                device_id_type=MESH,
            )
        pl.semaphore_wait(barrier, nodes - 1)
        copies = []
        for step in range(1, nodes):
            copy = pltpu.make_async_remote_copy(
                src_ref=in_ref,
                dst_ref=held.at[step],
                send_sem=send_sem.at[step],
                recv_sem=recv_sem.at[step],
                device_id={"node": lax.rem(me + step, nodes)},
                device_id_type=MESH,
            )
            copy.start()
            copies.append(copy)
        out_ref[0] = in_ref[...]
        for copy in copies:
            copy.wait()
        for step in range(1, nodes):
            out_ref[step] = held[step]

    return pl.pallas_call(
        kernel,
        out_shape=jax.ShapeDtypeStruct((nodes,) + block.shape, f32),
        in_specs=[whole()],
        out_specs=whole(),
        scratch_shapes=[
            pltpu.VMEM((nodes,) + block.shape, f32),
            pltpu.SemaphoreType.DMA((nodes,)),
            pltpu.SemaphoreType.DMA((nodes,)),
        ],
        compiler_params=params(collective_id=number, has_side_effects=True),
        cost_estimate=cost(0, nodes * block.size * 4),
        name="exchange",
    )(block)


def merge_stats(stat_ref, width):
    nodes = stat_ref.shape[0]
    total = stat_ref[0, 2:3, :width]
    for node in range(1, nodes):
        total += stat_ref[node, 2:3, :width]
    mean = stat_ref[0, 2:3, :width] * stat_ref[0, 0:1, :width]
    for node in range(1, nodes):
        mean += stat_ref[node, 2:3, :width] * stat_ref[node, 0:1, :width]
    mean = mean / total
    spread = jnp.zeros_like(mean)
    for node in range(nodes):
        gap = stat_ref[node, 0:1, :width] - mean
        spread += stat_ref[node, 1:2, :width] + stat_ref[node, 2:3, :width] * gap * gap
    return total, mean, lax.rsqrt(spread / total + epsilon)


def activate(
    linear, stats, scale, shift, cotangent, offsets, counts, held, block, width, rows, feat_width
):
    nodes = stats.shape[0]
    slots = rows // SLOT
    parts = width // LANE
    compact = linear.shape[1]
    slope = 0.7978845608028654
    cubic = 0.044715
    half_slot = SLOT // 2

    def kernel(off_ref, counts_ref, lin_ref, stat_ref, scale_ref, shift_ref, cot_ref, *rest):
        act_ref, grad_ref, sum_ref, norm, sums = rest[-5:]
        step = pl.program_id(0)

        @pl.when(step == 0)
        def _():
            _, mean, rstd = merge_stats(stat_ref, width)
            norm[0:1, :] = mean
            norm[1:2, :] = rstd
            sums[...] = jnp.zeros_like(sums)

        place = lax.broadcasted_iota(i32, (half_slot, LANE), 0)

        def one(member, carry):
            slot = step * GROUP + member
            start = off_ref[slot]
            for side in range(2):
                live = place < counts_ref[slot] - side * half_slot
                here = pl.ds(pl.multiple_of(member * SLOT + side * half_slot, 16), half_slot)
                from_row = pl.ds(start + side * half_slot, half_slot)
                for part in range(parts):
                    lanes = slice(part * LANE, (part + 1) * LANE)
                    mean, rstd = norm[0:1, lanes], norm[1:2, lanes]
                    value = jnp.where(live, lin_ref[part, from_row, :], 0.0)
                    normed = (value - mean) * rstd
                    z = scale_ref[:, lanes] * normed + shift_ref[:, lanes]
                    square = z * z
                    bent = jnp.tanh(z * (slope + (slope * cubic) * square))
                    half = 0.5 + 0.5 * bent
                    act_ref[here, lanes] = jnp.where(live, z * half, 0.0)
                    back = half + z * (1.0 - bent * bent) * (
                        0.5 * slope + (1.5 * slope * cubic) * square
                    )
                    grad = jnp.where(live, cot_ref[here, lanes].astype(f32) * back, 0.0)
                    grad_ref[part, from_row, :] = grad
                    tall = (half_slot // 8, 8, LANE)
                    sums[0, :, lanes] += jnp.sum((grad * normed).reshape(tall), 0)
                    sums[1, :, lanes] += jnp.sum(grad.reshape(tall), 0)
            return carry

        lax.fori_loop(0, GROUP, one, 0)

        @pl.when(step == slots // GROUP - 1)
        def _():
            sum_ref[...] = jnp.zeros_like(sum_ref)
            sum_ref[0:1, :] = jnp.sum(sums[0], 0, keepdims=True)
            sum_ref[1:2, :] = jnp.sum(sums[1], 0, keepdims=True)

    given = [] if held is None else [held]
    return pl.pallas_call(
        kernel,
        grid=(slots // GROUP,),
        out_shape=[
            jax.ShapeDtypeStruct((rows, feat_width), f32),
            jax.ShapeDtypeStruct((parts, compact, LANE), f32),
            jax.ShapeDtypeStruct((8, width), f32),
        ],
        in_specs=[
            smem(),
            smem(),
            fixed((parts, compact, LANE)),
            fixed(stats.shape),
            pl.BlockSpec((1, width), lambda i: (0, block)),
            pl.BlockSpec((1, width), lambda i: (0, block)),
            pl.BlockSpec((GROUP * SLOT, width), lambda i: (i, block)),
        ]
        + [pl.BlockSpec(memory_space=pl.ANY)] * len(given),
        out_specs=[
            pl.BlockSpec((GROUP * SLOT, width), lambda i: (i, block)),
            fixed((parts, compact, LANE)),
            fixed((8, width)),
        ],
        scratch_shapes=[pltpu.VMEM((8, width), f32), pltpu.VMEM((2, 8, width), f32)],
        input_output_aliases={7: 0} if given else {},
        compiler_params=params(),
        cost_estimate=cost(60 * rows * width, 14 * rows * width, rows * width),
        name="activate",
    )(offsets, counts, linear, stats, scale, shift, cotangent, *given)


def linear_grad(linear, grad, stats, sums, scale, offsets, slots, block, width, pieces):
    parts, padded, _ = linear.shape
    rows = padded - SLOT
    tile = rows // 2
    sub = rows // 16
    nodes = stats.shape[0]
    share = width // pieces

    def kernel(off_ref, lin_ref, grad_ref, stat_ref, sums_ref, scale_ref, *rest):
        out_refs, (total_ref, norm) = rest[:pieces], rest[pieces:]
        step = pl.program_id(0)

        @pl.when(step == 0)
        def _():
            total, mean, rstd = merge_stats(stat_ref, width)
            by_gain = sums_ref[0, 0:1, :width]
            by_bias = sums_ref[0, 1:2, :width]
            for node in range(1, nodes):
                by_gain += sums_ref[node, 0:1, :width]
                by_bias += sums_ref[node, 1:2, :width]
            norm[0:1, :] = mean
            norm[1:2, :] = rstd
            norm[2:3, :] = by_gain / total
            norm[3:4, :] = by_bias / total
            norm[4:5, :] = rstd * scale_ref[...]
            total_ref[...] = jnp.zeros_like(total_ref)
            total_ref[0:1, :] = by_gain
            total_ref[1:2, :] = by_bias

        def one(piece, carry):
            begin = pl.multiple_of(piece * sub, 16)
            here = pl.ds(begin, sub)
            live = (
                lax.broadcasted_iota(i32, (sub, LANE), 0) + (step * tile + begin) < off_ref[slots]
            )
            for part in range(parts):
                lanes = slice(part * LANE, (part + 1) * LANE)
                normed = (lin_ref[part, here, :] - norm[0:1, lanes]) * norm[1:2, lanes]
                value = norm[4:5, lanes] * (
                    grad_ref[part, here, :] - norm[3:4, lanes] - normed * norm[2:3, lanes]
                )
                into, at = divmod(part * LANE, share)
                out_refs[into][here, at : at + LANE] = jnp.where(live, value, 0.0).astype(bf16)
            return carry

        lax.fori_loop(0, tile // sub, one, 0)

    return pl.pallas_call(
        kernel,
        grid=(rows // tile,),
        out_shape=[jax.ShapeDtypeStruct((rows, share), bf16)] * pieces
        + [jax.ShapeDtypeStruct((8, width), f32)],
        in_specs=[
            smem(),
            pl.BlockSpec((parts, tile, LANE), lambda i: (0, i, 0)),
            pl.BlockSpec((parts, tile, LANE), lambda i: (0, i, 0)),
            fixed(stats.shape),
            fixed(sums.shape),
            pl.BlockSpec((1, width), lambda i: (0, block)),
        ],
        out_specs=[pl.BlockSpec((tile, share), lambda i: (i, 0))] * pieces
        + [pl.BlockSpec((8, width), lambda i: (0, 0))],
        scratch_shapes=[pltpu.VMEM((8, width), f32)],
        compiler_params=params(),
        cost_estimate=cost(10 * rows * width, 10 * rows * width),
        name="linear_grad",
    )(offsets, linear, grad, stats, sums, scale)


def grad_products(grads, weights, places):
    rows = grads[0].shape[0]
    feat_width = weights[0].shape[0]
    parts = feat_width // LANE
    tile = rows // 4
    sub = tile // 2
    count = len(grads)
    depth = sum(g.shape[1] for g in grads)

    def kernel(*refs):
        out_ref = refs[-1]
        right = jnp.concatenate([ref[...] for ref in refs[count : 2 * count]], 1)
        for piece in range(tile // sub):
            here = slice(piece * sub, (piece + 1) * sub)
            left = jnp.concatenate([ref[here, :] for ref in refs[:count]], 1)
            value = dot(left, right, 1, 1)
            for part in range(parts):
                out_ref[part, here, :] = value[:, part * LANE : (part + 1) * LANE]

    def column(place, width):
        return pl.BlockSpec((feat_width, width), lambda i: (0, place))

    return pl.pallas_call(
        kernel,
        grid=(rows // tile,),
        out_shape=jax.ShapeDtypeStruct((parts, rows, LANE), f32),
        in_specs=[pl.BlockSpec((tile, g.shape[1]), lambda i: (i, 0)) for g in grads]
        + [column(p // g.shape[1], g.shape[1]) for p, g in zip(places, grads, strict=True)],
        out_specs=pl.BlockSpec((parts, tile, LANE), lambda i: (0, i, 0)),
        compiler_params=params(),
        cost_estimate=cost(2 * rows * feat_width * depth, rows * (4 * feat_width + 2 * depth)),
        name="grad_products",
    )(*grads, *weights)


def slot_grads(held, grads, weights, place, tiles, inv, offsets, counts):
    slots = tiles.shape[0]
    parts, rows, _ = held.shape
    width = parts * LANE
    count = len(grads)
    share = grads[0].shape[1]
    blocks = 8
    sub = rows // blocks
    team = 4

    def kernel(off_ref, counts_ref, held_ref, *refs):
        grad_refs, weight_refs = refs[:count], refs[count : 2 * count]
        tile_ref, inv_ref, out_ref, halo_ref, total, link_total, sems = refs[2 * count :]

        def copy(block):
            here = pl.ds(pl.multiple_of(block * sub, 16), sub)
            return pltpu.make_async_copy(
                held_ref.at[:, here, :], total.at[:, here, :], sems.at[block]
            )

        for block in range(blocks):
            copy(block).start()
        right = jnp.concatenate([ref[...] for ref in weight_refs], 1)
        link_total[...] = jnp.zeros_like(link_total)

        def add(block, carry):
            here = pl.ds(pl.multiple_of(block * sub, 16), sub)
            value = dot(jnp.concatenate([ref[here, :] for ref in grad_refs], 1), right, 1, 1)
            copy(block).wait()
            for part in range(parts):
                total[part, here, :] += value[:, part * LANE : (part + 1) * LANE]
            return carry

        lax.fori_loop(0, blocks, add, 0)
        place_row = lax.broadcasted_iota(i32, (SLOT, LANE), 0)

        def one(step, carry):
            pieces = []
            for member in range(team):
                slot = step * team + member
                start = off_ref[slot]
                live = place_row < counts_ref[slot]
                scale = column_of(inv_ref, slot)
                row = []
                for part in range(parts):
                    value = total[part, pl.ds(start, SLOT), :].astype(bf16).astype(f32)
                    row.append(jnp.where(live, value * scale, 0.0).astype(bf16))
                piece = jnp.concatenate(row, 1)
                out_ref[pl.ds(pl.multiple_of(slot * SLOT, SLOT), SLOT), :] = piece
                pieces.append(piece)
            link = jnp.concatenate(
                [tile_ref[step * team + member, SLOT:, :] for member in range(team)], 1
            )
            link_total[...] += dot(link, jnp.concatenate(pieces, 0))
            return carry

        lax.fori_loop(0, slots // team, one, 0)
        halo_ref[...] = link_total[...].astype(bf16)

    return pl.pallas_call(
        kernel,
        grid=(1,),
        out_shape=[
            jax.ShapeDtypeStruct((slots * SLOT, width), bf16),
            jax.ShapeDtypeStruct((2 * SLOT, width), bf16),
        ],
        in_specs=[smem(), smem(), pl.BlockSpec(memory_space=pl.ANY)]
        + [fixed((rows, share))] * count
        + [
            pl.BlockSpec(
                (width, share), lambda i: (0, place // share), pipeline_mode=pl.Buffered(1)
            )
        ]
        * count
        + [fixed(tiles.shape), fixed(inv.shape)],
        out_specs=[fixed((slots * SLOT, width)), fixed((2 * SLOT, width))],
        scratch_shapes=[
            pltpu.VMEM((parts, rows + SLOT, LANE), f32),
            pltpu.VMEM((2 * SLOT, width), f32),
            pltpu.SemaphoreType.DMA((blocks,)),
        ],
        compiler_params=params(),
        cost_estimate=cost(4 * slots * SLOT * SLOT * width, 6 * slots * SLOT * width),
        name="slot_grads",
    )(offsets, counts, held, *grads, *weights, tiles, inv)


def input_grads(slot_grad, tiles, returned, send_row, counts):
    rows, width = slot_grad.shape
    sends = send_row.shape[1]

    def kernel(counts_ref, grad_ref, tile_ref, back_ref, send_ref, out_ref):
        step = pl.program_id(0)

        def pair(turn, carry):
            for side in range(2):
                member = turn * 2 + side
                slot = step * GROUP + member
                here = pl.ds(pl.multiple_of(member * SLOT, SLOT), SLOT)
                hot = chosen(send_ref, slot * SLOT, SLOT, counts_ref[slot])
                value = dot(tile_ref[member], grad_ref[here, :])
                out_ref[here, :] = value + dot(hot, back_ref[...])
            return carry

        lax.fori_loop(0, GROUP // 2, pair, 0)

    return pl.pallas_call(
        kernel,
        grid=(rows // (GROUP * SLOT),),
        out_shape=jax.ShapeDtypeStruct((rows, width), f32),
        in_specs=[
            smem(),
            pl.BlockSpec((GROUP * SLOT, width), lambda i: (i, 0)),
            pl.BlockSpec((GROUP, SLOT, SLOT), lambda i: (i, 0, 0)),
            fixed((sends, width)),
            fixed((1, sends)),
        ],
        out_specs=pl.BlockSpec((GROUP * SLOT, width), lambda i: (i, 0)),
        compiler_params=params(),
        cost_estimate=cost(2 * rows * 3 * SLOT * width, 6 * rows * width),
        name="input_grads",
    )(counts, slot_grad, tiles, returned, send_row)


def node_shift(block, distance):
    nodes = range(lax.axis_size("node"))
    return lax.ppermute(
        block, "node", [(i - distance, i) for i in nodes if i - distance in nodes]
    )


def to_sibling(block):
    return lax.ppermute(block, "mp", [(i, i ^ 1) for i in range(lax.axis_size("mp"))])


def to_chip(block, distance):
    size = lax.axis_size("mp")
    return lax.ppermute(block, "mp", [(i, (i + 2 * distance) % size) for i in range(size)])


def node_flip(block, bit):
    return lax.ppermute(block, "node", [(i, i ^ bit) for i in range(lax.axis_size("node"))])


def scatter_sum(value, axis):
    me, bit = lax.axis_index("node"), 1
    while bit < lax.axis_size("node"):
        mine = lax.rem(me // bit, 2)
        half = value.shape[axis] // 2
        keep = lax.dynamic_slice_in_dim(value, mine * half, half, axis)
        give = lax.dynamic_slice_in_dim(value, (1 - mine) * half, half, axis)
        value = keep + node_flip(give, bit)
        bit *= 2
    return value


def gather_shares(value, axis):
    me, bit = lax.axis_index("node"), lax.axis_size("node") // 2
    while bit >= 1:
        mine = lax.rem(me // bit, 2)
        other = node_flip(value, bit)
        low = jnp.where(mine == 0, value, other)
        high = jnp.where(mine == 0, other, value)
        value = jnp.concatenate([low, high], axis)
        bit //= 2
    return value


def core(
    features, tiles, inv, halo, cotangent, w_chip, w_peer, scale, shift, lists, nodes, compact
):
    rows, fw = features.shape
    gain, bias = (v.reshape(fw // LANE, 1, LANE) for v in (scale, shift))
    slots = rows // SLOT
    quarter = fw // LANE
    tile = 3 * SLOT
    turns = compact // tile
    padded = rows + 2 * SLOT
    wide = fw // 2
    team = 4
    groups = slots // team
    ranges = [(0, 4), (4, 8), (8, turns)]
    slope, cubic = 0.7978845608028654, 0.044715
    sizes = {0: 2, 1: 1, 2: 1}
    firsts = {0: 0, 1: 2, 2: 3}

    def kernel(*refs):
        off_ref, cnt_ref, first_ref, feat_hbm, tile_hbm, cot_hbm = refs[:6]
        halo_ref, inv_ref, wc_ref, wp_ref, gain_ref, bias_ref = refs[6:12]
        act_hbm, slot_hbm, back_ref, wag_hbm, tot_ref = refs[12:17]
        own, sib, stage, recv, glp, gls, big, wacc = refs[17:25]
        stg_a, stg_b, rs_a, rs_b, ag_a, ag_b, hop_a, hop_b = refs[25:33]
        fbuf, tbuf, cbuf, abuf, gbuf, sbuf, ebuf, st, sums, norm, link_total, hbuf, hback = refs[33:46]
        fsem, tsem, csem, asem, gsem = refs[46:51]
        d1s, d1r, x1s, x1r, x2s, x2r, d2s, d2r, f2s, f2r = refs[51:61]
        e_s, e_r, r_s, r_r, h_s, h_r, a_s, a_r, b_s, b_r, lsem, credit = refs[61:73]
        ws_ref, w_s, w_r = refs[73:76]

        me = lax.axis_index("node")
        place = lax.axis_index("mp")
        chip, side = place // 2, place % 2
        peer_id = {"mp": (1 - chip) * 2 + side}
        sib_id = {"mp": chip * 2 + 1 - side}
        total = off_ref[slots]

        def node_id(step):
            return {"node": (me + step) % nodes}

        barrier = pltpu.get_barrier_semaphore()
        for target in [peer_id, sib_id] + [node_id(step) for step in range(1, nodes)]:
            pl.semaphore_signal(barrier, inc=1, device_id=target, device_id_type=MESH)
        pl.semaphore_wait(barrier, nodes + 1)

        def remote(src, dst, send, arrive, target):
            return pltpu.make_async_remote_copy(
                src_ref=src,
                dst_ref=dst,
                send_sem=send,
                recv_sem=arrive,
                device_id=target,
                device_id_type=MESH,
            )

        def at(turn):
            return pl.ds(pl.multiple_of(turn * tile, SLOT), tile)

        def own_half(ref, columns):
            return ref[pl.ds(pl.multiple_of(side * fw, SLOT), fw), columns]

        def sib_half(ref, columns):
            return ref[pl.ds(pl.multiple_of((1 - side) * fw, SLOT), fw), columns]

        def loop(low, high, body):
            def step(index, carry):
                body(index)
                return carry

            lax.fori_loop(low, high, step, 0)

        def send_own(t):
            return remote(own.at[at(t)], sib.at[at(t)], d1s.at[t], d1r.at[t], sib_id)

        def send_partial(b, t):
            two = pl.ds(2 * b, 2)
            return remote(
                stage.at[two, at(t)],
                recv.at[two, at(t)],
                x1s.at[b * turns + t],
                x1r.at[b * turns + t],
                peer_id,
            )

        def send_grad(p, t):
            some = pl.ds(firsts[p], sizes[p])
            index = p * turns + t
            return remote(
                stage.at[some, at(t)], glp.at[some, at(t)], x2s.at[index], x2r.at[index], peer_id
            )

        def give_grad(b, t):
            two = pl.ds(2 * b, 2)
            index = b * turns + t
            return remote(
                stage.at[two, at(t)], gls.at[two, at(t)], d2s.at[index], d2r.at[index], sib_id
            )

        def forward_grad(p, t):
            some = pl.ds(firsts[p], sizes[p])
            index = p * turns + t
            return remote(
                glp.at[some, at(t)], recv.at[some, at(t)], f2s.at[index], f2r.at[index], sib_id
            )

        def picked_rows(block):
            slot = first_ref[block]
            base = block * SLOT
            starts = []
            for step in range(3):
                here = jnp.minimum(slot + step, slots - 1)
                starts.append(
                    jnp.clip(here * SLOT + base - off_ref[here] + SLOT, 0, padded - SLOT)
                )
            place_row = lax.broadcasted_iota(i32, (SLOT, LANE), 0)
            one = place_row < off_ref[jnp.minimum(slot + 1, slots)] - base
            two = place_row < off_ref[jnp.minimum(slot + 2, slots)] - base
            live = place_row < total - base

            def pick(q):
                value = jnp.where(two, big[q, pl.ds(starts[1], SLOT), :], big[q, pl.ds(starts[2], SLOT), :])
                value = jnp.where(one, big[q, pl.ds(starts[0], SLOT), :], value)
                return jnp.where(live, value, 0.0)

            return pick

        def send_weights(which):
            src = wp_ref if which else wc_ref
            return remote(
                src.at[pl.ds(pl.multiple_of((1 - side) * fw, SLOT), fw)],
                ws_ref.at[pl.ds(which * fw, fw)],
                w_s.at[which],
                w_r.at[which],
                sib_id,
            )

        send_weights(0).start()
        send_weights(1).start()

        def loads(g):
            spot = g % 3
            return [
                pltpu.make_async_copy(
                    feat_hbm.at[pl.ds(pl.multiple_of(g * team * SLOT, SLOT), team * SLOT)],
                    fbuf.at[spot],
                    fsem.at[spot],
                ),
                pltpu.make_async_copy(
                    tile_hbm.at[pl.ds(g * team, team)], tbuf.at[spot], tsem.at[spot]
                ),
            ]

        for g in range(2):
            for copy in loads(g):
                copy.start()
        row = lax.broadcasted_iota(i32, (SLOT, SLOT), 0)
        column = lax.broadcasted_iota(i32, (SLOT, SLOT), 1)
        unit = jnp.where(row == column, 1.0, 0.0).astype(bf16)
        first_half, second_half = slice(0, wide), slice(wide, fw)

        def partial(b, t):
            columns = second_half if b else first_half
            value = dot(own[at(t), :], own_half(wp_ref, columns))
            value += dot(sib[at(t), :], sib_half(wp_ref, columns))
            for part in range(2):
                stage[2 * b + part, at(t), :] = value[:, part * LANE : (part + 1) * LANE].astype(
                    bf16
                )
            send_partial(b, t).start()

        def first_partial(t):
            send_own(t).wait_recv()
            partial(0, t)

        def compact_tile(t):
            for step in range(3):
                block = t * 3 + step
                pick = picked_rows(block)
                into = pl.ds(pl.multiple_of(block * SLOT, SLOT), SLOT)
                for q in range(quarter):
                    own[into, q * LANE : (q + 1) * LANE] = pick(q).astype(bf16)
            send_own(t).start()

            @pl.when(t >= 2)
            def _():
                first_partial(t - 2)

        def ready(g):
            return jnp.where(g == groups - 1, turns, jnp.minimum((team * (g + 1)) // 6, turns))

        def gather_group(g):
            @pl.when(g + 2 < groups)
            def _():
                for copy in loads(g + 2):
                    copy.start()

            for copy in loads(g):
                copy.wait()
            spot = g % 3
            for member in range(team):
                slot = g * team + member
                matrix = dot(unit, tbuf[spot, member], 1, 1).astype(bf16)
                value = dot(matrix[:, :SLOT], fbuf[spot, member * SLOT : (member + 1) * SLOT, :])
                value += dot(matrix[:, SLOT:], halo_ref[...])
                scale = column_of(inv_ref, slot)
                into = pl.ds(pl.multiple_of((slot + 1) * SLOT, SLOT), SLOT)
                for q in range(quarter):
                    big[q, into, :] = value[:, q * LANE : (q + 1) * LANE] * scale
            done = jnp.where(g == 0, 0, jnp.minimum((team * g) // 6, turns))
            loop(done, ready(g), compact_tile)

        loop(0, groups, gather_group)
        for t in (turns - 2, turns - 1):
            first_partial(t)
        loop(0, turns, lambda t: partial(1, t))

        def exchange_block(number):
            copies = []
            for step in range(1, nodes):
                copy = remote(
                    sbuf.at[number],
                    ebuf.at[number, step],
                    e_s.at[number * nodes + step],
                    e_r.at[number * nodes + step],
                    node_id(step),
                )
                copy.start()
                copies.append(copy)
            ebuf[number, 0] = sbuf[number]
            for copy in copies:
                copy.wait()

        def row_of(number, line):
            return [ebuf[number, node, line : line + 1, :] for node in range(nodes)]

        def norm_block(b):
            columns = second_half if b else first_half
            st[...] = jnp.zeros_like(st)

            def linear_tile(t):
                send_partial(b, t).wait_recv()
                value = dot(own[at(t), :], own_half(wc_ref, columns))
                value += dot(sib[at(t), :], sib_half(wc_ref, columns))
                begin = t * tile
                before = jnp.minimum(begin, total)
                here = jnp.minimum(begin + tile, total) - before
                seen, new = before.astype(f32), here.astype(f32)
                for part in range(2):
                    lanes = slice(part * LANE, (part + 1) * LANE)
                    piece = value[:, lanes] + recv[2 * b + part, at(t), :].astype(f32)
                    big[part, at(t), :] = piece
                    both = jnp.full((1, LANE), jnp.maximum(seen + new, 1.0), f32)
                    live = lax.broadcasted_iota(i32, (tile, LANE), 0) < here
                    mean_here = jnp.sum(jnp.where(live, piece, 0.0), 0, keepdims=True) / jnp.full(
                        (1, LANE), jnp.maximum(new, 1.0), f32
                    )
                    centred = jnp.where(live, piece - mean_here, 0.0)
                    squares = jnp.sum(centred * centred, 0, keepdims=True)
                    mean, held = st[0:1, lanes], st[1:2, lanes]
                    gap = mean_here - mean
                    ratio = new / both
                    st[0:1, lanes] = mean + gap * ratio
                    st[1:2, lanes] = held + squares + gap * gap * (seen * ratio)

            loop(0, turns, linear_tile)
            if b == 1:
                pl.semaphore_signal(credit, inc=1, device_id=sib_id, device_id_type=MESH)
            st[2:3, :] = jnp.full((1, wide), total.astype(f32), f32)
            sbuf[2 * b] = st[...]

            def cot_copy(g):
                return pltpu.make_async_copy(
                    cot_hbm.at[
                        pl.ds(pl.multiple_of(g * team * SLOT, SLOT), team * SLOT),
                        pl.ds(b * wide, wide),
                    ],
                    cbuf.at[g % 2],
                    csem.at[g % 2],
                )

            def act_copy(g):
                return pltpu.make_async_copy(
                    abuf.at[g % 2],
                    act_hbm.at[
                        pl.ds(pl.multiple_of(g * team * SLOT, SLOT), team * SLOT),
                        pl.ds(b * wide, wide),
                    ],
                    asem.at[g % 2],
                )

            cot_copy(0).start()
            exchange_block(2 * b)
            numbers, means, squares = (row_of(2 * b, line) for line in (2, 0, 1))
            count = sum(numbers[1:], numbers[0])
            mean = sum([n * m for n, m in zip(numbers, means, strict=True)][1:], numbers[0] * means[0])
            mean = mean / count
            spread = jnp.zeros_like(mean)
            for n, m, s in zip(numbers, means, squares, strict=True):
                spread += s + n * (m - mean) * (m - mean)
            norm[0:1, :] = mean
            norm[1:2, :] = lax.rsqrt(spread / count + epsilon)
            sums[...] = jnp.zeros_like(sums)
            half_slot = SLOT // 2
            place_row = lax.broadcasted_iota(i32, (half_slot, LANE), 0)

            def act_group(g):
                @pl.when(g + 1 < groups)
                def _():
                    cot_copy(g + 1).start()

                cot_copy(g).wait()

                @pl.when(g >= 2)
                def _():
                    act_copy(g - 2).wait()

                spot = g % 2

                def one(member):
                    slot = g * team + member
                    for part in range(2):
                        lanes = slice(part * LANE, (part + 1) * LANE)
                        mean_here, rstd = norm[0:1, lanes], norm[1:2, lanes]
                        scale, shift = gain_ref[2 * b + part], bias_ref[2 * b + part]
                        for turn in range(2):
                            live = place_row < cnt_ref[slot] - turn * half_slot
                            here = pl.ds(
                                pl.multiple_of(member * SLOT + turn * half_slot, half_slot),
                                half_slot,
                            )
                            value = big[
                                part, pl.ds(off_ref[slot] + turn * half_slot, half_slot), :
                            ]
                            value = jnp.where(live, value, 0.0)
                            normed = (value - mean_here) * rstd
                            z = scale * normed + shift
                            square = z * z
                            bent = jnp.tanh(z * (slope + (slope * cubic) * square))
                            half = 0.5 + 0.5 * bent
                            abuf[spot, here, lanes] = jnp.where(live, z * half, 0.0)
                            back = half + z * (1.0 - bent * bent) * (
                                0.5 * slope + (1.5 * slope * cubic) * square
                            )
                            grad = jnp.where(live, cbuf[spot, here, lanes].astype(f32) * back, 0.0)
                            into = pl.ds(
                                pl.multiple_of((slot + 1) * SLOT + turn * half_slot, half_slot),
                                half_slot,
                            )
                            big[2 + part, into, :] = grad
                            tall = (half_slot // 8, 8, LANE)
                            sums[0, :, lanes] += jnp.sum((grad * normed).reshape(tall), 0)
                            sums[1, :, lanes] += jnp.sum(grad.reshape(tall), 0)

                loop(0, team, one)
                act_copy(g).start()

            loop(0, groups, act_group)
            sbuf[2 * b + 1] = jnp.zeros((8, wide), f32)
            sbuf[2 * b + 1, 0:1, :] = jnp.sum(sums[0], 0, keepdims=True)
            sbuf[2 * b + 1, 1:2, :] = jnp.sum(sums[1], 0, keepdims=True)
            exchange_block(2 * b + 1)
            by_gain, by_bias = (row_of(2 * b + 1, line) for line in (0, 1))
            by_gain = sum(by_gain[1:], by_gain[0])
            by_bias = sum(by_bias[1:], by_bias[0])
            tot_ref[0:1, columns] = by_gain
            tot_ref[1:2, columns] = by_bias
            norm[2:3, :] = by_gain / count
            norm[3:4, :] = by_bias / count
            act_copy(groups - 2).wait()
            act_copy(groups - 1).wait()

            def grad_tile(t):
                send_partial(b, t).wait_send()
                for step in range(3):
                    block = t * 3 + step
                    pick = picked_rows(block)
                    here = pl.ds(pl.multiple_of(block * SLOT, SLOT), SLOT)
                    live = lax.broadcasted_iota(i32, (SLOT, LANE), 0) < total - block * SLOT
                    for part in range(2):
                        lanes = slice(part * LANE, (part + 1) * LANE)
                        rstd = norm[1:2, lanes]
                        normed = (big[part, here, :] - norm[0:1, lanes]) * rstd
                        value = (rstd * gain_ref[2 * b + part]) * (
                            pick(2 + part) - norm[3:4, lanes] - normed * norm[2:3, lanes]
                        )
                        stage[2 * b + part, here, :] = jnp.where(live, value, 0.0).astype(bf16)
                send_grad(b, t).start()
                give_grad(b, t).start()

            loop(0, turns, grad_tile)
            if b == 1:
                loop(0, turns, lambda t: send_grad(2, t).start())

        def weight_part(source, qs, low, high, fresh):
            some = pl.ds(low * tile, (high - low) * tile)
            left = jnp.concatenate([source[q, some, :] for q in qs], 1)
            width = LANE * len(qs)
            for number, half in enumerate((own, sib)):
                into = slice(number * fw, (number + 1) * fw)
                value = dot(left, half[some, :], 0, 0)
                if fresh:
                    wacc[:width, into] = value
                else:
                    wacc[:width, into] += value

        def share_of(p, kind):
            return (stg_a, rs_a, ag_a, kind) if p == 0 else (stg_b, rs_b, ag_b, 2 * p - 2 + kind)

        def store_shares(p, kind, line):
            stg, _, _, k = share_of(p, kind)
            width = sizes[p] * LANE
            per = fw // LANE
            for number in range(2):
                base = (side if number == 0 else 1 - side) * per
                for step in range(per):
                    lanes = slice(number * fw + step * LANE, number * fw + (step + 1) * LANE)
                    stg[k, base + step] = wacc[line : line + width, lanes].astype(bf16)

        def scatter(p, kind):
            stg, rs, _, k = share_of(p, kind)
            index = (2 * p + kind) * nodes
            return [
                remote(
                    stg.at[k, (me + step) % nodes],
                    rs.at[k, step],
                    r_s.at[index + step],
                    r_r.at[index + step],
                    node_id(step),
                )
                for step in range(1, nodes)
            ]

        def begin(copies):
            for copy in copies:
                copy.start()

        def finish(copies):
            for copy in copies:
                copy.wait()

        def hop(p):
            src, dst = (hop_a, hop_a) if p == 0 else (hop_b, hop_b)
            k = 0 if p == 0 else 2 * p - 2
            return remote(src.at[k], dst.at[k + 1], h_s.at[p], h_r.at[p], peer_id)

        def spread_share(p, kind):
            if kind == 0:
                _, _, ag, k = share_of(p, 0)
                src = ag.at[k // 2]
            else:
                src = hop_a.at[1] if p == 0 else hop_b.at[2 * p - 1]
            index = (2 * p + kind) * nodes
            which = chip if kind == 0 else 1 - chip
            dst = wag_hbm.at[me, which, :, pl.ds(firsts[p] * LANE, sizes[p] * LANE)]
            copies = [
                remote(src, dst, a_s.at[index + step], a_r.at[index + step], node_id(step))
                for step in range(1, nodes)
            ]
            return copies, pltpu.make_async_copy(src, dst, lsem.at[2 * p + kind])

        def begin_spread(p, kind):
            copies, here = spread_share(p, kind)
            begin(copies)
            here.start()

        def finish_spread(p, kind):
            copies, here = spread_share(p, kind)
            finish(copies)
            here.wait()

        def sum_shares(p, kind):
            finish(scatter(p, kind))
            stg, rs, ag, k = share_of(p, kind)
            value = stg[k, me].astype(f32)
            for step in range(1, nodes):
                value += rs[k, step].astype(f32)
            value = jnp.transpose(value).astype(bf16)
            if kind == 0:
                ag[k // 2] = value
                begin_spread(p, 0)
            else:
                if p == 0:
                    hop_a[0] = value
                else:
                    hop_b[2 * p - 2] = value
                hop(p).start()

        def end_hop(p):
            hop(p).wait()
            begin_spread(p, 1)

        def product(p, t, fresh):
            qs = range(firsts[p], firsts[p] + sizes[p])
            columns = slice(firsts[p] * LANE, (firsts[p] + sizes[p]) * LANE)
            forward_grad(p, t).wait_recv()
            left = jnp.concatenate([ref[q, at(t), :] for ref in (stage, glp, gls, recv) for q in qs], 1)
            right = jnp.concatenate(
                [
                    own_half(wc_ref, columns),
                    own_half(wp_ref, columns),
                    ws_ref[:fw, columns],
                    ws_ref[fw:, columns],
                ],
                1,
            )
            value = dot(left, right, 1, 1)
            for q in range(quarter):
                piece = value[:, q * LANE : (q + 1) * LANE]
                if fresh:
                    big[q, at(t), :] = piece
                else:
                    big[q, at(t), :] += piece

        norm_block(0)
        send_weights(0).wait()
        send_weights(1).wait()
        for low, high in ranges:
            weight_part(stage, (0, 1), low, high, low == 0)
        store_shares(0, 0, 0)
        begin(scatter(0, 0))
        norm_block(1)
        for low, high in ranges:
            weight_part(stage, (2, 3), low, high, low == 0)
        store_shares(1, 0, 0)
        store_shares(2, 0, LANE)
        begin(scatter(1, 0))
        begin(scatter(2, 0))
        sum_shares(0, 0)
        pl.semaphore_wait(credit, 1)

        def pass_on(p, t):
            send_grad(p, t).wait_recv()
            forward_grad(p, t).start()

        for low, high in ranges:
            loop(low, high, lambda t: pass_on(0, t))
            weight_part(glp, (0, 1), low, high, low == 0)
        store_shares(0, 1, 0)
        begin(scatter(0, 1))

        def first_product(t):
            give_grad(0, t).wait_recv()
            give_grad(1, t).wait_recv()
            product(0, t, True)

        loop(0, turns, first_product)
        sum_shares(1, 0)
        sum_shares(2, 0)
        sum_shares(0, 1)
        for low, high in ranges:
            loop(low, high, lambda t: pass_on(1, t))
            weight_part(glp, (2,), low, high, low == 0)
        store_shares(1, 1, 0)
        begin(scatter(1, 1))
        loop(0, turns, lambda t: product(1, t, False))
        end_hop(0)
        sum_shares(1, 1)

        def last_turn(t):
            pass_on(2, t)

            @pl.when(t >= 2)
            def _():
                product(2, t - 2, False)

        for low, high in ranges:
            loop(low, high, last_turn)
            weight_part(glp, (3,), low, high, low == 0)
        store_shares(2, 1, 0)
        begin(scatter(2, 1))
        for t in (turns - 2, turns - 1):
            product(2, t, False)
        end_hop(1)

        def link_copy(g):
            return pltpu.make_async_copy(
                tile_hbm.at[pl.ds(g * team, team), pl.ds(SLOT, 2 * SLOT)],
                tbuf.at[g % 3, :, pl.ds(SLOT, 2 * SLOT)],
                tsem.at[g % 3],
            )

        def slot_copy(g):
            return pltpu.make_async_copy(
                gbuf.at[g % 2],
                slot_hbm.at[pl.ds(pl.multiple_of(g * team * SLOT, SLOT), team * SLOT)],
                gsem.at[g % 2],
            )

        link_copy(0).start()
        link_copy(1).start()
        link_total[...] = jnp.zeros_like(link_total)
        place_row = lax.broadcasted_iota(i32, (SLOT, LANE), 0)

        def slot_group(g):
            @pl.when(g + 2 < groups)
            def _():
                link_copy(g + 2).start()

            link_copy(g).wait()

            @pl.when(g >= 2)
            def _():
                slot_copy(g - 2).wait()

            for member in range(team):
                slot = g * team + member
                live = place_row < cnt_ref[slot]
                scale = column_of(inv_ref, slot)
                for q in range(quarter):
                    value = big[q, pl.ds(off_ref[slot], SLOT), :].astype(bf16).astype(f32)
                    gbuf[g % 2, member * SLOT : (member + 1) * SLOT, q * LANE : (q + 1) * LANE] = (
                        jnp.where(live, value * scale, 0.0).astype(bf16)
                    )
            link = jnp.concatenate([tbuf[g % 3, member, SLOT:, :] for member in range(team)], 1)
            link_total[...] += dot(link, gbuf[g % 2])
            slot_copy(g).start()

        loop(0, groups, slot_group)
        hbuf[...] = link_total[...].astype(bf16)
        half = hbuf.shape[0] // 2
        returns = [
            remote(hbuf.at[:half], hback.at[:half], b_s.at[0], b_r.at[0], node_id(nodes - 1)),
            remote(hbuf.at[half:], hback.at[half:], b_s.at[1], b_r.at[1], node_id(1)),
        ]
        begin(returns)
        sum_shares(2, 1)
        slot_copy(groups - 2).wait()
        slot_copy(groups - 1).wait()
        finish(returns)
        back_ref[:half, :] = jnp.where(me == nodes - 1, 0.0, hback[:half, :].astype(f32)).astype(bf16)
        back_ref[half:, :] = jnp.where(me == 0, 0.0, hback[half:, :].astype(f32)).astype(bf16)
        end_hop(2)

        def settle(t):
            send_own(t).wait_send()
            for b in range(2):
                give_grad(b, t).wait_send()
            for p in range(3):
                send_grad(p, t).wait_send()
                forward_grad(p, t).wait_send()

        loop(0, turns, settle)
        for p in range(3):
            for kind in range(2):
                finish_spread(p, kind)

    anywhere = pl.BlockSpec(memory_space=pl.ANY)
    dma = pltpu.SemaphoreType.DMA
    lane_rows = (quarter, compact, LANE)
    outs = [
        jax.ShapeDtypeStruct((rows, fw), f32),
        jax.ShapeDtypeStruct((rows, fw), bf16),
        jax.ShapeDtypeStruct((2 * SLOT, fw), bf16),
        jax.ShapeDtypeStruct((nodes, 2, LANE, fw), bf16),
        jax.ShapeDtypeStruct((8, fw), f32),
    ]
    scratch = [
        pltpu.VMEM((compact, fw), bf16),
        pltpu.VMEM((compact, fw), bf16),
        pltpu.VMEM(lane_rows, bf16),
        pltpu.VMEM(lane_rows, bf16),
        pltpu.VMEM(lane_rows, bf16),
        pltpu.VMEM(lane_rows, bf16),
        pltpu.VMEM((quarter, padded, LANE), f32),
        pltpu.VMEM((wide, 2 * fw), f32),
        pltpu.VMEM((2, nodes, wide, LANE), bf16),
        pltpu.VMEM((4, nodes, LANE, LANE), bf16),
        pltpu.VMEM((2, nodes, wide, LANE), bf16),
        pltpu.VMEM((4, nodes, LANE, LANE), bf16),
        pltpu.VMEM((1, LANE, wide), bf16),
        pltpu.VMEM((2, LANE, LANE), bf16),
        pltpu.VMEM((2, LANE, wide), bf16),
        pltpu.VMEM((4, LANE, LANE), bf16),
        pltpu.VMEM((3, team * SLOT, fw), bf16),
        pltpu.VMEM((3, team, 3 * SLOT, SLOT), bf16),
        pltpu.VMEM((2, team * SLOT, wide), bf16),
        pltpu.VMEM((2, team * SLOT, wide), f32),
        pltpu.VMEM((2, team * SLOT, fw), bf16),
        pltpu.VMEM((4, 8, wide), f32),
        pltpu.VMEM((4, nodes, 8, wide), f32),
        pltpu.VMEM((8, wide), f32),
        pltpu.VMEM((2, 8, wide), f32),
        pltpu.VMEM((8, wide), f32),
        pltpu.VMEM((2 * SLOT, fw), f32),
        pltpu.VMEM((2 * SLOT, fw), bf16),
        pltpu.VMEM((2 * SLOT, fw), bf16),
        dma((3,)),
        dma((3,)),
        dma((2,)),
        dma((2,)),
        dma((2,)),
        dma((turns,)),
        dma((turns,)),
        dma((2 * turns,)),
        dma((2 * turns,)),
        dma((3 * turns,)),
        dma((3 * turns,)),
        dma((2 * turns,)),
        dma((2 * turns,)),
        dma((3 * turns,)),
        dma((3 * turns,)),
        dma((4 * nodes,)),
        dma((4 * nodes,)),
        dma((6 * nodes,)),
        dma((6 * nodes,)),
        dma((3,)),
        dma((3,)),
        dma((6 * nodes,)),
        dma((6 * nodes,)),
        dma((2,)),
        dma((2,)),
        dma((6,)),
        pltpu.SemaphoreType.REGULAR,
        pltpu.VMEM((2 * fw, fw), bf16),
        dma((2,)),
        dma((2,)),
    ]
    return pl.pallas_call(
        kernel,
        out_shape=outs,
        in_specs=[smem()] * 3 + [anywhere] * 3 + [whole()] * 6,
        out_specs=[anywhere, anywhere, whole(), anywhere, whole()],
        scratch_shapes=scratch,
        compiler_params=pltpu.CompilerParams(
            vmem_limit_bytes=CORE_BYTES, collective_id=2, has_side_effects=True
        ),
        cost_estimate=cost(0, 0),
        name="core",
    )(*lists, features, tiles, cotangent, halo, inv, w_chip, w_peer[0], gain, bias)


def every_row(
    features, tiles, inv, halo, cotangent, w_chip, w_peer, scale, shift, lists, nodes, chips
):
    offsets, counts = lists[:2]
    rows, fw = features.shape
    slots = rows // SLOT
    chip, core_side = lax.axis_index("mp") // 2, lax.rem(lax.axis_index("mp"), 2)
    core_word = core_side.astype(i32)[None]
    half = halo.shape[0] // 2
    others = range(1, chips)
    wide = fw // 2

    def half_of(block, which):
        return lax.dynamic_slice_in_dim(block, which * fw, fw, 0)

    w_all = [w_chip] + w_peer
    got = to_sibling(jnp.concatenate([half_of(w, 1 - core_side) for w in w_all], 0))
    wb = [half_of(w, core_side) for w in w_all] + [got[i * fw : (i + 1) * fw] for i in range(chips)]
    own = aggregate(tiles, inv, features, halo, offsets, counts, 0, rows)
    sib = to_sibling(own)
    received = []
    for b in range(2):
        parts = [partial_product(own, sib, w, core_word, b, wide) for w in w_peer]
        received.append([to_chip(p, -d) for p, d in zip(parts, others, strict=True)])
    gain, bias = scale[None, :], shift[None, :]
    act, grads, totals, weight_grads = None, [], [], []
    for b in range(2):
        lin, stat = linear_stats(
            own, sib, w_chip, core_word, received[b], offsets, slots, b, wide
        )
        stats = exchange(stat, nodes)
        act, grad_pre, sums = activate(
            lin, stats, gain, bias, cotangent, offsets, counts, act, b, wide, rows, fw
        )
        sums = exchange(sums, nodes)
        grad_lin, summed = linear_grad(
            lin, grad_pre, stats, sums, gain, offsets, slots, b, wide, 1
        )
        totals.append(summed)
        mine = [grad_lin] + [to_chip(grad_lin, d) for d in others]
        grads.append(mine + [to_sibling(g) for g in mine])
        sets = []
        for g in mine:
            left = jnp.einsum("rf,rc->fc", own, g, preferred_element_type=f32)
            right = jnp.einsum("rf,rc->fc", sib, g, preferred_element_type=f32)
            sets.append(
                jnp.concatenate(
                    [
                        jnp.where(core_side == 1, right, left),
                        jnp.where(core_side == 1, left, right),
                    ],
                    0,
                )
            )
        share = scatter_sum(jnp.stack(sets), 1)
        shares = [share[0]] + [to_chip(share[d], -d) for d in others]
        full = gather_shares(jnp.stack(shares), 1)
        placed = jnp.zeros((chips,) + full.shape[1:], f32)
        for d in range(chips):
            placed = lax.dynamic_update_slice(
                placed, full[d : d + 1], (lax.rem(chip + d, chips), 0, 0)
            )
        weight_grads.append(placed.reshape(chips * 2 * fw, wide))
    grad_agg = grad_products(grads[0], wb, [0] * len(wb))
    slot_grad, halo_grad = slot_grads(grad_agg, grads[1], wb, wide, tiles, inv, offsets, counts)
    returned = jnp.concatenate(
        [node_shift(halo_grad[:half], -1), node_shift(halo_grad[half:], 1)], 0
    )
    return (
        act,
        slot_grad,
        returned,
        jnp.concatenate(weight_grads, 1),
        jnp.concatenate(totals, 1),
    )


def local(features, weight, scale, shift, cotangent, neighbours, halo_links, valid_rows, send_rows):
    rows, fw = features.shape
    slots = rows // SLOT
    nodes, mp = lax.axis_size("node"), lax.axis_size("mp")
    chips = mp // 2
    chip = lax.axis_index("mp") // 2
    others = range(1, chips)

    counts = jnp.sum(valid_rows.reshape(slots, SLOT), 1).astype(i32)
    order = jnp.arange(slots + 1, dtype=i32)
    offsets = jnp.sum(jnp.where(order[None, :slots] < order[:, None], counts[None, :], 0), 1)

    def chip_rows(which):
        return lax.dynamic_slice_in_dim(weight, which * 2 * fw, 2 * fw, 0).astype(bf16)

    w_sent = [chip_rows(lax.rem(chip + d, chips)) for d in others]
    w_peer = [to_chip(w, d) for w, d in zip(w_sent, others, strict=True)]

    total = jnp.broadcast_to(after(offsets[slots], *w_sent).astype(f32), (8, LANE))
    most = jnp.max(exchange(total, nodes, 3))

    half = send_rows.shape[0]
    send_list = jnp.concatenate([send_rows[:, 1], send_rows[:, 0]], 0)
    send_row = send_list[None, :]
    picked = pick_rows(
        after(features, *w_sent), send_list[:, None], valid_rows[None, :].astype(i32)
    )
    halo = jnp.concatenate([node_shift(picked[:half], 1), node_shift(picked[half:], -1)], 0)
    tiles, inv = count_tiles(after(neighbours.T, picked, most), halo_links.T, counts)
    w_chip = chip_rows(chip)

    compact = rows * 13 // 16 // (3 * SLOT) * (3 * SLOT)
    blocks = jnp.arange(compact // SLOT, dtype=i32) * SLOT
    first = jnp.minimum(
        jnp.sum((offsets[None, 1:] <= blocks[:, None]).astype(i32), 1), slots - 1
    ).astype(i32)
    operands = (
        features,
        tiles,
        inv,
        halo,
        cotangent,
        w_chip,
        w_peer,
        scale,
        shift,
        (offsets, counts, first),
    )

    def all_rows(*args):
        return every_row(*args, nodes, chips)

    if chips == 2 and fw == 4 * LANE and 2 * fw == nodes * LANE and slots % 4 == 0:

        def few_rows(*args):
            act, slot_grad, returned, shares, totals = core(*args, nodes, compact)
            weight_grad = jnp.transpose(shares, (1, 0, 2, 3)).reshape(mp * fw, fw).astype(f32)
            return act, slot_grad, returned, weight_grad, totals

        results = lax.cond(most <= compact, few_rows, all_rows, *operands)
    else:
        results = all_rows(*operands)
    act, slot_grad, returned, weight_grad, totals = results
    input_grad = input_grads(slot_grad, tiles, returned, send_row, counts)
    return act, input_grad, weight_grad, totals[0], totals[1]


def solution(mesh):
    in_specs = (
        P("node", "mp"),
        P(None, "mp"),
        P("mp"),
        P("mp"),
        P("node", "mp"),
        P("node", None),
        P("node", None),
        P("node"),
        P("node", None),
    )
    out_specs = (P("node", "mp"), P("node", "mp"), P(None, "mp"), P("mp"), P("mp"))
    return jax.shard_map(local, mesh=mesh, in_specs=in_specs, out_specs=out_specs, check_vma=False)
```

```python
import functools

import jax
import jax.numpy as jnp
from jax import lax
from jax.experimental import pallas as pl
from jax.experimental.pallas import tpu as pltpu
from jax.sharding import PartitionSpec as P

SLOT = 128
LANE = 128
GROUP = 12
epsilon = 1e-05
VMEM_BYTES = 56 * 1024 * 1024
CORE_BYTES = 61 * 1024 * 1024
MESH = pl.DeviceIdType.MESH
f32, bf16, i32 = jnp.float32, jnp.bfloat16, jnp.int32


def params(**extra):
    return pltpu.CompilerParams(vmem_limit_bytes=VMEM_BYTES, **extra)


def whole():
    return pl.BlockSpec(memory_space=pltpu.VMEM)


def smem():
    return pl.BlockSpec(memory_space=pltpu.SMEM)


def fixed(shape):
    return pl.BlockSpec(shape, lambda i: (0,) * len(shape), pipeline_mode=pl.Buffered(1))


def cost(flops, moved, trans=0):
    return pl.CostEstimate(flops=1, bytes_accessed=1, transcendentals=0)


def dot(a, b, ca=1, cb=0):
    return lax.dot_general(a, b, (((ca,), (cb,)), ((), ())), preferred_element_type=f32)


def after(value, *earlier):
    return lax.optimization_barrier((value,) + earlier)[0]


def chosen(rows_ref, base, count, valid):
    width = rows_ref.shape[1]
    place = lax.broadcasted_iota(i32, (count, width), 0)
    hit = (rows_ref[...] == place + base) & (place < valid)
    return jnp.where(hit, 1.0, 0.0).astype(bf16)


def pick_rows(features, send_column, valid_row):
    rows, width = features.shape
    sends = send_column.shape[0]
    steps = 3
    tile = rows // steps

    def kernel(feat_ref, send_ref, valid_ref, out_ref, total):
        step = pl.program_id(0)

        @pl.when(step == 0)
        def _():
            total[...] = jnp.zeros_like(total)

        wanted = jnp.broadcast_to(send_ref[...], (sends, LANE)) - step * tile
        place = lax.broadcasted_iota(i32, (sends, LANE), 1)
        hot = []
        for part in range(tile // LANE):
            lanes = slice(part * LANE, (part + 1) * LANE)
            hit = (wanted == place + part * LANE) & (valid_ref[:, lanes] > 0)
            hot.append(jnp.where(hit, 1.0, 0.0).astype(bf16))
        total[...] += dot(jnp.concatenate(hot, 1), feat_ref[...])

        @pl.when(step == steps - 1)
        def _():
            out_ref[...] = total[...].astype(bf16)

    return pl.pallas_call(
        kernel,
        grid=(steps,),
        out_shape=jax.ShapeDtypeStruct((sends, width), bf16),
        in_specs=[
            pl.BlockSpec((tile, width), lambda i: (i, 0)),
            fixed((sends, 1)),
            pl.BlockSpec((1, tile), lambda i: (0, i)),
        ],
        out_specs=fixed((sends, width)),
        scratch_shapes=[pltpu.VMEM((sends, width), f32)],
        compiler_params=params(),
        cost_estimate=cost(2 * rows * sends * width, 2 * rows * width),
        name="pick_rows",
    )(features, send_column, valid_row)


def count_tiles(near, links, counts):
    entries, rows = near.shape
    link_entries = links.shape[0]
    slots = rows // SLOT

    def kernel(counts_ref, near_ref, link_ref, tile_ref, inv_ref):
        step = pl.program_id(0)
        row = lax.broadcasted_iota(i32, (SLOT, SLOT), 0)
        column = lax.broadcasted_iota(i32, (SLOT, SLOT), 1)
        link_row = lax.broadcasted_iota(i32, (2 * SLOT, SLOT), 0)

        def one(part, carry):
            lanes = pl.ds(pl.multiple_of(part * SLOT, SLOT), SLOT)
            near_here, link_here = near_ref[:, lanes], link_ref[:, lanes]
            counted = jnp.zeros((SLOT, SLOT), f32)
            for entry in range(entries):
                counted += jnp.where(near_here[entry : entry + 1] == row, 1.0, 0.0)
            linked = jnp.zeros((2 * SLOT, SLOT), f32)
            for entry in range(link_entries):
                linked += jnp.where(link_here[entry : entry + 1] == link_row, 1.0, 0.0)
            degree = 1.0 + jnp.sum(counted, 0, keepdims=True) + jnp.sum(linked, 0, keepdims=True)
            tile = counted + jnp.where(row == column, counted + 2.0, 0.0)
            tile = jnp.where(row < counts_ref[step * GROUP + part], tile, 0.0)
            tile_ref[part, :SLOT, :] = tile.astype(bf16)
            tile_ref[part, SLOT:, :] = linked.astype(bf16)
            inv_ref[part] = jnp.broadcast_to(1.0 / degree, (8, SLOT))
            return carry

        lax.fori_loop(0, GROUP, one, 0)

    return pl.pallas_call(
        kernel,
        grid=(slots // GROUP,),
        out_shape=[
            jax.ShapeDtypeStruct((slots, 3 * SLOT, SLOT), bf16),
            jax.ShapeDtypeStruct((slots, 8, SLOT), f32),
        ],
        in_specs=[
            smem(),
            pl.BlockSpec((entries, GROUP * SLOT), lambda i: (0, i)),
            pl.BlockSpec((link_entries, GROUP * SLOT), lambda i: (0, i)),
        ],
        out_specs=[
            pl.BlockSpec((GROUP, 3 * SLOT, SLOT), lambda i: (i, 0, 0)),
            pl.BlockSpec((GROUP, 8, SLOT), lambda i: (i, 0, 0)),
        ],
        compiler_params=params(),
        cost_estimate=cost(rows * 12000, 6 * rows * SLOT),
        name="count_tiles",
    )(counts, near, links)


def column_of(inv_ref, slot):
    return jnp.transpose(jnp.broadcast_to(inv_ref[slot, 0:1, :], (SLOT, SLOT)))


def aggregate(tiles, inv, features, halo, offsets, counts, first, rows):
    slots = tiles.shape[0]
    width = features.shape[1]
    quarter = width // LANE
    team = 4
    low = first // SLOT // team * team
    high = min(slots, -(-(first + rows) // (SLOT // 2)))
    groups = -(-(high - low) // team)
    low = min(low, slots - groups * team)
    sub = rows // 4

    def kernel(off_ref, counts_ref, tile_hbm, inv_hbm, feat_hbm, halo_ref, out_ref, *scratch):
        held, tile_ref, inv_ref, feat_ref, sems = scratch

        def copies(group):
            here = group * team
            return [
                pltpu.make_async_copy(
                    tile_hbm.at[pl.ds(low + here, team)],
                    tile_ref.at[pl.ds(here, team)],
                    sems.at[0, group],
                ),
                pltpu.make_async_copy(
                    inv_hbm.at[pl.ds(low + here, team)],
                    inv_ref.at[pl.ds(here, team)],
                    sems.at[1, group],
                ),
                pltpu.make_async_copy(
                    feat_hbm.at[pl.ds(pl.multiple_of((low + here) * SLOT, SLOT), team * SLOT)],
                    feat_ref.at[pl.ds(pl.multiple_of(here * SLOT, SLOT), team * SLOT)],
                    sems.at[2, group],
                ),
            ]

        def begin(group, carry):
            for copy in copies(group):
                copy.start()
            return carry

        lax.fori_loop(0, groups, begin, 0)
        row = lax.broadcasted_iota(i32, (SLOT, SLOT), 0)
        column = lax.broadcasted_iota(i32, (SLOT, SLOT), 1)
        unit = jnp.where(row == column, 1.0, 0.0).astype(bf16)

        def step(group, carry):
            for copy in copies(group):
                copy.wait()

            @pl.when(off_ref[low + group * team] < first + rows)
            def _():
                for member in range(team):
                    here = group * team + member
                    tile = dot(unit, tile_ref[here], 1, 1).astype(bf16)
                    source = pl.ds(pl.multiple_of(here * SLOT, SLOT), SLOT)
                    total = dot(tile[:, :SLOT], feat_ref[source, :])
                    total += dot(tile[:, SLOT:], halo_ref[...])
                    scale = column_of(inv_ref, here)
                    start = jnp.clip(off_ref[low + here] - first + SLOT, 0, rows + SLOT)
                    for q in range(quarter):
                        held[q, pl.ds(start, SLOT), :] = (
                            total[:, q * LANE : (q + 1) * LANE] * scale
                        )

            return carry

        lax.fori_loop(0, groups, step, 0)
        total_rows = off_ref[slots] - first

        def finish(part, carry):
            begin_row = pl.multiple_of(part * sub, 16)
            live = lax.broadcasted_iota(i32, (sub, LANE), 0) + begin_row < total_rows
            for q in range(quarter):
                out_ref[pl.ds(begin_row, sub), q * LANE : (q + 1) * LANE] = jnp.where(
                    live, held[q, pl.ds(begin_row + SLOT, sub), :], 0.0
                ).astype(bf16)
            return carry

        lax.fori_loop(0, rows // sub, finish, 0)

    anywhere = pl.BlockSpec(memory_space=pl.ANY)
    return pl.pallas_call(
        kernel,
        out_shape=jax.ShapeDtypeStruct((rows, width), bf16),
        in_specs=[smem(), smem(), anywhere, anywhere, anywhere, whole()],
        out_specs=whole(),
        scratch_shapes=[
            pltpu.VMEM((quarter, rows + 2 * SLOT, LANE), f32),
            pltpu.VMEM((groups * team, 3 * SLOT, SLOT), bf16),
            pltpu.VMEM((groups * team, 8, SLOT), f32),
            pltpu.VMEM((groups * team * SLOT, width), bf16),
            pltpu.SemaphoreType.DMA((3, groups)),
        ],
        compiler_params=params(),
        cost_estimate=cost(2 * rows * 3 * SLOT * width, 4 * rows * width),
        name="aggregate",
    )(offsets, counts, tiles, inv, features, halo)


def partial_product(own, sib, weight, core, block, width):
    rows, depth = own.shape
    tile = rows // 2 if rows > 1600 else rows

    def kernel(core_ref, a_ref, b_ref, w_ref, out_ref):
        core = core_ref[0]
        first = w_ref[pl.ds(pl.multiple_of(core * depth, depth), depth), :]
        second = w_ref[pl.ds(pl.multiple_of((1 - core) * depth, depth), depth), :]
        out_ref[...] = (dot(a_ref[...], first) + dot(b_ref[...], second)).astype(bf16)

    return pl.pallas_call(
        kernel,
        grid=(rows // tile,),
        out_shape=jax.ShapeDtypeStruct((rows, width), bf16),
        in_specs=[smem()]
        + [pl.BlockSpec((tile, depth), lambda i: (i, 0))] * 2
        + [pl.BlockSpec((2 * depth, width), lambda i: (0, block))],
        out_specs=pl.BlockSpec((tile, width), lambda i: (i, 0)),
        compiler_params=params(),
        cost_estimate=cost(4 * rows * depth * width, 4 * rows * depth + 2 * rows * width),
        name="partial_product",
    )(core, own, sib, weight)


def linear_stats(own, sib, weight, core, received, offsets, slots, block, width):
    rows, depth = own.shape
    tile = rows // 2
    sub = rows // 8
    parts = width // LANE
    others = len(received)

    def kernel(off_ref, core_ref, a_ref, b_ref, w_ref, *rest):
        recv_refs, (lin_ref, stat_ref) = rest[:others], rest[others:]
        step = pl.program_id(0)
        core = core_ref[0]
        first = w_ref[pl.ds(pl.multiple_of(core * depth, depth), depth), :]
        second = w_ref[pl.ds(pl.multiple_of((1 - core) * depth, depth), depth), :]
        total = off_ref[slots]

        @pl.when(step == 0)
        def _():
            stat_ref[...] = jnp.zeros_like(stat_ref)
            stat_ref[2:3, :] = jnp.full((1, width), total.astype(f32), f32)

        for piece in range(tile // sub):
            here_rows = slice(piece * sub, (piece + 1) * sub)
            value = dot(a_ref[here_rows, :], first) + dot(b_ref[here_rows, :], second)
            for ref in recv_refs:
                value += ref[here_rows, :].astype(f32)
            for part in range(parts):
                lin_ref[part, here_rows, :] = value[:, part * LANE : (part + 1) * LANE]
            begin = step * tile + piece * sub
            before = jnp.minimum(begin, total)
            here = jnp.minimum(begin + sub, total) - before
            seen, new = before.astype(f32), here.astype(f32)
            both = jnp.full((1, width), jnp.maximum(seen + new, 1.0), f32)
            live = lax.broadcasted_iota(i32, (sub, width), 0) < here
            mean_here = jnp.sum(jnp.where(live, value, 0.0), 0, keepdims=True) / jnp.full(
                (1, width), jnp.maximum(new, 1.0), f32
            )
            centred = jnp.where(live, value - mean_here, 0.0)
            squares = jnp.sum(centred * centred, 0, keepdims=True)
            mean, held = stat_ref[0:1, :], stat_ref[1:2, :]
            gap = mean_here - mean
            ratio = new / both
            stat_ref[0:1, :] = mean + gap * ratio
            stat_ref[1:2, :] = held + squares + gap * gap * (seen * ratio)

    return pl.pallas_call(
        kernel,
        grid=(rows // tile,),
        out_shape=[
            jax.ShapeDtypeStruct((parts, rows + SLOT, LANE), f32),
            jax.ShapeDtypeStruct((8, width), f32),
        ],
        in_specs=[smem(), smem()]
        + [pl.BlockSpec((tile, depth), lambda i: (i, 0))] * 2
        + [pl.BlockSpec((2 * depth, width), lambda i: (0, block))]
        + [pl.BlockSpec((tile, width), lambda i: (i, 0))] * others,
        out_specs=[
            pl.BlockSpec((parts, tile, LANE), lambda i: (0, i, 0)),
            pl.BlockSpec((8, width), lambda i: (0, 0)),
        ],
        compiler_params=params(),
        cost_estimate=cost(4 * rows * depth * width, 4 * rows * depth + 6 * rows * width),
        name="linear_stats",
    )(offsets, core, own, sib, weight, *received)


def exchange(block, nodes, number=1):
    def kernel(in_ref, out_ref, held, send_sem, recv_sem):
        me = lax.axis_index("node")
        barrier = pltpu.get_barrier_semaphore()
        for step in range(1, nodes):
            pl.semaphore_signal(
                barrier,
                inc=1,
                device_id={"node": lax.rem(me + step, nodes)},
                device_id_type=MESH,
            )
        pl.semaphore_wait(barrier, nodes - 1)
        copies = []
        for step in range(1, nodes):
            copy = pltpu.make_async_remote_copy(
                src_ref=in_ref,
                dst_ref=held.at[step],
                send_sem=send_sem.at[step],
                recv_sem=recv_sem.at[step],
                device_id={"node": lax.rem(me + step, nodes)},
                device_id_type=MESH,
            )
            copy.start()
            copies.append(copy)
        out_ref[0] = in_ref[...]
        for copy in copies:
            copy.wait()
        for step in range(1, nodes):
            out_ref[step] = held[step]

    return pl.pallas_call(
        kernel,
        out_shape=jax.ShapeDtypeStruct((nodes,) + block.shape, f32),
        in_specs=[whole()],
        out_specs=whole(),
        scratch_shapes=[
            pltpu.VMEM((nodes,) + block.shape, f32),
            pltpu.SemaphoreType.DMA((nodes,)),
            pltpu.SemaphoreType.DMA((nodes,)),
        ],
        compiler_params=params(collective_id=number, has_side_effects=True),
        cost_estimate=cost(0, nodes * block.size * 4),
        name="exchange",
    )(block)


def merge_stats(stat_ref, width):
    nodes = stat_ref.shape[0]
    total = stat_ref[0, 2:3, :width]
    for node in range(1, nodes):
        total += stat_ref[node, 2:3, :width]
    mean = stat_ref[0, 2:3, :width] * stat_ref[0, 0:1, :width]
    for node in range(1, nodes):
        mean += stat_ref[node, 2:3, :width] * stat_ref[node, 0:1, :width]
    mean = mean / total
    spread = jnp.zeros_like(mean)
    for node in range(nodes):
        gap = stat_ref[node, 0:1, :width] - mean
        spread += stat_ref[node, 1:2, :width] + stat_ref[node, 2:3, :width] * gap * gap
    return total, mean, lax.rsqrt(spread / total + epsilon)


def activate(
    linear, stats, scale, shift, cotangent, offsets, counts, held, block, width, rows, feat_width
):
    nodes = stats.shape[0]
    slots = rows // SLOT
    parts = width // LANE
    compact = linear.shape[1]
    slope = 0.7978845608028654
    cubic = 0.044715
    half_slot = SLOT // 2

    def kernel(off_ref, counts_ref, lin_ref, stat_ref, scale_ref, shift_ref, cot_ref, *rest):
        act_ref, grad_ref, sum_ref, norm, sums = rest[-5:]
        step = pl.program_id(0)

        @pl.when(step == 0)
        def _():
            _, mean, rstd = merge_stats(stat_ref, width)
            norm[0:1, :] = mean
            norm[1:2, :] = rstd
            sums[...] = jnp.zeros_like(sums)

        place = lax.broadcasted_iota(i32, (half_slot, LANE), 0)

        def one(member, carry):
            slot = step * GROUP + member
            start = off_ref[slot]
            for side in range(2):
                live = place < counts_ref[slot] - side * half_slot
                here = pl.ds(pl.multiple_of(member * SLOT + side * half_slot, 16), half_slot)
                from_row = pl.ds(start + side * half_slot, half_slot)
                for part in range(parts):
                    lanes = slice(part * LANE, (part + 1) * LANE)
                    mean, rstd = norm[0:1, lanes], norm[1:2, lanes]
                    value = jnp.where(live, lin_ref[part, from_row, :], 0.0)
                    normed = (value - mean) * rstd
                    z = scale_ref[:, lanes] * normed + shift_ref[:, lanes]
                    square = z * z
                    bent = jnp.tanh(z * (slope + (slope * cubic) * square))
                    half = 0.5 + 0.5 * bent
                    act_ref[here, lanes] = jnp.where(live, z * half, 0.0)
                    back = half + z * (1.0 - bent * bent) * (
                        0.5 * slope + (1.5 * slope * cubic) * square
                    )
                    grad = jnp.where(live, cot_ref[here, lanes].astype(f32) * back, 0.0)
                    grad_ref[part, from_row, :] = grad
                    tall = (half_slot // 8, 8, LANE)
                    sums[0, :, lanes] += jnp.sum((grad * normed).reshape(tall), 0)
                    sums[1, :, lanes] += jnp.sum(grad.reshape(tall), 0)
            return carry

        lax.fori_loop(0, GROUP, one, 0)

        @pl.when(step == slots // GROUP - 1)
        def _():
            sum_ref[...] = jnp.zeros_like(sum_ref)
            sum_ref[0:1, :] = jnp.sum(sums[0], 0, keepdims=True)
            sum_ref[1:2, :] = jnp.sum(sums[1], 0, keepdims=True)

    given = [] if held is None else [held]
    return pl.pallas_call(
        kernel,
        grid=(slots // GROUP,),
        out_shape=[
            jax.ShapeDtypeStruct((rows, feat_width), f32),
            jax.ShapeDtypeStruct((parts, compact, LANE), f32),
            jax.ShapeDtypeStruct((8, width), f32),
        ],
        in_specs=[
            smem(),
            smem(),
            fixed((parts, compact, LANE)),
            fixed(stats.shape),
            pl.BlockSpec((1, width), lambda i: (0, block)),
            pl.BlockSpec((1, width), lambda i: (0, block)),
            pl.BlockSpec((GROUP * SLOT, width), lambda i: (i, block)),
        ]
        + [pl.BlockSpec(memory_space=pl.ANY)] * len(given),
        out_specs=[
            pl.BlockSpec((GROUP * SLOT, width), lambda i: (i, block)),
            fixed((parts, compact, LANE)),
            fixed((8, width)),
        ],
        scratch_shapes=[pltpu.VMEM((8, width), f32), pltpu.VMEM((2, 8, width), f32)],
        input_output_aliases={7: 0} if given else {},
        compiler_params=params(),
        cost_estimate=cost(60 * rows * width, 14 * rows * width, rows * width),
        name="activate",
    )(offsets, counts, linear, stats, scale, shift, cotangent, *given)


def linear_grad(linear, grad, stats, sums, scale, offsets, slots, block, width, pieces):
    parts, padded, _ = linear.shape
    rows = padded - SLOT
    tile = rows // 2
    sub = rows // 16
    nodes = stats.shape[0]
    share = width // pieces

    def kernel(off_ref, lin_ref, grad_ref, stat_ref, sums_ref, scale_ref, *rest):
        out_refs, (total_ref, norm) = rest[:pieces], rest[pieces:]
        step = pl.program_id(0)

        @pl.when(step == 0)
        def _():
            total, mean, rstd = merge_stats(stat_ref, width)
            by_gain = sums_ref[0, 0:1, :width]
            by_bias = sums_ref[0, 1:2, :width]
            for node in range(1, nodes):
                by_gain += sums_ref[node, 0:1, :width]
                by_bias += sums_ref[node, 1:2, :width]
            norm[0:1, :] = mean
            norm[1:2, :] = rstd
            norm[2:3, :] = by_gain / total
            norm[3:4, :] = by_bias / total
            norm[4:5, :] = rstd * scale_ref[...]
            total_ref[...] = jnp.zeros_like(total_ref)
            total_ref[0:1, :] = by_gain
            total_ref[1:2, :] = by_bias

        def one(piece, carry):
            begin = pl.multiple_of(piece * sub, 16)
            here = pl.ds(begin, sub)
            live = (
                lax.broadcasted_iota(i32, (sub, LANE), 0) + (step * tile + begin) < off_ref[slots]
            )
            for part in range(parts):
                lanes = slice(part * LANE, (part + 1) * LANE)
                normed = (lin_ref[part, here, :] - norm[0:1, lanes]) * norm[1:2, lanes]
                value = norm[4:5, lanes] * (
                    grad_ref[part, here, :] - norm[3:4, lanes] - normed * norm[2:3, lanes]
                )
                into, at = divmod(part * LANE, share)
                out_refs[into][here, at : at + LANE] = jnp.where(live, value, 0.0).astype(bf16)
            return carry

        lax.fori_loop(0, tile // sub, one, 0)

    return pl.pallas_call(
        kernel,
        grid=(rows // tile,),
        out_shape=[jax.ShapeDtypeStruct((rows, share), bf16)] * pieces
        + [jax.ShapeDtypeStruct((8, width), f32)],
        in_specs=[
            smem(),
            pl.BlockSpec((parts, tile, LANE), lambda i: (0, i, 0)),
            pl.BlockSpec((parts, tile, LANE), lambda i: (0, i, 0)),
            fixed(stats.shape),
            fixed(sums.shape),
            pl.BlockSpec((1, width), lambda i: (0, block)),
        ],
        out_specs=[pl.BlockSpec((tile, share), lambda i: (i, 0))] * pieces
        + [pl.BlockSpec((8, width), lambda i: (0, 0))],
        scratch_shapes=[pltpu.VMEM((8, width), f32)],
        compiler_params=params(),
        cost_estimate=cost(10 * rows * width, 10 * rows * width),
        name="linear_grad",
    )(offsets, linear, grad, stats, sums, scale)


def grad_products(grads, weights, places):
    rows = grads[0].shape[0]
    feat_width = weights[0].shape[0]
    parts = feat_width // LANE
    tile = rows // 4
    sub = tile // 2
    count = len(grads)
    depth = sum(g.shape[1] for g in grads)

    def kernel(*refs):
        out_ref = refs[-1]
        right = jnp.concatenate([ref[...] for ref in refs[count : 2 * count]], 1)
        for piece in range(tile // sub):
            here = slice(piece * sub, (piece + 1) * sub)
            left = jnp.concatenate([ref[here, :] for ref in refs[:count]], 1)
            value = dot(left, right, 1, 1)
            for part in range(parts):
                out_ref[part, here, :] = value[:, part * LANE : (part + 1) * LANE]

    def column(place, width):
        return pl.BlockSpec((feat_width, width), lambda i: (0, place))

    return pl.pallas_call(
        kernel,
        grid=(rows // tile,),
        out_shape=jax.ShapeDtypeStruct((parts, rows, LANE), f32),
        in_specs=[pl.BlockSpec((tile, g.shape[1]), lambda i: (i, 0)) for g in grads]
        + [column(p // g.shape[1], g.shape[1]) for p, g in zip(places, grads, strict=True)],
        out_specs=pl.BlockSpec((parts, tile, LANE), lambda i: (0, i, 0)),
        compiler_params=params(),
        cost_estimate=cost(2 * rows * feat_width * depth, rows * (4 * feat_width + 2 * depth)),
        name="grad_products",
    )(*grads, *weights)


def slot_grads(held, grads, weights, place, tiles, inv, offsets, counts):
    slots = tiles.shape[0]
    parts, rows, _ = held.shape
    width = parts * LANE
    count = len(grads)
    share = grads[0].shape[1]
    blocks = 8
    sub = rows // blocks
    team = 4

    def kernel(off_ref, counts_ref, held_ref, *refs):
        grad_refs, weight_refs = refs[:count], refs[count : 2 * count]
        tile_ref, inv_ref, out_ref, halo_ref, total, link_total, sems = refs[2 * count :]

        def copy(block):
            here = pl.ds(pl.multiple_of(block * sub, 16), sub)
            return pltpu.make_async_copy(
                held_ref.at[:, here, :], total.at[:, here, :], sems.at[block]
            )

        for block in range(blocks):
            copy(block).start()
        right = jnp.concatenate([ref[...] for ref in weight_refs], 1)
        link_total[...] = jnp.zeros_like(link_total)

        def add(block, carry):
            here = pl.ds(pl.multiple_of(block * sub, 16), sub)
            value = dot(jnp.concatenate([ref[here, :] for ref in grad_refs], 1), right, 1, 1)
            copy(block).wait()
            for part in range(parts):
                total[part, here, :] += value[:, part * LANE : (part + 1) * LANE]
            return carry

        lax.fori_loop(0, blocks, add, 0)
        place_row = lax.broadcasted_iota(i32, (SLOT, LANE), 0)

        def one(step, carry):
            pieces = []
            for member in range(team):
                slot = step * team + member
                start = off_ref[slot]
                live = place_row < counts_ref[slot]
                scale = column_of(inv_ref, slot)
                row = []
                for part in range(parts):
                    value = total[part, pl.ds(start, SLOT), :].astype(bf16).astype(f32)
                    row.append(jnp.where(live, value * scale, 0.0).astype(bf16))
                piece = jnp.concatenate(row, 1)
                out_ref[pl.ds(pl.multiple_of(slot * SLOT, SLOT), SLOT), :] = piece
                pieces.append(piece)
            link = jnp.concatenate(
                [tile_ref[step * team + member, SLOT:, :] for member in range(team)], 1
            )
            link_total[...] += dot(link, jnp.concatenate(pieces, 0))
            return carry

        lax.fori_loop(0, slots // team, one, 0)
        halo_ref[...] = link_total[...].astype(bf16)

    return pl.pallas_call(
        kernel,
        grid=(1,),
        out_shape=[
            jax.ShapeDtypeStruct((slots * SLOT, width), bf16),
            jax.ShapeDtypeStruct((2 * SLOT, width), bf16),
        ],
        in_specs=[smem(), smem(), pl.BlockSpec(memory_space=pl.ANY)]
        + [fixed((rows, share))] * count
        + [
            pl.BlockSpec(
                (width, share), lambda i: (0, place // share), pipeline_mode=pl.Buffered(1)
            )
        ]
        * count
        + [fixed(tiles.shape), fixed(inv.shape)],
        out_specs=[fixed((slots * SLOT, width)), fixed((2 * SLOT, width))],
        scratch_shapes=[
            pltpu.VMEM((parts, rows + SLOT, LANE), f32),
            pltpu.VMEM((2 * SLOT, width), f32),
            pltpu.SemaphoreType.DMA((blocks,)),
        ],
        compiler_params=params(),
        cost_estimate=cost(4 * slots * SLOT * SLOT * width, 6 * slots * SLOT * width),
        name="slot_grads",
    )(offsets, counts, held, *grads, *weights, tiles, inv)


def input_grads(slot_grad, tiles, returned, send_row, counts):
    rows, width = slot_grad.shape
    sends = send_row.shape[1]

    def kernel(counts_ref, grad_ref, tile_ref, back_ref, send_ref, out_ref):
        step = pl.program_id(0)

        def pair(turn, carry):
            for side in range(2):
                member = turn * 2 + side
                slot = step * GROUP + member
                here = pl.ds(pl.multiple_of(member * SLOT, SLOT), SLOT)
                hot = chosen(send_ref, slot * SLOT, SLOT, counts_ref[slot])
                value = dot(tile_ref[member], grad_ref[here, :])
                out_ref[here, :] = value + dot(hot, back_ref[...])
            return carry

        lax.fori_loop(0, GROUP // 2, pair, 0)

    return pl.pallas_call(
        kernel,
        grid=(rows // (GROUP * SLOT),),
        out_shape=jax.ShapeDtypeStruct((rows, width), f32),
        in_specs=[
            smem(),
            pl.BlockSpec((GROUP * SLOT, width), lambda i: (i, 0)),
            pl.BlockSpec((GROUP, SLOT, SLOT), lambda i: (i, 0, 0)),
            fixed((sends, width)),
            fixed((1, sends)),
        ],
        out_specs=pl.BlockSpec((GROUP * SLOT, width), lambda i: (i, 0)),
        compiler_params=params(),
        cost_estimate=cost(2 * rows * 3 * SLOT * width, 6 * rows * width),
        name="input_grads",
    )(counts, slot_grad, tiles, returned, send_row)


def last_pass(act, slot_grad, returned, shares, tiles, send_row, counts):
    rows, width = slot_grad.shape
    sends = send_row.shape[1]
    nodes = shares.shape[0]
    group = rows // SLOT // nodes

    def kernel(counts_ref, act_ref, grad_ref, tile_ref, back_ref, send_ref, share_ref, *outs):
        act_out, grad_out, weight_out = outs
        step = pl.program_id(0)
        act_out[...] = act_ref[...]
        weight_out[...] = share_ref[...].astype(f32).reshape(weight_out.shape)

        def pair(turn, carry):
            for side in range(2):
                member = turn * 2 + side
                slot = step * group + member
                here = pl.ds(pl.multiple_of(member * SLOT, SLOT), SLOT)
                hot = chosen(send_ref, slot * SLOT, SLOT, counts_ref[slot])
                value = dot(tile_ref[member], grad_ref[here, :])
                grad_out[here, :] = value + dot(hot, back_ref[...])
            return carry

        lax.fori_loop(0, group // 2, pair, 0)

    return pl.pallas_call(
        kernel,
        grid=(nodes,),
        out_shape=[
            jax.ShapeDtypeStruct((rows, width), f32),
            jax.ShapeDtypeStruct((rows, width), f32),
            jax.ShapeDtypeStruct((2, nodes, LANE, width), f32),
        ],
        in_specs=[
            smem(),
            pl.BlockSpec((group * SLOT, width), lambda i: (i, 0)),
            pl.BlockSpec((group * SLOT, width), lambda i: (i, 0)),
            pl.BlockSpec((group, SLOT, SLOT), lambda i: (i, 0, 0)),
            fixed((sends, width)),
            fixed((1, sends)),
            pl.BlockSpec((1, 2, LANE, width), lambda i: (i, 0, 0, 0)),
        ],
        out_specs=[
            pl.BlockSpec((group * SLOT, width), lambda i: (i, 0)),
            pl.BlockSpec((group * SLOT, width), lambda i: (i, 0)),
            pl.BlockSpec((2, 1, LANE, width), lambda i: (0, i, 0, 0)),
        ],
        compiler_params=params(),
        cost_estimate=cost(0, 0),
        name="last_pass",
    )(counts, act, slot_grad, tiles, returned, send_row, shares)


def node_shift(block, distance):
    nodes = range(lax.axis_size("node"))
    return lax.ppermute(
        block, "node", [(i - distance, i) for i in nodes if i - distance in nodes]
    )


def to_sibling(block):
    return lax.ppermute(block, "mp", [(i, i ^ 1) for i in range(lax.axis_size("mp"))])


def to_chip(block, distance):
    size = lax.axis_size("mp")
    return lax.ppermute(block, "mp", [(i, (i + 2 * distance) % size) for i in range(size)])


def node_flip(block, bit):
    return lax.ppermute(block, "node", [(i, i ^ bit) for i in range(lax.axis_size("node"))])


def scatter_sum(value, axis):
    me, bit = lax.axis_index("node"), 1
    while bit < lax.axis_size("node"):
        mine = lax.rem(me // bit, 2)
        half = value.shape[axis] // 2
        keep = lax.dynamic_slice_in_dim(value, mine * half, half, axis)
        give = lax.dynamic_slice_in_dim(value, (1 - mine) * half, half, axis)
        value = keep + node_flip(give, bit)
        bit *= 2
    return value


def gather_shares(value, axis):
    me, bit = lax.axis_index("node"), lax.axis_size("node") // 2
    while bit >= 1:
        mine = lax.rem(me // bit, 2)
        other = node_flip(value, bit)
        low = jnp.where(mine == 0, value, other)
        high = jnp.where(mine == 0, other, value)
        value = jnp.concatenate([low, high], axis)
        bit //= 2
    return value


def core(
    features, weight, cotangent, near, links, send_row, scale, shift, lists, nodes, compact
):
    rows, fw = features.shape
    entries, link_entries = near.shape[0], links.shape[0]
    gain, bias = (v.reshape(fw // LANE, 1, LANE) for v in (scale, shift))
    slots = rows // SLOT
    quarter = fw // LANE
    tile = 3 * SLOT
    turns = compact // tile
    padded = rows + 2 * SLOT
    wide = fw // 2
    team = 4
    groups = slots // team
    ranges = [(0, 4), (4, 8), (8, turns)]
    slope, cubic = 0.7978845608028654, 0.044715
    sizes = {0: 2, 1: 1, 2: 1}
    firsts = {0: 0, 1: 2, 2: 3}

    def kernel(*refs):
        off_ref, cnt_ref, first_ref, feat_hbm, w_hbm, cot_hbm = refs[:6]
        near_ref, link_ref, send_ref, gain_ref, bias_ref = refs[6:11]
        act_hbm, slot_hbm, back_ref, wag_hbm, tot_ref, tile_hbm = refs[11:17]
        own, sib, stage, recv, glp, gls, big, wacc = refs[17:25]
        stg_a, stg_b, rs_a, rs_b, ag_a, ag_b, hop_a, hop_b = refs[25:33]
        fbuf, tbuf, cbuf, abuf, gbuf, sbuf, ebuf, st, sums, norm, link_total, hbuf, hback = refs[33:46]
        fsem, tsem, csem, asem, gsem = refs[46:51]
        d1s, d1r, x1s, x1r, x2s, x2r, d2s, d2r, f2s, f2r = refs[51:61]
        e_s, e_r, r_s, r_r, h_s, h_r, a_s, a_r, b_s, b_r, lsem, credit = refs[61:73]
        ws_ref, w_s, w_r, wc_ref, wp_ref, wsem, v_s, v_r, halo_ref, inv_ref = refs[73:83]

        me = lax.axis_index("node")
        place = lax.axis_index("mp")
        chip, side = place // 2, place % 2
        peer_id = {"mp": (1 - chip) * 2 + side}
        sib_id = {"mp": chip * 2 + 1 - side}
        total = off_ref[slots]

        def node_id(step):
            return {"node": (me + step) % nodes}

        def weight_copy(mine, q):
            chosen_rows = chip if mine else 1 - chip
            return pltpu.make_async_copy(
                w_hbm.at[
                    pl.ds(pl.multiple_of(chosen_rows * 2 * fw, SLOT), 2 * fw),
                    pl.ds(q * LANE, LANE),
                ],
                big.at[q, pl.ds(mine * 2 * fw, 2 * fw)],
                wsem.at[mine * quarter + q],
            )

        for mine in range(2):
            for q in range(quarter):
                weight_copy(mine, q).start()
        barrier = pltpu.get_barrier_semaphore()
        for target in [peer_id, sib_id] + [node_id(step) for step in range(1, nodes)]:
            pl.semaphore_signal(barrier, inc=1, device_id=target, device_id_type=MESH)

        def remote(src, dst, send, arrive, target):
            return pltpu.make_async_remote_copy(
                src_ref=src,
                dst_ref=dst,
                send_sem=send,
                recv_sem=arrive,
                device_id=target,
                device_id_type=MESH,
            )

        def at(turn):
            return pl.ds(pl.multiple_of(turn * tile, SLOT), tile)

        def own_half(ref, columns):
            return ref[pl.ds(pl.multiple_of(side * fw, SLOT), fw), columns]

        def sib_half(ref, columns):
            return ref[pl.ds(pl.multiple_of((1 - side) * fw, SLOT), fw), columns]

        def loop(low, high, body):
            def step(index, carry):
                body(index)
                return carry

            lax.fori_loop(low, high, step, 0)

        def send_own(t):
            return remote(own.at[at(t)], sib.at[at(t)], d1s.at[t], d1r.at[t], sib_id)

        def send_partial(b, t):
            two = pl.ds(2 * b, 2)
            return remote(
                stage.at[two, at(t)],
                recv.at[two, at(t)],
                x1s.at[b * turns + t],
                x1r.at[b * turns + t],
                peer_id,
            )

        def send_grad(p, t):
            some = pl.ds(firsts[p], sizes[p])
            index = p * turns + t
            return remote(
                stage.at[some, at(t)], glp.at[some, at(t)], x2s.at[index], x2r.at[index], peer_id
            )

        def give_grad(b, t):
            two = pl.ds(2 * b, 2)
            index = b * turns + t
            return remote(
                stage.at[two, at(t)], gls.at[two, at(t)], d2s.at[index], d2r.at[index], sib_id
            )

        def forward_grad(p, t):
            some = pl.ds(firsts[p], sizes[p])
            index = p * turns + t
            return remote(
                glp.at[some, at(t)], recv.at[some, at(t)], f2s.at[index], f2r.at[index], sib_id
            )

        def picked_rows(block):
            slot = first_ref[block]
            base = block * SLOT
            starts = []
            for step in range(3):
                here = jnp.minimum(slot + step, slots - 1)
                starts.append(
                    jnp.clip(here * SLOT + base - off_ref[here] + SLOT, 0, padded - SLOT)
                )
            place_row = lax.broadcasted_iota(i32, (SLOT, LANE), 0)
            one = place_row < off_ref[jnp.minimum(slot + 1, slots)] - base
            two = place_row < off_ref[jnp.minimum(slot + 2, slots)] - base
            live = place_row < total - base

            def pick(q):
                value = jnp.where(two, big[q, pl.ds(starts[1], SLOT), :], big[q, pl.ds(starts[2], SLOT), :])
                value = jnp.where(one, big[q, pl.ds(starts[0], SLOT), :], value)
                return jnp.where(live, value, 0.0)

            return pick

        def send_weights(which):
            src = wp_ref if which else wc_ref
            return remote(
                src.at[pl.ds(pl.multiple_of((1 - side) * fw, SLOT), fw)],
                ws_ref.at[pl.ds(which * fw, fw)],
                w_s.at[which],
                w_r.at[which],
                sib_id,
            )

        def send_peer_weights(half, number):
            columns = pl.ds(half * wide, wide)
            return remote(
                gbuf.at[number, :, columns],
                wp_ref.at[pl.ds(number * fw, fw), columns],
                v_s.at[2 * half + number],
                v_r.at[2 * half + number],
                peer_id,
            )

        def loads(g):
            return pltpu.make_async_copy(
                feat_hbm.at[pl.ds(pl.multiple_of(g * team * SLOT, SLOT), team * SLOT)],
                fbuf.at[g % 3],
                fsem.at[g % 3],
            )

        for g in range(3):
            loads(g).start()
        for q in range(quarter):
            lanes = slice(q * LANE, (q + 1) * LANE)
            weight_copy(0, q).wait()
            for number in range(2):
                gbuf[number, :, lanes] = big[q, number * fw : (number + 1) * fw, :].astype(bf16)
        pl.semaphore_wait(barrier, nodes + 1)
        for half in range(2):
            for number in range(2):
                send_peer_weights(half, number).start()
        for q in range(quarter):
            weight_copy(1, q).wait()
            wc_ref[:, q * LANE : (q + 1) * LANE] = big[q, 2 * fw : 4 * fw, :].astype(bf16)

        wanted = [
            jnp.transpose(
                jnp.broadcast_to(
                    send_ref[:, part * LANE : (part + 1) * LANE].astype(f32), (LANE, LANE)
                )
            )
            for part in range(2)
        ]
        wanted = jnp.concatenate(wanted, 0).astype(i32)
        lane = lax.broadcasted_iota(i32, (2 * SLOT, LANE), 1)
        link_total[...] = jnp.zeros_like(link_total)

        def pick_group(g):
            loads(g).wait()
            hot = []
            for member in range(team):
                slot = g * team + member
                hit = (wanted == lane + slot * SLOT) & (lane < cnt_ref[slot])
                hot.append(jnp.where(hit, 1.0, 0.0).astype(bf16))
            link_total[...] += dot(jnp.concatenate(hot, 1), fbuf[g % 3])

            @pl.when(g + 3 < groups)
            def _():
                loads(g + 3).start()

        loop(0, groups, pick_group)
        hbuf[...] = link_total[...].astype(bf16)
        half_rows = SLOT
        halo_in = [
            remote(
                hbuf.at[:half_rows], halo_ref.at[:half_rows], b_s.at[2], b_r.at[2], node_id(1)
            ),
            remote(
                hbuf.at[half_rows:],
                halo_ref.at[half_rows:],
                b_s.at[3],
                b_r.at[3],
                node_id(nodes - 1),
            ),
        ]
        for copy in halo_in:
            copy.start()
        for g in range(2):
            loads(g).start()

        row = lax.broadcasted_iota(i32, (SLOT, SLOT), 0)
        column = lax.broadcasted_iota(i32, (SLOT, SLOT), 1)
        link_row = lax.broadcasted_iota(i32, (2 * SLOT, SLOT), 0)
        unit = jnp.where(row == column, 1.0, 0.0).astype(bf16)
        first_half, second_half = slice(0, wide), slice(wide, fw)

        def tile_copy(g):
            return pltpu.make_async_copy(
                tbuf.at[g % 3], tile_hbm.at[pl.ds(g * team, team)], tsem.at[g % 3]
            )

        def count_group(g):
            spot = g % 3

            def one(member):
                slot = g * team + member
                lanes = pl.ds(pl.multiple_of(slot * SLOT, SLOT), SLOT)
                near_here, link_here = near_ref[:, lanes], link_ref[:, lanes]
                counted = jnp.zeros((SLOT, SLOT), f32)
                for entry in range(entries):
                    counted += jnp.where(near_here[entry : entry + 1] == row, 1.0, 0.0)
                linked = jnp.zeros((2 * SLOT, SLOT), f32)
                for entry in range(link_entries):
                    linked += jnp.where(link_here[entry : entry + 1] == link_row, 1.0, 0.0)
                degree = (
                    1.0 + jnp.sum(counted, 0, keepdims=True) + jnp.sum(linked, 0, keepdims=True)
                )
                matrix = counted + jnp.where(row == column, counted + 2.0, 0.0)
                matrix = jnp.where(row < cnt_ref[slot], matrix, 0.0)
                tbuf[spot, member, :SLOT, :] = matrix.astype(bf16)
                tbuf[spot, member, SLOT:, :] = linked.astype(bf16)
                inv_ref[slot] = jnp.broadcast_to(1.0 / degree, (8, SLOT))

            loop(0, team, one)
            tile_copy(g).start()

        count_group(0)
        count_group(1)
        for copy in halo_in:
            copy.wait()
        halo_ref[:half_rows, :] = jnp.where(
            me == 0, 0.0, halo_ref[:half_rows, :].astype(f32)
        ).astype(bf16)
        halo_ref[half_rows:, :] = jnp.where(
            me == nodes - 1, 0.0, halo_ref[half_rows:, :].astype(f32)
        ).astype(bf16)

        def partial(b, t):
            columns = second_half if b else first_half
            value = dot(own[at(t), :], own_half(wp_ref, columns))
            value += dot(sib[at(t), :], sib_half(wp_ref, columns))
            for part in range(2):
                stage[2 * b + part, at(t), :] = value[:, part * LANE : (part + 1) * LANE].astype(
                    bf16
                )
            send_partial(b, t).start()

        def first_partial(t):
            send_own(t).wait_recv()
            partial(0, t)

        def compact_tile(t):
            for step in range(3):
                block = t * 3 + step
                pick = picked_rows(block)
                into = pl.ds(pl.multiple_of(block * SLOT, SLOT), SLOT)
                for q in range(quarter):
                    own[into, q * LANE : (q + 1) * LANE] = pick(q).astype(bf16)
            send_own(t).start()

            @pl.when(t == 1)
            def _():
                for number in range(2):
                    send_peer_weights(0, number).wait_recv()

            @pl.when(t >= 1)
            def _():
                first_partial(t - 1)

        def ready(g):
            return jnp.where(g == groups - 1, turns, jnp.minimum((team * (g + 1)) // 6, turns))

        def gather_group(g):
            @pl.when(g + 2 < groups)
            def _():
                loads(g + 2).start()

                @pl.when(g >= 1)
                def _():
                    tile_copy(g - 1).wait()

                count_group(g + 2)

            loads(g).wait()
            spot = g % 3
            for member in range(team):
                slot = g * team + member
                matrix = dot(unit, tbuf[spot, member], 1, 1).astype(bf16)
                value = dot(matrix[:, :SLOT], fbuf[spot, member * SLOT : (member + 1) * SLOT, :])
                value += dot(matrix[:, SLOT:], halo_ref[...])
                scale = column_of(inv_ref, slot)
                into = pl.ds(pl.multiple_of((slot + 1) * SLOT, SLOT), SLOT)
                for q in range(quarter):
                    big[q, into, :] = value[:, q * LANE : (q + 1) * LANE] * scale
            done = jnp.where(g == 0, 0, jnp.minimum((team * g) // 6, turns))
            loop(done, ready(g), compact_tile)

        loop(0, groups, gather_group)
        first_partial(turns - 1)
        for number in range(2):
            send_peer_weights(1, number).wait_recv()
        loop(0, turns, lambda t: partial(1, t))
        send_weights(0).start()
        send_weights(1).start()
        for half in range(2):
            for number in range(2):
                send_peer_weights(half, number).wait_send()
        for g in range(groups - 3, groups):
            tile_copy(g).wait()

        def exchange_block(number):
            copies = []
            for step in range(1, nodes):
                copy = remote(
                    sbuf.at[number],
                    ebuf.at[number, step],
                    e_s.at[number * nodes + step],
                    e_r.at[number * nodes + step],
                    node_id(step),
                )
                copy.start()
                copies.append(copy)
            ebuf[number, 0] = sbuf[number]
            for copy in copies:
                copy.wait()

        def row_of(number, line):
            return [ebuf[number, node, line : line + 1, :] for node in range(nodes)]

        def norm_block(b):
            columns = second_half if b else first_half
            st[...] = jnp.zeros_like(st)

            def linear_tile(t):
                send_partial(b, t).wait_recv()
                value = dot(own[at(t), :], own_half(wc_ref, columns))
                value += dot(sib[at(t), :], sib_half(wc_ref, columns))
                begin = t * tile
                before = jnp.minimum(begin, total)
                here = jnp.minimum(begin + tile, total) - before
                seen, new = before.astype(f32), here.astype(f32)
                for part in range(2):
                    lanes = slice(part * LANE, (part + 1) * LANE)
                    piece = value[:, lanes] + recv[2 * b + part, at(t), :].astype(f32)
                    big[part, at(t), :] = piece
                    both = jnp.full((1, LANE), jnp.maximum(seen + new, 1.0), f32)
                    live = lax.broadcasted_iota(i32, (tile, LANE), 0) < here
                    mean_here = jnp.sum(jnp.where(live, piece, 0.0), 0, keepdims=True) / jnp.full(
                        (1, LANE), jnp.maximum(new, 1.0), f32
                    )
                    centred = jnp.where(live, piece - mean_here, 0.0)
                    squares = jnp.sum(centred * centred, 0, keepdims=True)
                    mean, held = st[0:1, lanes], st[1:2, lanes]
                    gap = mean_here - mean
                    ratio = new / both
                    st[0:1, lanes] = mean + gap * ratio
                    st[1:2, lanes] = held + squares + gap * gap * (seen * ratio)

            loop(0, turns, linear_tile)
            if b == 1:
                pl.semaphore_signal(credit, inc=1, device_id=sib_id, device_id_type=MESH)
            st[2:3, :] = jnp.full((1, wide), total.astype(f32), f32)
            sbuf[2 * b] = st[...]

            def cot_copy(g):
                return pltpu.make_async_copy(
                    cot_hbm.at[
                        pl.ds(pl.multiple_of(g * team * SLOT, SLOT), team * SLOT),
                        pl.ds(b * wide, wide),
                    ],
                    cbuf.at[g % 2],
                    csem.at[g % 2],
                )

            def act_copy(g):
                return pltpu.make_async_copy(
                    abuf.at[g % 2],
                    act_hbm.at[
                        pl.ds(pl.multiple_of(g * team * SLOT, SLOT), team * SLOT),
                        pl.ds(b * wide, wide),
                    ],
                    asem.at[g % 2],
                )

            cot_copy(0).start()
            exchange_block(2 * b)
            numbers, means, squares = (row_of(2 * b, line) for line in (2, 0, 1))
            count = sum(numbers[1:], numbers[0])
            mean = sum([n * m for n, m in zip(numbers, means, strict=True)][1:], numbers[0] * means[0])
            mean = mean / count
            spread = jnp.zeros_like(mean)
            for n, m, s in zip(numbers, means, squares, strict=True):
                spread += s + n * (m - mean) * (m - mean)
            norm[0:1, :] = mean
            norm[1:2, :] = lax.rsqrt(spread / count + epsilon)
            sums[...] = jnp.zeros_like(sums)
            half_slot = SLOT // 2
            place_row = lax.broadcasted_iota(i32, (half_slot, LANE), 0)

            def act_group(g):
                @pl.when(g + 1 < groups)
                def _():
                    cot_copy(g + 1).start()

                cot_copy(g).wait()

                @pl.when(g >= 2)
                def _():
                    act_copy(g - 2).wait()

                spot = g % 2

                def one(member):
                    slot = g * team + member
                    for part in range(2):
                        lanes = slice(part * LANE, (part + 1) * LANE)
                        mean_here, rstd = norm[0:1, lanes], norm[1:2, lanes]
                        scale, shift = gain_ref[2 * b + part], bias_ref[2 * b + part]
                        for turn in range(2):
                            live = place_row < cnt_ref[slot] - turn * half_slot
                            here = pl.ds(
                                pl.multiple_of(member * SLOT + turn * half_slot, half_slot),
                                half_slot,
                            )
                            value = big[
                                part, pl.ds(off_ref[slot] + turn * half_slot, half_slot), :
                            ]
                            value = jnp.where(live, value, 0.0)
                            normed = (value - mean_here) * rstd
                            z = scale * normed + shift
                            square = z * z
                            bent = jnp.tanh(z * (slope + (slope * cubic) * square))
                            half = 0.5 + 0.5 * bent
                            abuf[spot, here, lanes] = jnp.where(live, z * half, 0.0)
                            back = half + z * (1.0 - bent * bent) * (
                                0.5 * slope + (1.5 * slope * cubic) * square
                            )
                            grad = jnp.where(live, cbuf[spot, here, lanes].astype(f32) * back, 0.0)
                            into = pl.ds(
                                pl.multiple_of((slot + 1) * SLOT + turn * half_slot, half_slot),
                                half_slot,
                            )
                            big[2 + part, into, :] = grad
                            tall = (half_slot // 8, 8, LANE)
                            sums[0, :, lanes] += jnp.sum((grad * normed).reshape(tall), 0)
                            sums[1, :, lanes] += jnp.sum(grad.reshape(tall), 0)

                loop(0, team, one)
                act_copy(g).start()

            loop(0, groups, act_group)
            sbuf[2 * b + 1] = jnp.zeros((8, wide), f32)
            sbuf[2 * b + 1, 0:1, :] = jnp.sum(sums[0], 0, keepdims=True)
            sbuf[2 * b + 1, 1:2, :] = jnp.sum(sums[1], 0, keepdims=True)
            exchange_block(2 * b + 1)
            by_gain, by_bias = (row_of(2 * b + 1, line) for line in (0, 1))
            by_gain = sum(by_gain[1:], by_gain[0])
            by_bias = sum(by_bias[1:], by_bias[0])
            fullest = numbers[0]
            for number in numbers[1:]:
                fullest = jnp.maximum(fullest, number)
            tot_ref[2:3, columns] = fullest
            tot_ref[0:1, columns] = by_gain
            tot_ref[1:2, columns] = by_bias
            norm[2:3, :] = by_gain / count
            norm[3:4, :] = by_bias / count
            act_copy(groups - 2).wait()
            act_copy(groups - 1).wait()

            def grad_tile(t):
                send_partial(b, t).wait_send()
                for step in range(3):
                    block = t * 3 + step
                    pick = picked_rows(block)
                    here = pl.ds(pl.multiple_of(block * SLOT, SLOT), SLOT)
                    live = lax.broadcasted_iota(i32, (SLOT, LANE), 0) < total - block * SLOT
                    for part in range(2):
                        lanes = slice(part * LANE, (part + 1) * LANE)
                        rstd = norm[1:2, lanes]
                        normed = (big[part, here, :] - norm[0:1, lanes]) * rstd
                        value = (rstd * gain_ref[2 * b + part]) * (
                            pick(2 + part) - norm[3:4, lanes] - normed * norm[2:3, lanes]
                        )
                        stage[2 * b + part, here, :] = jnp.where(live, value, 0.0).astype(bf16)
                send_grad(b, t).start()
                give_grad(b, t).start()

            loop(0, turns, grad_tile)
            if b == 1:
                loop(0, turns, lambda t: send_grad(2, t).start())

        def weight_part(source, qs, low, high, fresh):
            some = pl.ds(low * tile, (high - low) * tile)
            left = jnp.concatenate([source[q, some, :] for q in qs], 1)
            width = LANE * len(qs)
            for number, half in enumerate((own, sib)):
                into = slice(number * fw, (number + 1) * fw)
                value = dot(left, half[some, :], 0, 0)
                if fresh:
                    wacc[:width, into] = value
                else:
                    wacc[:width, into] += value

        def share_of(p, kind):
            return (stg_a, rs_a, ag_a, kind) if p == 0 else (stg_b, rs_b, ag_b, 2 * p - 2 + kind)

        def store_shares(p, kind, line):
            stg, _, _, k = share_of(p, kind)
            width = sizes[p] * LANE
            per = fw // LANE
            for number in range(2):
                base = (side if number == 0 else 1 - side) * per
                for step in range(per):
                    lanes = slice(number * fw + step * LANE, number * fw + (step + 1) * LANE)
                    stg[k, base + step] = wacc[line : line + width, lanes].astype(bf16)

        def scatter(p, kind):
            stg, rs, _, k = share_of(p, kind)
            index = (2 * p + kind) * nodes
            return [
                remote(
                    stg.at[k, (me + step) % nodes],
                    rs.at[k, step],
                    r_s.at[index + step],
                    r_r.at[index + step],
                    node_id(step),
                )
                for step in range(1, nodes)
            ]

        def begin(copies):
            for copy in copies:
                copy.start()

        def finish(copies):
            for copy in copies:
                copy.wait()

        def hop(p):
            src, dst = (hop_a, hop_a) if p == 0 else (hop_b, hop_b)
            k = 0 if p == 0 else 2 * p - 2
            return remote(src.at[k], dst.at[k + 1], h_s.at[p], h_r.at[p], peer_id)

        def spread_share(p, kind):
            if kind == 0:
                _, _, ag, k = share_of(p, 0)
                src = ag.at[k // 2]
            else:
                src = hop_a.at[1] if p == 0 else hop_b.at[2 * p - 1]
            index = (2 * p + kind) * nodes
            which = chip if kind == 0 else 1 - chip
            dst = wag_hbm.at[me, which, :, pl.ds(firsts[p] * LANE, sizes[p] * LANE)]
            copies = [
                remote(src, dst, a_s.at[index + step], a_r.at[index + step], node_id(step))
                for step in range(1, nodes)
            ]
            return copies, pltpu.make_async_copy(src, dst, lsem.at[2 * p + kind])

        def begin_spread(p, kind):
            copies, here = spread_share(p, kind)
            begin(copies)
            here.start()

        def finish_spread(p, kind):
            copies, here = spread_share(p, kind)
            finish(copies)
            here.wait()

        def sum_shares(p, kind):
            finish(scatter(p, kind))
            stg, rs, ag, k = share_of(p, kind)
            value = stg[k, me].astype(f32)
            for step in range(1, nodes):
                value += rs[k, step].astype(f32)
            value = jnp.transpose(value).astype(bf16)
            if kind == 0:
                ag[k // 2] = value
                begin_spread(p, 0)
            else:
                if p == 0:
                    hop_a[0] = value
                else:
                    hop_b[2 * p - 2] = value
                hop(p).start()

        def end_hop(p):
            hop(p).wait()
            begin_spread(p, 1)

        def product(p, t, fresh):
            qs = range(firsts[p], firsts[p] + sizes[p])
            columns = slice(firsts[p] * LANE, (firsts[p] + sizes[p]) * LANE)
            forward_grad(p, t).wait_recv()
            left = jnp.concatenate([ref[q, at(t), :] for ref in (stage, glp, gls, recv) for q in qs], 1)
            right = jnp.concatenate(
                [
                    own_half(wc_ref, columns),
                    own_half(wp_ref, columns),
                    ws_ref[:fw, columns],
                    ws_ref[fw:, columns],
                ],
                1,
            )
            value = dot(left, right, 1, 1)
            for q in range(quarter):
                piece = value[:, q * LANE : (q + 1) * LANE]
                if fresh:
                    big[q, at(t), :] = piece
                else:
                    big[q, at(t), :] += piece

        norm_block(0)
        send_weights(0).wait()
        send_weights(1).wait()
        for low, high in ranges:
            weight_part(stage, (0, 1), low, high, low == 0)
        store_shares(0, 0, 0)
        begin(scatter(0, 0))
        norm_block(1)
        for low, high in ranges:
            weight_part(stage, (2, 3), low, high, low == 0)
        store_shares(1, 0, 0)
        store_shares(2, 0, LANE)
        begin(scatter(1, 0))
        begin(scatter(2, 0))
        sum_shares(0, 0)
        pl.semaphore_wait(credit, 1)

        def pass_on(p, t):
            send_grad(p, t).wait_recv()
            forward_grad(p, t).start()

        for low, high in ranges:
            loop(low, high, lambda t: pass_on(0, t))
            weight_part(glp, (0, 1), low, high, low == 0)
        store_shares(0, 1, 0)
        begin(scatter(0, 1))

        def first_product(t):
            give_grad(0, t).wait_recv()
            give_grad(1, t).wait_recv()
            product(0, t, True)

        loop(0, turns, first_product)
        sum_shares(1, 0)
        sum_shares(2, 0)
        sum_shares(0, 1)
        for low, high in ranges:
            loop(low, high, lambda t: pass_on(1, t))
            weight_part(glp, (2,), low, high, low == 0)
        store_shares(1, 1, 0)
        begin(scatter(1, 1))
        loop(0, turns, lambda t: product(1, t, False))
        end_hop(0)
        sum_shares(1, 1)

        def last_turn(t):
            pass_on(2, t)

            @pl.when(t >= 2)
            def _():
                product(2, t - 2, False)

        for low, high in ranges:
            loop(low, high, last_turn)
            weight_part(glp, (3,), low, high, low == 0)
        store_shares(2, 1, 0)
        begin(scatter(2, 1))
        for t in (turns - 2, turns - 1):
            product(2, t, False)
        end_hop(1)

        def link_copy(g):
            return pltpu.make_async_copy(
                tile_hbm.at[pl.ds(g * team, team), pl.ds(SLOT, 2 * SLOT)],
                tbuf.at[g % 3, :, pl.ds(SLOT, 2 * SLOT)],
                tsem.at[g % 3],
            )

        def slot_copy(g):
            return pltpu.make_async_copy(
                gbuf.at[g % 2],
                slot_hbm.at[pl.ds(pl.multiple_of(g * team * SLOT, SLOT), team * SLOT)],
                gsem.at[g % 2],
            )

        link_copy(0).start()
        link_copy(1).start()
        link_total[...] = jnp.zeros_like(link_total)
        place_row = lax.broadcasted_iota(i32, (SLOT, LANE), 0)

        def slot_group(g):
            @pl.when(g + 2 < groups)
            def _():
                link_copy(g + 2).start()

            link_copy(g).wait()

            @pl.when(g >= 2)
            def _():
                slot_copy(g - 2).wait()

            for member in range(team):
                slot = g * team + member
                live = place_row < cnt_ref[slot]
                scale = column_of(inv_ref, slot)
                for q in range(quarter):
                    value = big[q, pl.ds(off_ref[slot], SLOT), :].astype(bf16).astype(f32)
                    gbuf[g % 2, member * SLOT : (member + 1) * SLOT, q * LANE : (q + 1) * LANE] = (
                        jnp.where(live, value * scale, 0.0).astype(bf16)
                    )
            link = jnp.concatenate([tbuf[g % 3, member, SLOT:, :] for member in range(team)], 1)
            link_total[...] += dot(link, gbuf[g % 2])
            slot_copy(g).start()

        loop(0, groups, slot_group)
        hbuf[...] = link_total[...].astype(bf16)
        half = hbuf.shape[0] // 2
        returns = [
            remote(hbuf.at[:half], hback.at[:half], b_s.at[0], b_r.at[0], node_id(nodes - 1)),
            remote(hbuf.at[half:], hback.at[half:], b_s.at[1], b_r.at[1], node_id(1)),
        ]
        begin(returns)
        sum_shares(2, 1)
        slot_copy(groups - 2).wait()
        slot_copy(groups - 1).wait()
        finish(returns)
        back_ref[:half, :] = jnp.where(me == nodes - 1, 0.0, hback[:half, :].astype(f32)).astype(bf16)
        back_ref[half:, :] = jnp.where(me == 0, 0.0, hback[half:, :].astype(f32)).astype(bf16)
        end_hop(2)

        def settle(t):
            send_own(t).wait_send()
            for b in range(2):
                give_grad(b, t).wait_send()
            for p in range(3):
                send_grad(p, t).wait_send()
                forward_grad(p, t).wait_send()

        loop(0, turns, settle)
        for p in range(3):
            for kind in range(2):
                finish_spread(p, kind)

    anywhere = pl.BlockSpec(memory_space=pl.ANY)
    dma = pltpu.SemaphoreType.DMA
    lane_rows = (quarter, compact, LANE)
    outs = [
        jax.ShapeDtypeStruct((rows, fw), f32),
        jax.ShapeDtypeStruct((rows, fw), bf16),
        jax.ShapeDtypeStruct((2 * SLOT, fw), bf16),
        jax.ShapeDtypeStruct((nodes, 2, LANE, fw), bf16),
        jax.ShapeDtypeStruct((8, fw), f32),
        jax.ShapeDtypeStruct((slots, 3 * SLOT, SLOT), bf16),
    ]
    scratch = [
        pltpu.VMEM((compact, fw), bf16),
        pltpu.VMEM((compact, fw), bf16),
        pltpu.VMEM(lane_rows, bf16),
        pltpu.VMEM(lane_rows, bf16),
        pltpu.VMEM(lane_rows, bf16),
        pltpu.VMEM(lane_rows, bf16),
        pltpu.VMEM((quarter, padded, LANE), f32),
        pltpu.VMEM((wide, 2 * fw), f32),
        pltpu.VMEM((2, nodes, wide, LANE), bf16),
        pltpu.VMEM((4, nodes, LANE, LANE), bf16),
        pltpu.VMEM((2, nodes, wide, LANE), bf16),
        pltpu.VMEM((4, nodes, LANE, LANE), bf16),
        pltpu.VMEM((1, LANE, wide), bf16),
        pltpu.VMEM((2, LANE, LANE), bf16),
        pltpu.VMEM((2, LANE, wide), bf16),
        pltpu.VMEM((4, LANE, LANE), bf16),
        pltpu.VMEM((3, team * SLOT, fw), bf16),
        pltpu.VMEM((3, team, 3 * SLOT, SLOT), bf16),
        pltpu.VMEM((2, team * SLOT, wide), bf16),
        pltpu.VMEM((2, team * SLOT, wide), f32),
        pltpu.VMEM((2, team * SLOT, fw), bf16),
        pltpu.VMEM((4, 8, wide), f32),
        pltpu.VMEM((4, nodes, 8, wide), f32),
        pltpu.VMEM((8, wide), f32),
        pltpu.VMEM((2, 8, wide), f32),
        pltpu.VMEM((8, wide), f32),
        pltpu.VMEM((2 * SLOT, fw), f32),
        pltpu.VMEM((2 * SLOT, fw), bf16),
        pltpu.VMEM((2 * SLOT, fw), bf16),
        dma((3,)),
        dma((3,)),
        dma((2,)),
        dma((2,)),
        dma((2,)),
        dma((turns,)),
        dma((turns,)),
        dma((2 * turns,)),
        dma((2 * turns,)),
        dma((3 * turns,)),
        dma((3 * turns,)),
        dma((2 * turns,)),
        dma((2 * turns,)),
        dma((3 * turns,)),
        dma((3 * turns,)),
        dma((4 * nodes,)),
        dma((4 * nodes,)),
        dma((6 * nodes,)),
        dma((6 * nodes,)),
        dma((3,)),
        dma((3,)),
        dma((6 * nodes,)),
        dma((6 * nodes,)),
        dma((4,)),
        dma((4,)),
        dma((6,)),
        pltpu.SemaphoreType.REGULAR,
        pltpu.VMEM((2 * fw, fw), bf16),
        dma((2,)),
        dma((2,)),
        pltpu.VMEM((2 * fw, fw), bf16),
        pltpu.VMEM((2 * fw, fw), bf16),
        dma((2 * quarter,)),
        dma((4,)),
        dma((4,)),
        pltpu.VMEM((2 * SLOT, fw), bf16),
        pltpu.VMEM((slots, 8, SLOT), f32),
    ]
    return pl.pallas_call(
        kernel,
        out_shape=outs,
        in_specs=[smem()] * 3 + [anywhere] * 3 + [whole()] * 5,
        out_specs=[anywhere, anywhere, whole(), anywhere, whole(), anywhere],
        scratch_shapes=scratch,
        compiler_params=pltpu.CompilerParams(
            vmem_limit_bytes=CORE_BYTES, collective_id=2, has_side_effects=True
        ),
        cost_estimate=cost(0, 0),
        name="core",
    )(*lists, features, weight, cotangent, near, links, send_row, gain, bias)


def every_row(
    features, weight, cotangent, near, links, send_list, valid_row, scale, shift, lists, nodes, chips
):
    offsets, counts = lists[:2]
    rows, fw = features.shape
    slots = rows // SLOT
    chip, core_side = lax.axis_index("mp") // 2, lax.rem(lax.axis_index("mp"), 2)
    core_word = core_side.astype(i32)[None]
    half = send_list.shape[0] // 2
    others = range(1, chips)
    wide = fw // 2

    def chip_rows(which):
        return lax.dynamic_slice_in_dim(weight, which * 2 * fw, 2 * fw, 0).astype(bf16)

    w_peer = [to_chip(chip_rows(lax.rem(chip + d, chips)), d) for d in others]
    w_chip = chip_rows(chip)
    picked = pick_rows(features, send_list[:, None], valid_row)
    halo = jnp.concatenate([node_shift(picked[:half], 1), node_shift(picked[half:], -1)], 0)
    tiles, inv = count_tiles(near, links, counts)

    def half_of(block, which):
        return lax.dynamic_slice_in_dim(block, which * fw, fw, 0)

    w_all = [w_chip] + w_peer
    got = to_sibling(jnp.concatenate([half_of(w, 1 - core_side) for w in w_all], 0))
    wb = [half_of(w, core_side) for w in w_all] + [got[i * fw : (i + 1) * fw] for i in range(chips)]
    own = aggregate(tiles, inv, features, halo, offsets, counts, 0, rows)
    sib = to_sibling(own)
    received = []
    for b in range(2):
        parts = [partial_product(own, sib, w, core_word, b, wide) for w in w_peer]
        received.append([to_chip(p, -d) for p, d in zip(parts, others, strict=True)])
    gain, bias = scale[None, :], shift[None, :]
    act, grads, totals, weight_grads = None, [], [], []
    for b in range(2):
        lin, stat = linear_stats(
            own, sib, w_chip, core_word, received[b], offsets, slots, b, wide
        )
        stats = exchange(stat, nodes)
        act, grad_pre, sums = activate(
            lin, stats, gain, bias, cotangent, offsets, counts, act, b, wide, rows, fw
        )
        sums = exchange(sums, nodes)
        grad_lin, summed = linear_grad(
            lin, grad_pre, stats, sums, gain, offsets, slots, b, wide, 1
        )
        totals.append(summed)
        mine = [grad_lin] + [to_chip(grad_lin, d) for d in others]
        grads.append(mine + [to_sibling(g) for g in mine])
        sets = []
        for g in mine:
            left = jnp.einsum("rf,rc->fc", own, g, preferred_element_type=f32)
            right = jnp.einsum("rf,rc->fc", sib, g, preferred_element_type=f32)
            sets.append(
                jnp.concatenate(
                    [
                        jnp.where(core_side == 1, right, left),
                        jnp.where(core_side == 1, left, right),
                    ],
                    0,
                )
            )
        share = scatter_sum(jnp.stack(sets), 1)
        shares = [share[0]] + [to_chip(share[d], -d) for d in others]
        full = gather_shares(jnp.stack(shares), 1)
        placed = jnp.zeros((chips,) + full.shape[1:], f32)
        for d in range(chips):
            placed = lax.dynamic_update_slice(
                placed, full[d : d + 1], (lax.rem(chip + d, chips), 0, 0)
            )
        weight_grads.append(placed.reshape(chips * 2 * fw, wide))
    grad_agg = grad_products(grads[0], wb, [0] * len(wb))
    slot_grad, halo_grad = slot_grads(grad_agg, grads[1], wb, wide, tiles, inv, offsets, counts)
    returned = jnp.concatenate(
        [node_shift(halo_grad[:half], -1), node_shift(halo_grad[half:], 1)], 0
    )
    input_grad = input_grads(slot_grad, tiles, returned, send_list[None, :], counts)
    totals = jnp.concatenate(totals, 1)
    return act, input_grad, jnp.concatenate(weight_grads, 1), totals[0], totals[1]


def local(features, weight, scale, shift, cotangent, neighbours, halo_links, valid_rows, send_rows):
    rows, fw = features.shape
    slots = rows // SLOT
    nodes, mp = lax.axis_size("node"), lax.axis_size("mp")
    chips = mp // 2

    counts = jnp.sum(valid_rows.reshape(slots, SLOT), 1).astype(i32)
    order = jnp.arange(slots + 1, dtype=i32)
    offsets = jnp.sum(jnp.where(order[None, :slots] < order[:, None], counts[None, :], 0), 1)
    compact = rows * 13 // 16 // (3 * SLOT) * (3 * SLOT)
    blocks = jnp.arange(compact // SLOT, dtype=i32) * SLOT
    first = jnp.minimum(
        jnp.sum((offsets[None, 1:] <= blocks[:, None]).astype(i32), 1), slots - 1
    ).astype(i32)
    lists = (offsets, counts, first)
    near, links = neighbours.T, halo_links.T
    send_list = jnp.concatenate([send_rows[:, 1], send_rows[:, 0]], 0)
    valid_row = valid_rows[None, :].astype(i32)

    def all_rows(*args):
        return every_row(*args, lists, nodes, chips)

    given = (features, weight, cotangent, near, links, send_list, valid_row, scale, shift)
    if not (chips == 2 and fw == 4 * LANE and 2 * fw == nodes * LANE and slots % nodes == 0):
        return all_rows(*given)
    send_row = send_list[None, :]
    *made, totals, tiles = core(
        features, weight, cotangent, near, links, send_row, scale, shift, lists, nodes, compact
    )

    def few_rows(*args):
        act, input_grad, weight_grad = last_pass(*made, tiles, send_row, counts)
        return act, input_grad, weight_grad.reshape(mp * fw, fw), totals[0], totals[1]

    return lax.cond(totals[2, 0] <= compact, few_rows, all_rows, *given)


def solution(mesh):
    in_specs = (
        P("node", "mp"),
        P(None, "mp"),
        P("mp"),
        P("mp"),
        P("node", "mp"),
        P("node", None),
        P("node", None),
        P("node"),
        P("node", None),
    )
    out_specs = (P("node", "mp"), P("node", "mp"), P(None, "mp"), P("mp"), P("mp"))
    return jax.shard_map(local, mesh=mesh, in_specs=in_specs, out_specs=out_specs, check_vma=False)
```

```python
import functools

import jax
import jax.numpy as jnp
from jax import lax
from jax.experimental import pallas as pl
from jax.experimental.pallas import tpu as pltpu
from jax.sharding import PartitionSpec as P

SLOT = 128
LANE = 128
GROUP = 12
epsilon = 1e-05
VMEM_BYTES = 56 * 1024 * 1024
CORE_BYTES = 61 * 1024 * 1024
MESH = pl.DeviceIdType.MESH
f32, bf16, i32 = jnp.float32, jnp.bfloat16, jnp.int32


def params(**extra):
    return pltpu.CompilerParams(vmem_limit_bytes=VMEM_BYTES, **extra)


def whole():
    return pl.BlockSpec(memory_space=pltpu.VMEM)


def smem():
    return pl.BlockSpec(memory_space=pltpu.SMEM)


def fixed(shape):
    return pl.BlockSpec(shape, lambda i: (0,) * len(shape), pipeline_mode=pl.Buffered(1))


def cost(flops, moved, trans=0):
    return pl.CostEstimate(flops=1, bytes_accessed=1, transcendentals=0)


def dot(a, b, ca=1, cb=0):
    return lax.dot_general(a, b, (((ca,), (cb,)), ((), ())), preferred_element_type=f32)


def after(value, *earlier):
    return lax.optimization_barrier((value,) + earlier)[0]


def chosen(rows_ref, base, count, valid):
    width = rows_ref.shape[1]
    place = lax.broadcasted_iota(i32, (count, width), 0)
    hit = (rows_ref[...] == place + base) & (place < valid)
    return jnp.where(hit, 1.0, 0.0).astype(bf16)


def pick_rows(features, send_column, valid_row):
    rows, width = features.shape
    sends = send_column.shape[0]
    steps = 3
    tile = rows // steps

    def kernel(feat_ref, send_ref, valid_ref, out_ref, total):
        step = pl.program_id(0)

        @pl.when(step == 0)
        def _():
            total[...] = jnp.zeros_like(total)

        wanted = jnp.broadcast_to(send_ref[...], (sends, LANE)) - step * tile
        place = lax.broadcasted_iota(i32, (sends, LANE), 1)
        hot = []
        for part in range(tile // LANE):
            lanes = slice(part * LANE, (part + 1) * LANE)
            hit = (wanted == place + part * LANE) & (valid_ref[:, lanes] > 0)
            hot.append(jnp.where(hit, 1.0, 0.0).astype(bf16))
        total[...] += dot(jnp.concatenate(hot, 1), feat_ref[...])

        @pl.when(step == steps - 1)
        def _():
            out_ref[...] = total[...].astype(bf16)

    return pl.pallas_call(
        kernel,
        grid=(steps,),
        out_shape=jax.ShapeDtypeStruct((sends, width), bf16),
        in_specs=[
            pl.BlockSpec((tile, width), lambda i: (i, 0)),
            fixed((sends, 1)),
            pl.BlockSpec((1, tile), lambda i: (0, i)),
        ],
        out_specs=fixed((sends, width)),
        scratch_shapes=[pltpu.VMEM((sends, width), f32)],
        compiler_params=params(),
        cost_estimate=cost(2 * rows * sends * width, 2 * rows * width),
        name="pick_rows",
    )(features, send_column, valid_row)


def count_tiles(near, links, counts):
    entries, rows = near.shape
    link_entries = links.shape[0]
    slots = rows // SLOT

    def kernel(counts_ref, near_ref, link_ref, tile_ref, inv_ref):
        step = pl.program_id(0)
        row = lax.broadcasted_iota(i32, (SLOT, SLOT), 0)
        column = lax.broadcasted_iota(i32, (SLOT, SLOT), 1)
        link_row = lax.broadcasted_iota(i32, (2 * SLOT, SLOT), 0)

        def one(part, carry):
            lanes = pl.ds(pl.multiple_of(part * SLOT, SLOT), SLOT)
            near_here, link_here = near_ref[:, lanes], link_ref[:, lanes]
            counted = jnp.zeros((SLOT, SLOT), f32)
            for entry in range(entries):
                counted += jnp.where(near_here[entry : entry + 1] == row, 1.0, 0.0)
            linked = jnp.zeros((2 * SLOT, SLOT), f32)
            for entry in range(link_entries):
                linked += jnp.where(link_here[entry : entry + 1] == link_row, 1.0, 0.0)
            degree = 1.0 + jnp.sum(counted, 0, keepdims=True) + jnp.sum(linked, 0, keepdims=True)
            tile = counted + jnp.where(row == column, counted + 2.0, 0.0)
            tile = jnp.where(row < counts_ref[step * GROUP + part], tile, 0.0)
            tile_ref[part, :SLOT, :] = tile.astype(bf16)
            tile_ref[part, SLOT:, :] = linked.astype(bf16)
            inv_ref[part] = jnp.broadcast_to(1.0 / degree, (8, SLOT))
            return carry

        lax.fori_loop(0, GROUP, one, 0)

    return pl.pallas_call(
        kernel,
        grid=(slots // GROUP,),
        out_shape=[
            jax.ShapeDtypeStruct((slots, 3 * SLOT, SLOT), bf16),
            jax.ShapeDtypeStruct((slots, 8, SLOT), f32),
        ],
        in_specs=[
            smem(),
            pl.BlockSpec((entries, GROUP * SLOT), lambda i: (0, i)),
            pl.BlockSpec((link_entries, GROUP * SLOT), lambda i: (0, i)),
        ],
        out_specs=[
            pl.BlockSpec((GROUP, 3 * SLOT, SLOT), lambda i: (i, 0, 0)),
            pl.BlockSpec((GROUP, 8, SLOT), lambda i: (i, 0, 0)),
        ],
        compiler_params=params(),
        cost_estimate=cost(rows * 12000, 6 * rows * SLOT),
        name="count_tiles",
    )(counts, near, links)


def column_of(inv_ref, slot):
    return jnp.transpose(jnp.broadcast_to(inv_ref[slot, 0:1, :], (SLOT, SLOT)))


def aggregate(tiles, inv, features, halo, offsets, counts, first, rows):
    slots = tiles.shape[0]
    width = features.shape[1]
    quarter = width // LANE
    team = 4
    low = first // SLOT // team * team
    high = min(slots, -(-(first + rows) // (SLOT // 2)))
    groups = -(-(high - low) // team)
    low = min(low, slots - groups * team)
    sub = rows // 4

    def kernel(off_ref, counts_ref, tile_hbm, inv_hbm, feat_hbm, halo_ref, out_ref, *scratch):
        held, tile_ref, inv_ref, feat_ref, sems = scratch

        def copies(group):
            here = group * team
            return [
                pltpu.make_async_copy(
                    tile_hbm.at[pl.ds(low + here, team)],
                    tile_ref.at[pl.ds(here, team)],
                    sems.at[0, group],
                ),
                pltpu.make_async_copy(
                    inv_hbm.at[pl.ds(low + here, team)],
                    inv_ref.at[pl.ds(here, team)],
                    sems.at[1, group],
                ),
                pltpu.make_async_copy(
                    feat_hbm.at[pl.ds(pl.multiple_of((low + here) * SLOT, SLOT), team * SLOT)],
                    feat_ref.at[pl.ds(pl.multiple_of(here * SLOT, SLOT), team * SLOT)],
                    sems.at[2, group],
                ),
            ]

        def begin(group, carry):
            for copy in copies(group):
                copy.start()
            return carry

        lax.fori_loop(0, groups, begin, 0)
        row = lax.broadcasted_iota(i32, (SLOT, SLOT), 0)
        column = lax.broadcasted_iota(i32, (SLOT, SLOT), 1)
        unit = jnp.where(row == column, 1.0, 0.0).astype(bf16)

        def step(group, carry):
            for copy in copies(group):
                copy.wait()

            @pl.when(off_ref[low + group * team] < first + rows)
            def _():
                for member in range(team):
                    here = group * team + member
                    tile = dot(unit, tile_ref[here], 1, 1).astype(bf16)
                    source = pl.ds(pl.multiple_of(here * SLOT, SLOT), SLOT)
                    total = dot(tile[:, :SLOT], feat_ref[source, :])
                    total += dot(tile[:, SLOT:], halo_ref[...])
                    scale = column_of(inv_ref, here)
                    start = jnp.clip(off_ref[low + here] - first + SLOT, 0, rows + SLOT)
                    for q in range(quarter):
                        held[q, pl.ds(start, SLOT), :] = (
                            total[:, q * LANE : (q + 1) * LANE] * scale
                        )

            return carry

        lax.fori_loop(0, groups, step, 0)
        total_rows = off_ref[slots] - first

        def finish(part, carry):
            begin_row = pl.multiple_of(part * sub, 16)
            live = lax.broadcasted_iota(i32, (sub, LANE), 0) + begin_row < total_rows
            for q in range(quarter):
                out_ref[pl.ds(begin_row, sub), q * LANE : (q + 1) * LANE] = jnp.where(
                    live, held[q, pl.ds(begin_row + SLOT, sub), :], 0.0
                ).astype(bf16)
            return carry

        lax.fori_loop(0, rows // sub, finish, 0)

    anywhere = pl.BlockSpec(memory_space=pl.ANY)
    return pl.pallas_call(
        kernel,
        out_shape=jax.ShapeDtypeStruct((rows, width), bf16),
        in_specs=[smem(), smem(), anywhere, anywhere, anywhere, whole()],
        out_specs=whole(),
        scratch_shapes=[
            pltpu.VMEM((quarter, rows + 2 * SLOT, LANE), f32),
            pltpu.VMEM((groups * team, 3 * SLOT, SLOT), bf16),
            pltpu.VMEM((groups * team, 8, SLOT), f32),
            pltpu.VMEM((groups * team * SLOT, width), bf16),
            pltpu.SemaphoreType.DMA((3, groups)),
        ],
        compiler_params=params(),
        cost_estimate=cost(2 * rows * 3 * SLOT * width, 4 * rows * width),
        name="aggregate",
    )(offsets, counts, tiles, inv, features, halo)


def partial_product(own, sib, weight, core, block, width):
    rows, depth = own.shape
    tile = rows // 2 if rows > 1600 else rows

    def kernel(core_ref, a_ref, b_ref, w_ref, out_ref):
        core = core_ref[0]
        first = w_ref[pl.ds(pl.multiple_of(core * depth, depth), depth), :]
        second = w_ref[pl.ds(pl.multiple_of((1 - core) * depth, depth), depth), :]
        out_ref[...] = (dot(a_ref[...], first) + dot(b_ref[...], second)).astype(bf16)

    return pl.pallas_call(
        kernel,
        grid=(rows // tile,),
        out_shape=jax.ShapeDtypeStruct((rows, width), bf16),
        in_specs=[smem()]
        + [pl.BlockSpec((tile, depth), lambda i: (i, 0))] * 2
        + [pl.BlockSpec((2 * depth, width), lambda i: (0, block))],
        out_specs=pl.BlockSpec((tile, width), lambda i: (i, 0)),
        compiler_params=params(),
        cost_estimate=cost(4 * rows * depth * width, 4 * rows * depth + 2 * rows * width),
        name="partial_product",
    )(core, own, sib, weight)


def linear_stats(own, sib, weight, core, received, offsets, slots, block, width):
    rows, depth = own.shape
    tile = rows // 2
    sub = rows // 8
    parts = width // LANE
    others = len(received)

    def kernel(off_ref, core_ref, a_ref, b_ref, w_ref, *rest):
        recv_refs, (lin_ref, stat_ref) = rest[:others], rest[others:]
        step = pl.program_id(0)
        core = core_ref[0]
        first = w_ref[pl.ds(pl.multiple_of(core * depth, depth), depth), :]
        second = w_ref[pl.ds(pl.multiple_of((1 - core) * depth, depth), depth), :]
        total = off_ref[slots]

        @pl.when(step == 0)
        def _():
            stat_ref[...] = jnp.zeros_like(stat_ref)
            stat_ref[2:3, :] = jnp.full((1, width), total.astype(f32), f32)

        for piece in range(tile // sub):
            here_rows = slice(piece * sub, (piece + 1) * sub)
            value = dot(a_ref[here_rows, :], first) + dot(b_ref[here_rows, :], second)
            for ref in recv_refs:
                value += ref[here_rows, :].astype(f32)
            for part in range(parts):
                lin_ref[part, here_rows, :] = value[:, part * LANE : (part + 1) * LANE]
            begin = step * tile + piece * sub
            before = jnp.minimum(begin, total)
            here = jnp.minimum(begin + sub, total) - before
            seen, new = before.astype(f32), here.astype(f32)
            both = jnp.full((1, width), jnp.maximum(seen + new, 1.0), f32)
            live = lax.broadcasted_iota(i32, (sub, width), 0) < here
            mean_here = jnp.sum(jnp.where(live, value, 0.0), 0, keepdims=True) / jnp.full(
                (1, width), jnp.maximum(new, 1.0), f32
            )
            centred = jnp.where(live, value - mean_here, 0.0)
            squares = jnp.sum(centred * centred, 0, keepdims=True)
            mean, held = stat_ref[0:1, :], stat_ref[1:2, :]
            gap = mean_here - mean
            ratio = new / both
            stat_ref[0:1, :] = mean + gap * ratio
            stat_ref[1:2, :] = held + squares + gap * gap * (seen * ratio)

    return pl.pallas_call(
        kernel,
        grid=(rows // tile,),
        out_shape=[
            jax.ShapeDtypeStruct((parts, rows + SLOT, LANE), f32),
            jax.ShapeDtypeStruct((8, width), f32),
        ],
        in_specs=[smem(), smem()]
        + [pl.BlockSpec((tile, depth), lambda i: (i, 0))] * 2
        + [pl.BlockSpec((2 * depth, width), lambda i: (0, block))]
        + [pl.BlockSpec((tile, width), lambda i: (i, 0))] * others,
        out_specs=[
            pl.BlockSpec((parts, tile, LANE), lambda i: (0, i, 0)),
            pl.BlockSpec((8, width), lambda i: (0, 0)),
        ],
        compiler_params=params(),
        cost_estimate=cost(4 * rows * depth * width, 4 * rows * depth + 6 * rows * width),
        name="linear_stats",
    )(offsets, core, own, sib, weight, *received)


def exchange(block, nodes, number=1):
    def kernel(in_ref, out_ref, held, send_sem, recv_sem):
        me = lax.axis_index("node")
        barrier = pltpu.get_barrier_semaphore()
        for step in range(1, nodes):
            pl.semaphore_signal(
                barrier,
                inc=1,
                device_id={"node": lax.rem(me + step, nodes)},
                device_id_type=MESH,
            )
        pl.semaphore_wait(barrier, nodes - 1)
        copies = []
        for step in range(1, nodes):
            copy = pltpu.make_async_remote_copy(
                src_ref=in_ref,
                dst_ref=held.at[step],
                send_sem=send_sem.at[step],
                recv_sem=recv_sem.at[step],
                device_id={"node": lax.rem(me + step, nodes)},
                device_id_type=MESH,
            )
            copy.start()
            copies.append(copy)
        out_ref[0] = in_ref[...]
        for copy in copies:
            copy.wait()
        for step in range(1, nodes):
            out_ref[step] = held[step]

    return pl.pallas_call(
        kernel,
        out_shape=jax.ShapeDtypeStruct((nodes,) + block.shape, f32),
        in_specs=[whole()],
        out_specs=whole(),
        scratch_shapes=[
            pltpu.VMEM((nodes,) + block.shape, f32),
            pltpu.SemaphoreType.DMA((nodes,)),
            pltpu.SemaphoreType.DMA((nodes,)),
        ],
        compiler_params=params(collective_id=number, has_side_effects=True),
        cost_estimate=cost(0, nodes * block.size * 4),
        name="exchange",
    )(block)


def merge_stats(stat_ref, width):
    nodes = stat_ref.shape[0]
    total = stat_ref[0, 2:3, :width]
    for node in range(1, nodes):
        total += stat_ref[node, 2:3, :width]
    mean = stat_ref[0, 2:3, :width] * stat_ref[0, 0:1, :width]
    for node in range(1, nodes):
        mean += stat_ref[node, 2:3, :width] * stat_ref[node, 0:1, :width]
    mean = mean / total
    spread = jnp.zeros_like(mean)
    for node in range(nodes):
        gap = stat_ref[node, 0:1, :width] - mean
        spread += stat_ref[node, 1:2, :width] + stat_ref[node, 2:3, :width] * gap * gap
    return total, mean, lax.rsqrt(spread / total + epsilon)


def activate(
    linear, stats, scale, shift, cotangent, offsets, counts, held, block, width, rows, feat_width
):
    nodes = stats.shape[0]
    slots = rows // SLOT
    parts = width // LANE
    compact = linear.shape[1]
    slope = 0.7978845608028654
    cubic = 0.044715
    half_slot = SLOT // 2

    def kernel(off_ref, counts_ref, lin_ref, stat_ref, scale_ref, shift_ref, cot_ref, *rest):
        act_ref, grad_ref, sum_ref, norm, sums = rest[-5:]
        step = pl.program_id(0)

        @pl.when(step == 0)
        def _():
            _, mean, rstd = merge_stats(stat_ref, width)
            norm[0:1, :] = mean
            norm[1:2, :] = rstd
            sums[...] = jnp.zeros_like(sums)

        place = lax.broadcasted_iota(i32, (half_slot, LANE), 0)

        def one(member, carry):
            slot = step * GROUP + member
            start = off_ref[slot]
            for side in range(2):
                live = place < counts_ref[slot] - side * half_slot
                here = pl.ds(pl.multiple_of(member * SLOT + side * half_slot, 16), half_slot)
                from_row = pl.ds(start + side * half_slot, half_slot)
                for part in range(parts):
                    lanes = slice(part * LANE, (part + 1) * LANE)
                    mean, rstd = norm[0:1, lanes], norm[1:2, lanes]
                    value = jnp.where(live, lin_ref[part, from_row, :], 0.0)
                    normed = (value - mean) * rstd
                    z = scale_ref[:, lanes] * normed + shift_ref[:, lanes]
                    square = z * z
                    bent = jnp.tanh(z * (slope + (slope * cubic) * square))
                    half = 0.5 + 0.5 * bent
                    act_ref[here, lanes] = jnp.where(live, z * half, 0.0)
                    back = half + z * (1.0 - bent * bent) * (
                        0.5 * slope + (1.5 * slope * cubic) * square
                    )
                    grad = jnp.where(live, cot_ref[here, lanes].astype(f32) * back, 0.0)
                    grad_ref[part, from_row, :] = grad
                    tall = (half_slot // 8, 8, LANE)
                    sums[0, :, lanes] += jnp.sum((grad * normed).reshape(tall), 0)
                    sums[1, :, lanes] += jnp.sum(grad.reshape(tall), 0)
            return carry

        lax.fori_loop(0, GROUP, one, 0)

        @pl.when(step == slots // GROUP - 1)
        def _():
            sum_ref[...] = jnp.zeros_like(sum_ref)
            sum_ref[0:1, :] = jnp.sum(sums[0], 0, keepdims=True)
            sum_ref[1:2, :] = jnp.sum(sums[1], 0, keepdims=True)

    given = [] if held is None else [held]
    return pl.pallas_call(
        kernel,
        grid=(slots // GROUP,),
        out_shape=[
            jax.ShapeDtypeStruct((rows, feat_width), f32),
            jax.ShapeDtypeStruct((parts, compact, LANE), f32),
            jax.ShapeDtypeStruct((8, width), f32),
        ],
        in_specs=[
            smem(),
            smem(),
            fixed((parts, compact, LANE)),
            fixed(stats.shape),
            pl.BlockSpec((1, width), lambda i: (0, block)),
            pl.BlockSpec((1, width), lambda i: (0, block)),
            pl.BlockSpec((GROUP * SLOT, width), lambda i: (i, block)),
        ]
        + [pl.BlockSpec(memory_space=pl.ANY)] * len(given),
        out_specs=[
            pl.BlockSpec((GROUP * SLOT, width), lambda i: (i, block)),
            fixed((parts, compact, LANE)),
            fixed((8, width)),
        ],
        scratch_shapes=[pltpu.VMEM((8, width), f32), pltpu.VMEM((2, 8, width), f32)],
        input_output_aliases={7: 0} if given else {},
        compiler_params=params(),
        cost_estimate=cost(60 * rows * width, 14 * rows * width, rows * width),
        name="activate",
    )(offsets, counts, linear, stats, scale, shift, cotangent, *given)


def linear_grad(linear, grad, stats, sums, scale, offsets, slots, block, width, pieces):
    parts, padded, _ = linear.shape
    rows = padded - SLOT
    tile = rows // 2
    sub = rows // 16
    nodes = stats.shape[0]
    share = width // pieces

    def kernel(off_ref, lin_ref, grad_ref, stat_ref, sums_ref, scale_ref, *rest):
        out_refs, (total_ref, norm) = rest[:pieces], rest[pieces:]
        step = pl.program_id(0)

        @pl.when(step == 0)
        def _():
            total, mean, rstd = merge_stats(stat_ref, width)
            by_gain = sums_ref[0, 0:1, :width]
            by_bias = sums_ref[0, 1:2, :width]
            for node in range(1, nodes):
                by_gain += sums_ref[node, 0:1, :width]
                by_bias += sums_ref[node, 1:2, :width]
            norm[0:1, :] = mean
            norm[1:2, :] = rstd
            norm[2:3, :] = by_gain / total
            norm[3:4, :] = by_bias / total
            norm[4:5, :] = rstd * scale_ref[...]
            total_ref[...] = jnp.zeros_like(total_ref)
            total_ref[0:1, :] = by_gain
            total_ref[1:2, :] = by_bias

        def one(piece, carry):
            begin = pl.multiple_of(piece * sub, 16)
            here = pl.ds(begin, sub)
            live = (
                lax.broadcasted_iota(i32, (sub, LANE), 0) + (step * tile + begin) < off_ref[slots]
            )
            for part in range(parts):
                lanes = slice(part * LANE, (part + 1) * LANE)
                normed = (lin_ref[part, here, :] - norm[0:1, lanes]) * norm[1:2, lanes]
                value = norm[4:5, lanes] * (
                    grad_ref[part, here, :] - norm[3:4, lanes] - normed * norm[2:3, lanes]
                )
                into, at = divmod(part * LANE, share)
                out_refs[into][here, at : at + LANE] = jnp.where(live, value, 0.0).astype(bf16)
            return carry

        lax.fori_loop(0, tile // sub, one, 0)

    return pl.pallas_call(
        kernel,
        grid=(rows // tile,),
        out_shape=[jax.ShapeDtypeStruct((rows, share), bf16)] * pieces
        + [jax.ShapeDtypeStruct((8, width), f32)],
        in_specs=[
            smem(),
            pl.BlockSpec((parts, tile, LANE), lambda i: (0, i, 0)),
            pl.BlockSpec((parts, tile, LANE), lambda i: (0, i, 0)),
            fixed(stats.shape),
            fixed(sums.shape),
            pl.BlockSpec((1, width), lambda i: (0, block)),
        ],
        out_specs=[pl.BlockSpec((tile, share), lambda i: (i, 0))] * pieces
        + [pl.BlockSpec((8, width), lambda i: (0, 0))],
        scratch_shapes=[pltpu.VMEM((8, width), f32)],
        compiler_params=params(),
        cost_estimate=cost(10 * rows * width, 10 * rows * width),
        name="linear_grad",
    )(offsets, linear, grad, stats, sums, scale)


def grad_products(grads, weights, places):
    rows = grads[0].shape[0]
    feat_width = weights[0].shape[0]
    parts = feat_width // LANE
    tile = rows // 4
    sub = tile // 2
    count = len(grads)
    depth = sum(g.shape[1] for g in grads)

    def kernel(*refs):
        out_ref = refs[-1]
        right = jnp.concatenate([ref[...] for ref in refs[count : 2 * count]], 1)
        for piece in range(tile // sub):
            here = slice(piece * sub, (piece + 1) * sub)
            left = jnp.concatenate([ref[here, :] for ref in refs[:count]], 1)
            value = dot(left, right, 1, 1)
            for part in range(parts):
                out_ref[part, here, :] = value[:, part * LANE : (part + 1) * LANE]

    def column(place, width):
        return pl.BlockSpec((feat_width, width), lambda i: (0, place))

    return pl.pallas_call(
        kernel,
        grid=(rows // tile,),
        out_shape=jax.ShapeDtypeStruct((parts, rows, LANE), f32),
        in_specs=[pl.BlockSpec((tile, g.shape[1]), lambda i: (i, 0)) for g in grads]
        + [column(p // g.shape[1], g.shape[1]) for p, g in zip(places, grads, strict=True)],
        out_specs=pl.BlockSpec((parts, tile, LANE), lambda i: (0, i, 0)),
        compiler_params=params(),
        cost_estimate=cost(2 * rows * feat_width * depth, rows * (4 * feat_width + 2 * depth)),
        name="grad_products",
    )(*grads, *weights)


def slot_grads(held, grads, weights, place, tiles, inv, offsets, counts):
    slots = tiles.shape[0]
    parts, rows, _ = held.shape
    width = parts * LANE
    count = len(grads)
    share = grads[0].shape[1]
    blocks = 8
    sub = rows // blocks
    team = 4

    def kernel(off_ref, counts_ref, held_ref, *refs):
        grad_refs, weight_refs = refs[:count], refs[count : 2 * count]
        tile_ref, inv_ref, out_ref, halo_ref, total, link_total, sems = refs[2 * count :]

        def copy(block):
            here = pl.ds(pl.multiple_of(block * sub, 16), sub)
            return pltpu.make_async_copy(
                held_ref.at[:, here, :], total.at[:, here, :], sems.at[block]
            )

        for block in range(blocks):
            copy(block).start()
        right = jnp.concatenate([ref[...] for ref in weight_refs], 1)
        link_total[...] = jnp.zeros_like(link_total)

        def add(block, carry):
            here = pl.ds(pl.multiple_of(block * sub, 16), sub)
            value = dot(jnp.concatenate([ref[here, :] for ref in grad_refs], 1), right, 1, 1)
            copy(block).wait()
            for part in range(parts):
                total[part, here, :] += value[:, part * LANE : (part + 1) * LANE]
            return carry

        lax.fori_loop(0, blocks, add, 0)
        place_row = lax.broadcasted_iota(i32, (SLOT, LANE), 0)

        def one(step, carry):
            pieces = []
            for member in range(team):
                slot = step * team + member
                start = off_ref[slot]
                live = place_row < counts_ref[slot]
                scale = column_of(inv_ref, slot)
                row = []
                for part in range(parts):
                    value = total[part, pl.ds(start, SLOT), :].astype(bf16).astype(f32)
                    row.append(jnp.where(live, value * scale, 0.0).astype(bf16))
                piece = jnp.concatenate(row, 1)
                out_ref[pl.ds(pl.multiple_of(slot * SLOT, SLOT), SLOT), :] = piece
                pieces.append(piece)
            link = jnp.concatenate(
                [tile_ref[step * team + member, SLOT:, :] for member in range(team)], 1
            )
            link_total[...] += dot(link, jnp.concatenate(pieces, 0))
            return carry

        lax.fori_loop(0, slots // team, one, 0)
        halo_ref[...] = link_total[...].astype(bf16)

    return pl.pallas_call(
        kernel,
        grid=(1,),
        out_shape=[
            jax.ShapeDtypeStruct((slots * SLOT, width), bf16),
            jax.ShapeDtypeStruct((2 * SLOT, width), bf16),
        ],
        in_specs=[smem(), smem(), pl.BlockSpec(memory_space=pl.ANY)]
        + [fixed((rows, share))] * count
        + [
            pl.BlockSpec(
                (width, share), lambda i: (0, place // share), pipeline_mode=pl.Buffered(1)
            )
        ]
        * count
        + [fixed(tiles.shape), fixed(inv.shape)],
        out_specs=[fixed((slots * SLOT, width)), fixed((2 * SLOT, width))],
        scratch_shapes=[
            pltpu.VMEM((parts, rows + SLOT, LANE), f32),
            pltpu.VMEM((2 * SLOT, width), f32),
            pltpu.SemaphoreType.DMA((blocks,)),
        ],
        compiler_params=params(),
        cost_estimate=cost(4 * slots * SLOT * SLOT * width, 6 * slots * SLOT * width),
        name="slot_grads",
    )(offsets, counts, held, *grads, *weights, tiles, inv)


def input_grads(slot_grad, tiles, returned, send_row, counts):
    rows, width = slot_grad.shape
    sends = send_row.shape[1]

    def kernel(counts_ref, grad_ref, tile_ref, back_ref, send_ref, out_ref):
        step = pl.program_id(0)

        def pair(turn, carry):
            for side in range(2):
                member = turn * 2 + side
                slot = step * GROUP + member
                here = pl.ds(pl.multiple_of(member * SLOT, SLOT), SLOT)
                hot = chosen(send_ref, slot * SLOT, SLOT, counts_ref[slot])
                value = dot(tile_ref[member], grad_ref[here, :])
                out_ref[here, :] = value + dot(hot, back_ref[...])
            return carry

        lax.fori_loop(0, GROUP // 2, pair, 0)

    return pl.pallas_call(
        kernel,
        grid=(rows // (GROUP * SLOT),),
        out_shape=jax.ShapeDtypeStruct((rows, width), f32),
        in_specs=[
            smem(),
            pl.BlockSpec((GROUP * SLOT, width), lambda i: (i, 0)),
            pl.BlockSpec((GROUP, SLOT, SLOT), lambda i: (i, 0, 0)),
            fixed((sends, width)),
            fixed((1, sends)),
        ],
        out_specs=pl.BlockSpec((GROUP * SLOT, width), lambda i: (i, 0)),
        compiler_params=params(),
        cost_estimate=cost(2 * rows * 3 * SLOT * width, 6 * rows * width),
        name="input_grads",
    )(counts, slot_grad, tiles, returned, send_row)


def last_pass(act, slot_grad, returned, shares, tiles, send_row, counts):
    rows, width = slot_grad.shape
    sends = send_row.shape[1]
    nodes = shares.shape[0]
    group = rows // SLOT // nodes

    def kernel(counts_ref, act_ref, grad_ref, tile_ref, back_ref, send_ref, share_ref, *outs):
        act_out, grad_out, weight_out = outs
        step = pl.program_id(0)
        act_out[...] = act_ref[...]
        weight_out[...] = share_ref[...].astype(f32).reshape(weight_out.shape)

        def pair(turn, carry):
            for side in range(2):
                member = turn * 2 + side
                slot = step * group + member
                here = pl.ds(pl.multiple_of(member * SLOT, SLOT), SLOT)
                hot = chosen(send_ref, slot * SLOT, SLOT, counts_ref[slot])
                value = dot(tile_ref[member], grad_ref[here, :])
                grad_out[here, :] = value + dot(hot, back_ref[...])
            return carry

        lax.fori_loop(0, group // 2, pair, 0)

    return pl.pallas_call(
        kernel,
        grid=(nodes,),
        out_shape=[
            jax.ShapeDtypeStruct((rows, width), f32),
            jax.ShapeDtypeStruct((rows, width), f32),
            jax.ShapeDtypeStruct((2, nodes, LANE, width), f32),
        ],
        in_specs=[
            smem(),
            pl.BlockSpec((group * SLOT, width), lambda i: (i, 0)),
            pl.BlockSpec((group * SLOT, width), lambda i: (i, 0)),
            pl.BlockSpec((group, SLOT, SLOT), lambda i: (i, 0, 0)),
            fixed((sends, width)),
            fixed((1, sends)),
            pl.BlockSpec((1, 2, LANE, width), lambda i: (i, 0, 0, 0)),
        ],
        out_specs=[
            pl.BlockSpec((group * SLOT, width), lambda i: (i, 0)),
            pl.BlockSpec((group * SLOT, width), lambda i: (i, 0)),
            pl.BlockSpec((2, 1, LANE, width), lambda i: (0, i, 0, 0)),
        ],
        compiler_params=params(),
        cost_estimate=cost(0, 0),
        name="last_pass",
    )(counts, act, slot_grad, tiles, returned, send_row, shares)


def node_shift(block, distance):
    nodes = range(lax.axis_size("node"))
    return lax.ppermute(
        block, "node", [(i - distance, i) for i in nodes if i - distance in nodes]
    )


def to_sibling(block):
    return lax.ppermute(block, "mp", [(i, i ^ 1) for i in range(lax.axis_size("mp"))])


def to_chip(block, distance):
    size = lax.axis_size("mp")
    return lax.ppermute(block, "mp", [(i, (i + 2 * distance) % size) for i in range(size)])


def node_flip(block, bit):
    return lax.ppermute(block, "node", [(i, i ^ bit) for i in range(lax.axis_size("node"))])


def scatter_sum(value, axis):
    me, bit = lax.axis_index("node"), 1
    while bit < lax.axis_size("node"):
        mine = lax.rem(me // bit, 2)
        half = value.shape[axis] // 2
        keep = lax.dynamic_slice_in_dim(value, mine * half, half, axis)
        give = lax.dynamic_slice_in_dim(value, (1 - mine) * half, half, axis)
        value = keep + node_flip(give, bit)
        bit *= 2
    return value


def gather_shares(value, axis):
    me, bit = lax.axis_index("node"), lax.axis_size("node") // 2
    while bit >= 1:
        mine = lax.rem(me // bit, 2)
        other = node_flip(value, bit)
        low = jnp.where(mine == 0, value, other)
        high = jnp.where(mine == 0, other, value)
        value = jnp.concatenate([low, high], axis)
        bit //= 2
    return value


def core(
    features, weight, cotangent, near, links, send_row, scale, shift, lists, nodes, compact
):
    rows, fw = features.shape
    entries, link_entries = near.shape[0], links.shape[0]
    gain, bias = (v.reshape(fw // LANE, 1, LANE) for v in (scale, shift))
    slots = rows // SLOT
    quarter = fw // LANE
    tile = 3 * SLOT
    turns = compact // tile
    padded = rows + 2 * SLOT
    wide = fw // 2
    team = 4
    groups = slots // team
    ranges = [(0, 5), (5, 10), (10, turns)]
    early = 2
    slope, cubic = 0.7978845608028654, 0.044715
    sizes = {0: 2, 1: 1, 2: 1}
    firsts = {0: 0, 1: 2, 2: 3}

    def kernel(*refs):
        off_ref, cnt_ref, first_ref, feat_hbm, w_hbm, cot_hbm = refs[:6]
        near_ref, link_ref, send_ref, gain_ref, bias_ref = refs[6:11]
        act_hbm, slot_hbm, back_ref, wag_hbm, tot_ref, tile_hbm = refs[11:17]
        own, sib, stage, recv, glp, gls, big, wacc = refs[17:25]
        stg_a, stg_b, rs_a, rs_b, ag_a, ag_b, hop_a, hop_b = refs[25:33]
        fbuf, tbuf, cbuf, abuf, gbuf, sbuf, ebuf, st, sums, norm, link_total, hbuf, hback = refs[33:46]
        fsem, tsem, csem, asem, gsem = refs[46:51]
        d1s, d1r, x1s, x1r, x2s, x2r, d2s, d2r, f2s, f2r = refs[51:61]
        e_s, e_r, r_s, r_r, a_s, a_r, b_s, b_r, lsem, credit = refs[61:71]
        ws_ref, w_s, w_r, wc_ref, wp_ref, wsem, v_s, v_r, halo_ref, inv_ref = refs[71:81]
        u_s, u_r, h_s, h_r = refs[81:85]

        me = lax.axis_index("node")
        place = lax.axis_index("mp")
        chip, side = place // 2, place % 2
        peer_id = {"mp": (1 - chip) * 2 + side}
        sib_id = {"mp": chip * 2 + 1 - side}
        total = off_ref[slots]

        def node_id(step):
            return {"node": (me + step) % nodes}

        def across_id(step):
            return {"node": (me + step) % nodes, "mp": (1 - chip) * 2 + side}

        def weight_copy(mine, q):
            chosen_rows = chip if mine else 1 - chip
            return pltpu.make_async_copy(
                w_hbm.at[
                    pl.ds(pl.multiple_of(chosen_rows * 2 * fw, SLOT), 2 * fw),
                    pl.ds(q * LANE, LANE),
                ],
                big.at[q, pl.ds(mine * 2 * fw, 2 * fw)],
                wsem.at[mine * quarter + q],
            )

        for mine in range(2):
            for q in range(quarter):
                weight_copy(mine, q).start()
        barrier = pltpu.get_barrier_semaphore()
        targets = [sib_id] + [node_id(step) for step in range(1, nodes)]
        for target in targets + [across_id(step) for step in range(nodes)]:
            pl.semaphore_signal(barrier, inc=1, device_id=target, device_id_type=MESH)

        def remote(src, dst, send, arrive, target):
            return pltpu.make_async_remote_copy(
                src_ref=src,
                dst_ref=dst,
                send_sem=send,
                recv_sem=arrive,
                device_id=target,
                device_id_type=MESH,
            )

        def at(turn):
            return pl.ds(pl.multiple_of(turn * tile, SLOT), tile)

        def own_half(ref, columns):
            return ref[pl.ds(pl.multiple_of(side * fw, SLOT), fw), columns]

        def sib_half(ref, columns):
            return ref[pl.ds(pl.multiple_of((1 - side) * fw, SLOT), fw), columns]

        def loop(low, high, body):
            def step(index, carry):
                body(index)
                return carry

            lax.fori_loop(low, high, step, 0)

        def span(low, high):
            return pl.ds(pl.multiple_of(low * tile, SLOT), (high - low) * tile)

        every = span(0, turns)

        def send_own(t, rows_of=None):
            here = at(t) if rows_of is None else rows_of
            return remote(
                own.at[here], sib.at[here], d1s.at[0], d1r.at[0 if rows_of else t], sib_id
            )

        def send_partial(b, part, here):
            two = pl.ds(2 * b, 2)
            return remote(
                stage.at[two, here], recv.at[two, here], x1s.at[b], x1r.at[3 * b + part], peer_id
            )

        def send_grad(p, part, here):
            some = pl.ds(firsts[p], sizes[p])
            return remote(
                stage.at[some, here], glp.at[some, here], x2s.at[p], x2r.at[3 * p + part], peer_id
            )

        def give_grad(b, here):
            two = pl.ds(2 * b, 2)
            return remote(stage.at[two, here], gls.at[two, here], d2s.at[b], d2r.at[b], sib_id)

        def forward_grad(p, part, here):
            some = pl.ds(firsts[p], sizes[p])
            return remote(
                glp.at[some, here], recv.at[some, here], f2s.at[p], f2r.at[p + part], sib_id
            )

        def picked_rows(block):
            slot = first_ref[block]
            base = block * SLOT
            starts = []
            for step in range(3):
                here = jnp.minimum(slot + step, slots - 1)
                starts.append(
                    jnp.clip(here * SLOT + base - off_ref[here] + SLOT, 0, padded - SLOT)
                )
            place_row = lax.broadcasted_iota(i32, (SLOT, LANE), 0)
            one = place_row < off_ref[jnp.minimum(slot + 1, slots)] - base
            two = place_row < off_ref[jnp.minimum(slot + 2, slots)] - base
            live = place_row < total - base

            def pick(q):
                value = jnp.where(two, big[q, pl.ds(starts[1], SLOT), :], big[q, pl.ds(starts[2], SLOT), :])
                value = jnp.where(one, big[q, pl.ds(starts[0], SLOT), :], value)
                return jnp.where(live, value, 0.0)

            return pick

        def send_weights(which):
            src = wp_ref if which else wc_ref
            return remote(
                src.at[pl.ds(pl.multiple_of((1 - side) * fw, SLOT), fw)],
                ws_ref.at[pl.ds(which * fw, fw)],
                w_s.at[which],
                w_r.at[which],
                sib_id,
            )

        first_half, second_half = slice(0, wide), slice(wide, fw)

        def send_upper_weights():
            columns = pl.ds(0, wide)
            return remote(
                gbuf.at[0, :, columns], wp_ref.at[pl.ds(0, fw), columns], v_s.at[2], v_r.at[2], peer_id
            )

        per_half = nodes // 2

        def share_of_weights(which):
            if which == 0:
                start = pl.multiple_of(me * (LANE // 2), LANE // 2)
                source = gbuf.at[1, pl.ds(start, LANE // 2), pl.ds(0, wide)]
                return source, wp_ref.at[pl.ds(fw + start, LANE // 2), pl.ds(0, wide)]
            start = pl.multiple_of((me % per_half) * LANE, LANE)
            source = gbuf.at[me // per_half, pl.ds(start, LANE), pl.ds(wide, wide)]
            into = pl.ds(pl.multiple_of(me * LANE, LANE), LANE)
            return source, wp_ref.at[into, pl.ds(wide, wide)]

        def send_weight_share(which):
            source, into = share_of_weights(which)
            return remote(source, into, v_s.at[which], v_r.at[which], peer_id)

        def spread_weights(which):
            _, into = share_of_weights(which)
            for step in range(1, nodes):
                remote(into, into, u_s.at[which], u_r.at[which], node_id(step)).start()

        def spread_weights_end(which):
            count = (nodes - 1) * (LANE // 2 if which == 0 else LANE)
            some = wp_ref.at[pl.ds(0, count), pl.ds(which * wide, wide)]
            return remote(some, some, u_s.at[which], u_r.at[which], node_id(1))

        def loads(g):
            return pltpu.make_async_copy(
                feat_hbm.at[pl.ds(pl.multiple_of(g * team * SLOT, SLOT), team * SLOT)],
                fbuf.at[g % 3],
                fsem.at[g % 3],
            )

        for g in range(3):
            loads(g).start()
        for q in range(quarter):
            lanes = slice(q * LANE, (q + 1) * LANE)
            weight_copy(0, q).wait()
            for number in range(2):
                gbuf[number, :, lanes] = big[q, number * fw : (number + 1) * fw, :].astype(bf16)
        wanted = [
            jnp.transpose(
                jnp.broadcast_to(
                    send_ref[:, part * LANE : (part + 1) * LANE].astype(f32), (LANE, LANE)
                )
            )
            for part in range(2)
        ]
        wanted = jnp.concatenate(wanted, 0).astype(i32)
        lane = lax.broadcasted_iota(i32, (2 * SLOT, LANE), 1)
        link_total[...] = jnp.zeros_like(link_total)

        def pick_group(g):
            loads(g).wait()
            hot = []
            for member in range(team):
                slot = g * team + member
                hit = (wanted == lane + slot * SLOT) & (lane < cnt_ref[slot])
                hot.append(jnp.where(hit, 1.0, 0.0).astype(bf16))
            link_total[...] += dot(jnp.concatenate(hot, 1), fbuf[g % 3])

            @pl.when(g + 3 < groups)
            def _():
                loads(g + 3).start()

        loop(0, groups, pick_group)
        hbuf[...] = link_total[...].astype(bf16)
        half_rows = SLOT
        halo_in = [
            remote(
                hbuf.at[:half_rows], halo_ref.at[:half_rows], b_s.at[2], b_r.at[2], node_id(1)
            ),
            remote(
                hbuf.at[half_rows:],
                halo_ref.at[half_rows:],
                b_s.at[3],
                b_r.at[3],
                node_id(nodes - 1),
            ),
        ]
        pl.semaphore_wait(barrier, 2 * nodes)
        send_weight_share(0).start()
        send_upper_weights().start()
        send_weight_share(1).start()
        for copy in halo_in:
            copy.start()
        for q in range(quarter):
            weight_copy(1, q).wait()
            wc_ref[:, q * LANE : (q + 1) * LANE] = big[q, 2 * fw : 4 * fw, :].astype(bf16)
        for g in range(2):
            loads(g).start()

        row = lax.broadcasted_iota(i32, (SLOT, SLOT), 0)
        column = lax.broadcasted_iota(i32, (SLOT, SLOT), 1)
        link_row = lax.broadcasted_iota(i32, (2 * SLOT, SLOT), 0)
        unit = jnp.where(row == column, 1.0, 0.0).astype(bf16)

        def tile_copy(g):
            return pltpu.make_async_copy(
                tbuf.at[g % 3], tile_hbm.at[pl.ds(g * team, team)], tsem.at[g % 3]
            )

        def count_group(g):
            spot = g % 3

            def one(member):
                slot = g * team + member
                lanes = pl.ds(pl.multiple_of(slot * SLOT, SLOT), SLOT)
                near_here, link_here = near_ref[:, lanes], link_ref[:, lanes]
                counted = jnp.zeros((SLOT, SLOT), f32)
                for entry in range(entries):
                    counted += jnp.where(near_here[entry : entry + 1] == row, 1.0, 0.0)
                linked = jnp.zeros((2 * SLOT, SLOT), f32)
                for entry in range(link_entries):
                    linked += jnp.where(link_here[entry : entry + 1] == link_row, 1.0, 0.0)
                degree = (
                    1.0 + jnp.sum(counted, 0, keepdims=True) + jnp.sum(linked, 0, keepdims=True)
                )
                matrix = counted + jnp.where(row == column, counted + 2.0, 0.0)
                matrix = jnp.where(row < cnt_ref[slot], matrix, 0.0)
                tbuf[spot, member, :SLOT, :] = matrix.astype(bf16)
                tbuf[spot, member, SLOT:, :] = linked.astype(bf16)
                inv_ref[slot] = jnp.broadcast_to(1.0 / degree, (8, SLOT))

            loop(0, team, one)
            tile_copy(g).start()

        send_weight_share(0).wait_recv()
        spread_weights(0)
        count_group(0)
        count_group(1)
        for copy in halo_in:
            copy.wait()
        halo_ref[:half_rows, :] = jnp.where(
            me == 0, 0.0, halo_ref[:half_rows, :].astype(f32)
        ).astype(bf16)
        halo_ref[half_rows:, :] = jnp.where(
            me == nodes - 1, 0.0, halo_ref[half_rows:, :].astype(f32)
        ).astype(bf16)

        def partial(b, t):
            part = jnp.where(t < ranges[0][1], 0, jnp.where(t < ranges[1][1], 1, 2))
            columns = second_half if b else first_half
            value = dot(own[at(t), :], own_half(wp_ref, columns))
            value += dot(sib[at(t), :], sib_half(wp_ref, columns))
            for q in range(2):
                stage[2 * b + q, at(t), :] = value[:, q * LANE : (q + 1) * LANE].astype(bf16)
            send_partial(b, part, at(t)).start()

        def first_partial(t):
            send_own(t).wait_recv()
            partial(0, t)

        def compact_tile(t):
            for step in range(3):
                block = t * 3 + step
                pick = picked_rows(block)
                into = pl.ds(pl.multiple_of(block * SLOT, SLOT), SLOT)
                for q in range(quarter):
                    own[into, q * LANE : (q + 1) * LANE] = pick(q).astype(bf16)
            send_own(t).start()

            @pl.when(t == 1)
            def _():
                send_weight_share(1).wait_recv()
                spread_weights(1)
                send_upper_weights().wait_recv()
                spread_weights_end(0).wait_recv()

            @pl.when(t >= 1)
            def _():
                first_partial(t - 1)

        def ready(g):
            return jnp.where(g == groups - 1, turns, jnp.minimum((team * (g + 1)) // 6, turns))

        def gather_group(g):
            @pl.when(g + 2 < groups)
            def _():
                loads(g + 2).start()

                @pl.when(g >= 1)
                def _():
                    tile_copy(g - 1).wait()

                count_group(g + 2)

            loads(g).wait()
            spot = g % 3
            for member in range(team):
                slot = g * team + member
                matrix = dot(unit, tbuf[spot, member], 1, 1).astype(bf16)
                value = dot(matrix[:, :SLOT], fbuf[spot, member * SLOT : (member + 1) * SLOT, :])
                value += dot(matrix[:, SLOT:], halo_ref[...])
                scale = column_of(inv_ref, slot)
                into = pl.ds(pl.multiple_of((slot + 1) * SLOT, SLOT), SLOT)
                for q in range(quarter):
                    big[q, into, :] = value[:, q * LANE : (q + 1) * LANE] * scale
            done = jnp.where(g == 0, 0, jnp.minimum((team * g) // 6, turns))
            loop(done, ready(g), compact_tile)

        loop(0, groups, gather_group)
        first_partial(turns - 1)
        spread_weights_end(1).wait_recv()
        loop(0, turns, lambda t: partial(1, t))
        send_weights(0).start()
        send_weights(1).start()
        send_upper_weights().wait_send()
        for which in range(2):
            send_weight_share(which).wait_send()
            spread_weights_end(which).wait_send()
        for g in range(groups - 3, groups):
            tile_copy(g).wait()

        def exchange_block(number):
            for step in range(1, nodes):
                remote(
                    sbuf.at[number],
                    ebuf.at[number, step],
                    e_s.at[number],
                    e_r.at[number],
                    node_id(step),
                ).start()
            ebuf[number, 0] = sbuf[number]
            others = ebuf.at[number, pl.ds(1, nodes - 1)]
            remote(others, others, e_s.at[number], e_r.at[number], node_id(1)).wait()

        def row_of(number, line):
            return [ebuf[number, node, line : line + 1, :] for node in range(nodes)]

        def norm_block(b):
            columns = second_half if b else first_half
            st[...] = jnp.zeros_like(st)

            def linear_tile(t):
                value = dot(own[at(t), :], own_half(wc_ref, columns))
                value += dot(sib[at(t), :], sib_half(wc_ref, columns))
                begin = t * tile
                before = jnp.minimum(begin, total)
                here = jnp.minimum(begin + tile, total) - before
                seen, new = before.astype(f32), here.astype(f32)
                for part in range(2):
                    lanes = slice(part * LANE, (part + 1) * LANE)
                    piece = value[:, lanes] + recv[2 * b + part, at(t), :].astype(f32)
                    big[part, at(t), :] = piece
                    both = jnp.full((1, LANE), jnp.maximum(seen + new, 1.0), f32)
                    live = lax.broadcasted_iota(i32, (tile, LANE), 0) < here
                    mean_here = jnp.sum(jnp.where(live, piece, 0.0), 0, keepdims=True) / jnp.full(
                        (1, LANE), jnp.maximum(new, 1.0), f32
                    )
                    centred = jnp.where(live, piece - mean_here, 0.0)
                    squares = jnp.sum(centred * centred, 0, keepdims=True)
                    mean, held = st[0:1, lanes], st[1:2, lanes]
                    gap = mean_here - mean
                    ratio = new / both
                    st[0:1, lanes] = mean + gap * ratio
                    st[1:2, lanes] = held + squares + gap * gap * (seen * ratio)

            for part, (low, high) in enumerate(ranges):
                send_partial(b, part, span(low, high)).wait_recv()
                loop(low, high, linear_tile)
            if b == 1:
                pl.semaphore_signal(credit, inc=1, device_id=sib_id, device_id_type=MESH)
            st[2:3, :] = jnp.full((1, wide), total.astype(f32), f32)
            sbuf[2 * b] = st[...]

            def cot_copy(g):
                return pltpu.make_async_copy(
                    cot_hbm.at[
                        pl.ds(pl.multiple_of(g * team * SLOT, SLOT), team * SLOT),
                        pl.ds(b * wide, wide),
                    ],
                    cbuf.at[g % 2],
                    csem.at[g % 2],
                )

            def act_copy(g):
                return pltpu.make_async_copy(
                    abuf.at[g % 2],
                    act_hbm.at[
                        pl.ds(pl.multiple_of(g * team * SLOT, SLOT), team * SLOT),
                        pl.ds(b * wide, wide),
                    ],
                    asem.at[g % 2],
                )

            cot_copy(0).start()
            exchange_block(2 * b)
            numbers, means, squares = (row_of(2 * b, line) for line in (2, 0, 1))
            count = sum(numbers[1:], numbers[0])
            mean = sum([n * m for n, m in zip(numbers, means, strict=True)][1:], numbers[0] * means[0])
            mean = mean / count
            spread = jnp.zeros_like(mean)
            for n, m, s in zip(numbers, means, squares, strict=True):
                spread += s + n * (m - mean) * (m - mean)
            norm[0:1, :] = mean
            norm[1:2, :] = lax.rsqrt(spread / count + epsilon)
            sums[...] = jnp.zeros_like(sums)
            half_slot = SLOT // 2
            place_row = lax.broadcasted_iota(i32, (half_slot, LANE), 0)

            def act_group(g):
                @pl.when(g + 1 < groups)
                def _():
                    cot_copy(g + 1).start()

                cot_copy(g).wait()

                @pl.when(g >= 2)
                def _():
                    act_copy(g - 2).wait()

                spot = g % 2

                def one(member):
                    slot = g * team + member
                    for part in range(2):
                        lanes = slice(part * LANE, (part + 1) * LANE)
                        mean_here, rstd = norm[0:1, lanes], norm[1:2, lanes]
                        scale, shift = gain_ref[2 * b + part], bias_ref[2 * b + part]
                        for turn in range(2):
                            live = place_row < cnt_ref[slot] - turn * half_slot
                            here = pl.ds(
                                pl.multiple_of(member * SLOT + turn * half_slot, half_slot),
                                half_slot,
                            )
                            value = big[
                                part, pl.ds(off_ref[slot] + turn * half_slot, half_slot), :
                            ]
                            value = jnp.where(live, value, 0.0)
                            normed = (value - mean_here) * rstd
                            z = scale * normed + shift
                            square = z * z
                            bent = jnp.tanh(z * (slope + (slope * cubic) * square))
                            half = 0.5 + 0.5 * bent
                            abuf[spot, here, lanes] = jnp.where(live, z * half, 0.0)
                            back = half + z * (1.0 - bent * bent) * (
                                0.5 * slope + (1.5 * slope * cubic) * square
                            )
                            grad = jnp.where(live, cbuf[spot, here, lanes].astype(f32) * back, 0.0)
                            into = pl.ds(
                                pl.multiple_of((slot + 1) * SLOT + turn * half_slot, half_slot),
                                half_slot,
                            )
                            big[2 + part, into, :] = grad
                            tall = (half_slot // 8, 8, LANE)
                            sums[0, :, lanes] += jnp.sum((grad * normed).reshape(tall), 0)
                            sums[1, :, lanes] += jnp.sum(grad.reshape(tall), 0)

                loop(0, team, one)
                act_copy(g).start()

            loop(0, groups, act_group)
            sbuf[2 * b + 1] = jnp.zeros((8, wide), f32)
            sbuf[2 * b + 1, 0:1, :] = jnp.sum(sums[0], 0, keepdims=True)
            sbuf[2 * b + 1, 1:2, :] = jnp.sum(sums[1], 0, keepdims=True)
            exchange_block(2 * b + 1)
            by_gain, by_bias = (row_of(2 * b + 1, line) for line in (0, 1))
            by_gain = sum(by_gain[1:], by_gain[0])
            by_bias = sum(by_bias[1:], by_bias[0])
            fullest = numbers[0]
            for number in numbers[1:]:
                fullest = jnp.maximum(fullest, number)
            tot_ref[2:3, columns] = fullest
            tot_ref[0:1, columns] = by_gain
            tot_ref[1:2, columns] = by_bias
            norm[2:3, :] = by_gain / count
            norm[3:4, :] = by_bias / count
            act_copy(groups - 2).wait()
            act_copy(groups - 1).wait()

            def grad_tile(t):
                for step in range(3):
                    block = t * 3 + step
                    pick = picked_rows(block)
                    here = pl.ds(pl.multiple_of(block * SLOT, SLOT), SLOT)
                    live = lax.broadcasted_iota(i32, (SLOT, LANE), 0) < total - block * SLOT
                    for part in range(2):
                        lanes = slice(part * LANE, (part + 1) * LANE)
                        rstd = norm[1:2, lanes]
                        normed = (big[part, here, :] - norm[0:1, lanes]) * rstd
                        value = (rstd * gain_ref[2 * b + part]) * (
                            pick(2 + part) - norm[3:4, lanes] - normed * norm[2:3, lanes]
                        )
                        stage[2 * b + part, here, :] = jnp.where(live, value, 0.0).astype(bf16)
                give_grad(b, at(t)).start()
                send_grad(b, part_number[0], at(t)).start()

            send_partial(b, 0, every).wait_send()
            for part, (low, high) in enumerate(ranges):
                part_number = [part]
                loop(low, high, grad_tile)
            if b == 1:
                loop(0, early, lambda t: send_grad(2, t, at(t)).start())

        def weight_part(source, qs, low, high, fresh):
            some = pl.ds(low * tile, (high - low) * tile)
            left = jnp.concatenate([source[q, some, :] for q in qs], 1)
            width = LANE * len(qs)
            for number, half in enumerate((own, sib)):
                into = slice(number * fw, (number + 1) * fw)
                value = dot(left, half[some, :], 0, 0)
                if fresh:
                    wacc[:width, into] = value
                else:
                    wacc[:width, into] += value

        def share_of(p, kind):
            return (stg_a, rs_a, ag_a, kind) if p == 0 else (stg_b, rs_b, ag_b, 2 * p - 2 + kind)

        def store_shares(p, kind, line):
            stg, _, _, k = share_of(p, kind)
            width = sizes[p] * LANE
            per = fw // LANE
            for number in range(2):
                base = (side if number == 0 else 1 - side) * per
                for step in range(per):
                    lanes = slice(number * fw + step * LANE, number * fw + (step + 1) * LANE)
                    stg[k, base + step] = wacc[line : line + width, lanes].astype(bf16)

        def crosses(p, kind):
            return kind == 1 and p == 2

        def scatter(p, kind):
            stg, rs, _, k = share_of(p, kind)
            index = 2 * p + kind
            return [
                remote(
                    stg.at[k, (me + step) % nodes],
                    rs.at[k, step],
                    r_s.at[index],
                    r_r.at[index],
                    across_id(step) if crosses(p, kind) else node_id(step),
                )
                for step in range(0 if crosses(p, kind) else 1, nodes)
            ]

        def scattered(p, kind):
            _, rs, _, k = share_of(p, kind)
            first = 0 if crosses(p, kind) else 1
            shares = rs.at[k, pl.ds(first, nodes - first)]
            index = 2 * p + kind
            return remote(shares, shares, r_s.at[index], r_r.at[index], peer_id)

        def begin(copies):
            for copy in copies:
                copy.start()

        def finish(copies):
            for copy in copies:
                copy.wait()

        def hop(p):
            _, _, ag, k = share_of(p, 1)
            return remote(hop_b if p else hop_a, ag.at[k], h_s.at[p], h_r.at[p], peer_id)

        def spread_share(p, kind):
            _, _, ag, k = share_of(p, kind)
            src = ag.at[k]
            index = 2 * p + kind
            which = chip if kind == 0 else 1 - chip
            dst = wag_hbm.at[me, which, :, pl.ds(firsts[p] * LANE, sizes[p] * LANE)]
            copies = [
                remote(src, dst, a_s.at[index], a_r.at[index], node_id(step))
                for step in range(1, nodes)
            ]
            return copies, pltpu.make_async_copy(src, dst, lsem.at[2 * p + kind])

        def begin_spread(p, kind):
            copies, here = spread_share(p, kind)
            begin(copies)
            here.start()

        def finish_spread(p, kind):
            _, here = spread_share(p, kind)
            index = 2 * p + kind
            shares = wag_hbm.at[
                pl.ds(0, nodes - 1), 0, :, pl.ds(firsts[p] * LANE, sizes[p] * LANE)
            ]
            remote(shares, shares, a_s.at[index], a_r.at[index], node_id(1)).wait()
            here.wait()

        def sum_shares(p, kind):
            scattered(p, kind).wait()
            stg, rs, ag, k = share_of(p, kind)
            value = (rs[k, 0] if crosses(p, kind) else stg[k, me]).astype(f32)
            for step in range(1, nodes):
                value += rs[k, step].astype(f32)
            value = jnp.transpose(value).astype(bf16)
            if kind == 1 and not crosses(p, kind):
                (hop_b if p else hop_a)[...] = value
                hop(p).start()
            else:
                ag[k] = value
                begin_spread(p, kind)

        def end_hop(p):
            hop(p).wait()
            begin_spread(p, 1)

        def product(p, t, fresh):
            qs = range(firsts[p], firsts[p] + sizes[p])
            columns = slice(firsts[p] * LANE, (firsts[p] + sizes[p]) * LANE)
            left = jnp.concatenate([ref[q, at(t), :] for ref in (stage, glp, gls, recv) for q in qs], 1)
            right = jnp.concatenate(
                [
                    own_half(wc_ref, columns),
                    own_half(wp_ref, columns),
                    ws_ref[:fw, columns],
                    ws_ref[fw:, columns],
                ],
                1,
            )
            value = dot(left, right, 1, 1)
            for q in range(quarter):
                piece = value[:, q * LANE : (q + 1) * LANE]
                if fresh:
                    big[q, at(t), :] = piece
                else:
                    big[q, at(t), :] += piece

        norm_block(0)
        send_weights(0).wait()
        send_weights(1).wait()
        for low, high in ranges:
            weight_part(stage, (0, 1), low, high, low == 0)
        store_shares(0, 0, 0)
        begin(scatter(0, 0))
        sum_shares(0, 0)
        norm_block(1)
        for low, high in ranges:
            weight_part(stage, (2, 3), low, high, low == 0)
        store_shares(1, 0, 0)
        store_shares(2, 0, LANE)
        begin(scatter(1, 0))
        begin(scatter(2, 0))
        pl.semaphore_wait(credit, 1)

        def pass_range(p, part, low, high):
            send_grad(p, part, span(low, high)).wait_recv()
            forward_grad(p, 0, span(low, high)).start()

        for part, (low, high) in enumerate(ranges):
            pass_range(0, part, low, high)
            weight_part(glp, (0, 1), low, high, low == 0)
        store_shares(0, 1, 0)
        begin(scatter(0, 1))
        sum_shares(1, 0)
        sum_shares(2, 0)

        for b in range(2):
            give_grad(b, every).wait_recv()
        forward_grad(0, 0, every).wait_recv()
        loop(0, turns, lambda t: product(0, t, True))
        sum_shares(0, 1)
        loop(early, turns, lambda t: send_grad(2, t, at(t)).start())
        for part, (low, high) in enumerate(ranges):
            pass_range(1, part, low, high)
            weight_part(glp, (2,), low, high, low == 0)
        store_shares(1, 1, 0)
        begin(scatter(1, 1))
        forward_grad(1, 0, every).wait_recv()
        loop(0, turns, lambda t: product(1, t, False))
        end_hop(0)

        def link_copy(g):
            return pltpu.make_async_copy(
                tile_hbm.at[pl.ds(g * team, team), pl.ds(SLOT, 2 * SLOT)],
                tbuf.at[g % 3, :, pl.ds(SLOT, 2 * SLOT)],
                tsem.at[g % 3],
            )

        def slot_copy(g):
            return pltpu.make_async_copy(
                gbuf.at[g % 2],
                slot_hbm.at[pl.ds(pl.multiple_of(g * team * SLOT, SLOT), team * SLOT)],
                gsem.at[g % 2],
            )

        link_copy(0).start()
        link_copy(1).start()
        link_total[...] = jnp.zeros_like(link_total)
        place_row = lax.broadcasted_iota(i32, (SLOT, LANE), 0)

        def slot_group(g):
            @pl.when(g + 2 < groups)
            def _():
                link_copy(g + 2).start()

            link_copy(g).wait()

            @pl.when(g >= 2)
            def _():
                slot_copy(g - 2).wait()

            for member in range(team):
                slot = g * team + member
                live = place_row < cnt_ref[slot]
                scale = column_of(inv_ref, slot)
                for q in range(quarter):
                    value = big[q, pl.ds(off_ref[slot], SLOT), :].astype(bf16).astype(f32)
                    gbuf[g % 2, member * SLOT : (member + 1) * SLOT, q * LANE : (q + 1) * LANE] = (
                        jnp.where(live, value * scale, 0.0).astype(bf16)
                    )
            link = jnp.concatenate([tbuf[g % 3, member, SLOT:, :] for member in range(team)], 1)
            link_total[...] += dot(link, gbuf[g % 2])
            slot_copy(g).start()

        def slots_done(t):
            return (3 * t) // 4

        def last_turn(t):
            @pl.when(t >= 1)
            def _():
                forward_grad(2, t - 1, at(t - 1)).wait_recv()
                product(2, t - 1, False)
                loop(slots_done(t - 1), slots_done(t), slot_group)

            send_grad(2, t, at(t)).wait_recv()
            forward_grad(2, t, at(t)).start()

        for low, high in ranges:
            loop(low, high, last_turn)
            weight_part(glp, (3,), low, high, low == 0)
            if low == 5:
                sum_shares(1, 1)
        store_shares(2, 1, 0)
        begin(scatter(2, 1))
        end_hop(1)
        forward_grad(2, turns - 1, at(turns - 1)).wait_recv()
        product(2, turns - 1, False)
        loop(slots_done(turns - 1), groups, slot_group)
        hbuf[...] = link_total[...].astype(bf16)
        half = hbuf.shape[0] // 2
        returns = [
            remote(hbuf.at[:half], hback.at[:half], b_s.at[0], b_r.at[0], node_id(nodes - 1)),
            remote(hbuf.at[half:], hback.at[half:], b_s.at[1], b_r.at[1], node_id(1)),
        ]
        begin(returns)
        sum_shares(2, 1)
        slot_copy(groups - 2).wait()
        slot_copy(groups - 1).wait()
        finish(returns)
        back_ref[:half, :] = jnp.where(me == nodes - 1, 0.0, hback[:half, :].astype(f32)).astype(bf16)
        back_ref[half:, :] = jnp.where(me == 0, 0.0, hback[half:, :].astype(f32)).astype(bf16)

        send_own(0, every).wait_send()
        for b in range(2):
            give_grad(b, every).wait_send()
        for p in range(3):
            send_grad(p, 0, every).wait_send()
            forward_grad(p, 0, every).wait_send()
        for p in range(3):
            for kind in range(2):
                finish_spread(p, kind)

    anywhere = pl.BlockSpec(memory_space=pl.ANY)
    dma = pltpu.SemaphoreType.DMA
    lane_rows = (quarter, compact, LANE)
    outs = [
        jax.ShapeDtypeStruct((rows, fw), f32),
        jax.ShapeDtypeStruct((rows, fw), bf16),
        jax.ShapeDtypeStruct((2 * SLOT, fw), bf16),
        jax.ShapeDtypeStruct((nodes, 2, LANE, fw), bf16),
        jax.ShapeDtypeStruct((8, fw), f32),
        jax.ShapeDtypeStruct((slots, 3 * SLOT, SLOT), bf16),
    ]
    scratch = [
        pltpu.VMEM((compact, fw), bf16),
        pltpu.VMEM((compact, fw), bf16),
        pltpu.VMEM(lane_rows, bf16),
        pltpu.VMEM(lane_rows, bf16),
        pltpu.VMEM(lane_rows, bf16),
        pltpu.VMEM(lane_rows, bf16),
        pltpu.VMEM((quarter, padded, LANE), f32),
        pltpu.VMEM((wide, 2 * fw), f32),
        pltpu.VMEM((2, nodes, wide, LANE), bf16),
        pltpu.VMEM((4, nodes, LANE, LANE), bf16),
        pltpu.VMEM((2, nodes, wide, LANE), bf16),
        pltpu.VMEM((4, nodes, LANE, LANE), bf16),
        pltpu.VMEM((2, LANE, wide), bf16),
        pltpu.VMEM((4, LANE, LANE), bf16),
        pltpu.VMEM((LANE, wide), bf16),
        pltpu.VMEM((LANE, LANE), bf16),
        pltpu.VMEM((3, team * SLOT, fw), bf16),
        pltpu.VMEM((3, team, 3 * SLOT, SLOT), bf16),
        pltpu.VMEM((2, team * SLOT, wide), bf16),
        pltpu.VMEM((2, team * SLOT, wide), f32),
        pltpu.VMEM((2, team * SLOT, fw), bf16),
        pltpu.VMEM((4, 8, wide), f32),
        pltpu.VMEM((4, nodes, 8, wide), f32),
        pltpu.VMEM((8, wide), f32),
        pltpu.VMEM((2, 8, wide), f32),
        pltpu.VMEM((8, wide), f32),
        pltpu.VMEM((2 * SLOT, fw), f32),
        pltpu.VMEM((2 * SLOT, fw), bf16),
        pltpu.VMEM((2 * SLOT, fw), bf16),
        dma((3,)),
        dma((3,)),
        dma((2,)),
        dma((2,)),
        dma((2,)),
        dma((1,)),
        dma((turns,)),
        dma((2,)),
        dma((6,)),
        dma((3,)),
        dma((6 + turns,)),
        dma((2,)),
        dma((2,)),
        dma((3,)),
        dma((2 + turns,)),
        dma((4,)),
        dma((4,)),
        dma((6,)),
        dma((6,)),
        dma((6,)),
        dma((6,)),
        dma((4,)),
        dma((4,)),
        dma((6,)),
        pltpu.SemaphoreType.REGULAR,
        pltpu.VMEM((2 * fw, fw), bf16),
        dma((2,)),
        dma((2,)),
        pltpu.VMEM((2 * fw, fw), bf16),
        pltpu.VMEM((2 * fw, fw), bf16),
        dma((2 * quarter,)),
        dma((3,)),
        dma((3,)),
        pltpu.VMEM((2 * SLOT, fw), bf16),
        pltpu.VMEM((slots, 8, SLOT), f32),
        dma((2,)),
        dma((2,)),
        dma((2,)),
        dma((2,)),
    ]
    return pl.pallas_call(
        kernel,
        out_shape=outs,
        in_specs=[smem()] * 3 + [anywhere] * 3 + [whole()] * 5,
        out_specs=[anywhere, anywhere, whole(), anywhere, whole(), anywhere],
        scratch_shapes=scratch,
        compiler_params=pltpu.CompilerParams(
            vmem_limit_bytes=CORE_BYTES, collective_id=2, has_side_effects=True
        ),
        cost_estimate=cost(0, 0),
        name="core",
    )(*lists, features, weight, cotangent, near, links, send_row, gain, bias)


def every_row(
    features, weight, cotangent, near, links, send_list, valid_row, scale, shift, lists, nodes, chips
):
    offsets, counts = lists[:2]
    rows, fw = features.shape
    slots = rows // SLOT
    chip, core_side = lax.axis_index("mp") // 2, lax.rem(lax.axis_index("mp"), 2)
    core_word = core_side.astype(i32)[None]
    half = send_list.shape[0] // 2
    others = range(1, chips)
    wide = fw // 2

    def chip_rows(which):
        return lax.dynamic_slice_in_dim(weight, which * 2 * fw, 2 * fw, 0).astype(bf16)

    w_peer = [to_chip(chip_rows(lax.rem(chip + d, chips)), d) for d in others]
    w_chip = chip_rows(chip)
    picked = pick_rows(features, send_list[:, None], valid_row)
    halo = jnp.concatenate([node_shift(picked[:half], 1), node_shift(picked[half:], -1)], 0)
    tiles, inv = count_tiles(near, links, counts)

    def half_of(block, which):
        return lax.dynamic_slice_in_dim(block, which * fw, fw, 0)

    w_all = [w_chip] + w_peer
    got = to_sibling(jnp.concatenate([half_of(w, 1 - core_side) for w in w_all], 0))
    wb = [half_of(w, core_side) for w in w_all] + [got[i * fw : (i + 1) * fw] for i in range(chips)]
    own = aggregate(tiles, inv, features, halo, offsets, counts, 0, rows)
    sib = to_sibling(own)
    received = []
    for b in range(2):
        parts = [partial_product(own, sib, w, core_word, b, wide) for w in w_peer]
        received.append([to_chip(p, -d) for p, d in zip(parts, others, strict=True)])
    gain, bias = scale[None, :], shift[None, :]
    act, grads, totals, weight_grads = None, [], [], []
    for b in range(2):
        lin, stat = linear_stats(
            own, sib, w_chip, core_word, received[b], offsets, slots, b, wide
        )
        stats = exchange(stat, nodes)
        act, grad_pre, sums = activate(
            lin, stats, gain, bias, cotangent, offsets, counts, act, b, wide, rows, fw
        )
        sums = exchange(sums, nodes)
        grad_lin, summed = linear_grad(
            lin, grad_pre, stats, sums, gain, offsets, slots, b, wide, 1
        )
        totals.append(summed)
        mine = [grad_lin] + [to_chip(grad_lin, d) for d in others]
        grads.append(mine + [to_sibling(g) for g in mine])
        sets = []
        for g in mine:
            left = jnp.einsum("rf,rc->fc", own, g, preferred_element_type=f32)
            right = jnp.einsum("rf,rc->fc", sib, g, preferred_element_type=f32)
            sets.append(
                jnp.concatenate(
                    [
                        jnp.where(core_side == 1, right, left),
                        jnp.where(core_side == 1, left, right),
                    ],
                    0,
                )
            )
        share = scatter_sum(jnp.stack(sets), 1)
        shares = [share[0]] + [to_chip(share[d], -d) for d in others]
        full = gather_shares(jnp.stack(shares), 1)
        placed = jnp.zeros((chips,) + full.shape[1:], f32)
        for d in range(chips):
            placed = lax.dynamic_update_slice(
                placed, full[d : d + 1], (lax.rem(chip + d, chips), 0, 0)
            )
        weight_grads.append(placed.reshape(chips * 2 * fw, wide))
    grad_agg = grad_products(grads[0], wb, [0] * len(wb))
    slot_grad, halo_grad = slot_grads(grad_agg, grads[1], wb, wide, tiles, inv, offsets, counts)
    returned = jnp.concatenate(
        [node_shift(halo_grad[:half], -1), node_shift(halo_grad[half:], 1)], 0
    )
    input_grad = input_grads(slot_grad, tiles, returned, send_list[None, :], counts)
    totals = jnp.concatenate(totals, 1)
    return act, input_grad, jnp.concatenate(weight_grads, 1), totals[0], totals[1]


def local(features, weight, scale, shift, cotangent, neighbours, halo_links, valid_rows, send_rows):
    rows, fw = features.shape
    slots = rows // SLOT
    nodes, mp = lax.axis_size("node"), lax.axis_size("mp")
    chips = mp // 2

    counts = jnp.sum(valid_rows.reshape(slots, SLOT), 1).astype(i32)
    order = jnp.arange(slots + 1, dtype=i32)
    offsets = jnp.sum(jnp.where(order[None, :slots] < order[:, None], counts[None, :], 0), 1)
    compact = rows * 13 // 16 // (3 * SLOT) * (3 * SLOT)
    blocks = jnp.arange(compact // SLOT, dtype=i32) * SLOT
    first = jnp.minimum(
        jnp.sum((offsets[None, 1:] <= blocks[:, None]).astype(i32), 1), slots - 1
    ).astype(i32)
    lists = (offsets, counts, first)
    near, links = neighbours.T, halo_links.T
    send_list = jnp.concatenate([send_rows[:, 1], send_rows[:, 0]], 0)
    valid_row = valid_rows[None, :].astype(i32)

    def all_rows(*args):
        return every_row(*args, lists, nodes, chips)

    given = (features, weight, cotangent, near, links, send_list, valid_row, scale, shift)
    if not (chips == 2 and fw == 4 * LANE and 2 * fw == nodes * LANE and slots % nodes == 0):
        return all_rows(*given)
    send_row = send_list[None, :]
    *made, totals, tiles = core(
        features, weight, cotangent, near, links, send_row, scale, shift, lists, nodes, compact
    )

    def few_rows(*args):
        act, input_grad, weight_grad = last_pass(*made, tiles, send_row, counts)
        return act, input_grad, weight_grad.reshape(mp * fw, fw), totals[0], totals[1]

    return lax.cond(totals[2, 0] <= compact, few_rows, all_rows, *given)


def solution(mesh):
    in_specs = (
        P("node", "mp"),
        P(None, "mp"),
        P("mp"),
        P("mp"),
        P("node", "mp"),
        P("node", None),
        P("node", None),
        P("node"),
        P("node", None),
    )
    out_specs = (P("node", "mp"), P("node", "mp"), P(None, "mp"), P("mp"), P("mp"))
    return jax.shard_map(local, mesh=mesh, in_specs=in_specs, out_specs=out_specs, check_vma=False)
```

```python
import functools

import jax
import jax.numpy as jnp
from jax import lax
from jax.experimental import pallas as pl
from jax.experimental.pallas import tpu as pltpu
from jax.sharding import PartitionSpec as P

SLOT = 128
LANE = 128
GROUP = 12
epsilon = 1e-05
VMEM_BYTES = 56 * 1024 * 1024
CORE_BYTES = 61 * 1024 * 1024
MESH = pl.DeviceIdType.MESH
f32, bf16, i32 = jnp.float32, jnp.bfloat16, jnp.int32


def params(**extra):
    return pltpu.CompilerParams(vmem_limit_bytes=VMEM_BYTES, **extra)


def whole():
    return pl.BlockSpec(memory_space=pltpu.VMEM)


def smem():
    return pl.BlockSpec(memory_space=pltpu.SMEM)


def fixed(shape):
    return pl.BlockSpec(shape, lambda i: (0,) * len(shape), pipeline_mode=pl.Buffered(1))


def cost(flops, moved, trans=0):
    return pl.CostEstimate(flops=1, bytes_accessed=1, transcendentals=0)


def dot(a, b, ca=1, cb=0):
    return lax.dot_general(a, b, (((ca,), (cb,)), ((), ())), preferred_element_type=f32)


def after(value, *earlier):
    return lax.optimization_barrier((value,) + earlier)[0]


def chosen(rows_ref, base, count, valid):
    width = rows_ref.shape[1]
    place = lax.broadcasted_iota(i32, (count, width), 0)
    hit = (rows_ref[...] == place + base) & (place < valid)
    return jnp.where(hit, 1.0, 0.0).astype(bf16)


def pick_rows(features, send_column, valid_row):
    rows, width = features.shape
    sends = send_column.shape[0]
    steps = 3
    tile = rows // steps

    def kernel(feat_ref, send_ref, valid_ref, out_ref, total):
        step = pl.program_id(0)

        @pl.when(step == 0)
        def _():
            total[...] = jnp.zeros_like(total)

        wanted = jnp.broadcast_to(send_ref[...], (sends, LANE)) - step * tile
        place = lax.broadcasted_iota(i32, (sends, LANE), 1)
        hot = []
        for part in range(tile // LANE):
            lanes = slice(part * LANE, (part + 1) * LANE)
            hit = (wanted == place + part * LANE) & (valid_ref[:, lanes] > 0)
            hot.append(jnp.where(hit, 1.0, 0.0).astype(bf16))
        total[...] += dot(jnp.concatenate(hot, 1), feat_ref[...])

        @pl.when(step == steps - 1)
        def _():
            out_ref[...] = total[...].astype(bf16)

    return pl.pallas_call(
        kernel,
        grid=(steps,),
        out_shape=jax.ShapeDtypeStruct((sends, width), bf16),
        in_specs=[
            pl.BlockSpec((tile, width), lambda i: (i, 0)),
            fixed((sends, 1)),
            pl.BlockSpec((1, tile), lambda i: (0, i)),
        ],
        out_specs=fixed((sends, width)),
        scratch_shapes=[pltpu.VMEM((sends, width), f32)],
        compiler_params=params(),
        cost_estimate=cost(2 * rows * sends * width, 2 * rows * width),
        name="pick_rows",
    )(features, send_column, valid_row)


def count_tiles(near, links, counts):
    entries, rows = near.shape
    link_entries = links.shape[0]
    slots = rows // SLOT

    def kernel(counts_ref, near_ref, link_ref, tile_ref, inv_ref):
        step = pl.program_id(0)
        row = lax.broadcasted_iota(i32, (SLOT, SLOT), 0)
        column = lax.broadcasted_iota(i32, (SLOT, SLOT), 1)
        link_row = lax.broadcasted_iota(i32, (2 * SLOT, SLOT), 0)

        def one(part, carry):
            lanes = pl.ds(pl.multiple_of(part * SLOT, SLOT), SLOT)
            near_here, link_here = near_ref[:, lanes], link_ref[:, lanes]
            counted = jnp.zeros((SLOT, SLOT), f32)
            for entry in range(entries):
                counted += jnp.where(near_here[entry : entry + 1] == row, 1.0, 0.0)
            linked = jnp.zeros((2 * SLOT, SLOT), f32)
            for entry in range(link_entries):
                linked += jnp.where(link_here[entry : entry + 1] == link_row, 1.0, 0.0)
            degree = 1.0 + jnp.sum(counted, 0, keepdims=True) + jnp.sum(linked, 0, keepdims=True)
            tile = counted + jnp.where(row == column, counted + 2.0, 0.0)
            tile = jnp.where(row < counts_ref[step * GROUP + part], tile, 0.0)
            tile_ref[part, :SLOT, :] = tile.astype(bf16)
            tile_ref[part, SLOT:, :] = linked.astype(bf16)
            inv_ref[part] = jnp.broadcast_to(1.0 / degree, (8, SLOT))
            return carry

        lax.fori_loop(0, GROUP, one, 0)

    return pl.pallas_call(
        kernel,
        grid=(slots // GROUP,),
        out_shape=[
            jax.ShapeDtypeStruct((slots, 3 * SLOT, SLOT), bf16),
            jax.ShapeDtypeStruct((slots, 8, SLOT), f32),
        ],
        in_specs=[
            smem(),
            pl.BlockSpec((entries, GROUP * SLOT), lambda i: (0, i)),
            pl.BlockSpec((link_entries, GROUP * SLOT), lambda i: (0, i)),
        ],
        out_specs=[
            pl.BlockSpec((GROUP, 3 * SLOT, SLOT), lambda i: (i, 0, 0)),
            pl.BlockSpec((GROUP, 8, SLOT), lambda i: (i, 0, 0)),
        ],
        compiler_params=params(),
        cost_estimate=cost(rows * 12000, 6 * rows * SLOT),
        name="count_tiles",
    )(counts, near, links)


def column_of(inv_ref, slot):
    return jnp.transpose(jnp.broadcast_to(inv_ref[slot, 0:1, :], (SLOT, SLOT)))


def aggregate(tiles, inv, features, halo, offsets, counts, first, rows):
    slots = tiles.shape[0]
    width = features.shape[1]
    quarter = width // LANE
    team = 4
    low = first // SLOT // team * team
    high = min(slots, -(-(first + rows) // (SLOT // 2)))
    groups = -(-(high - low) // team)
    low = min(low, slots - groups * team)
    sub = rows // 4

    def kernel(off_ref, counts_ref, tile_hbm, inv_hbm, feat_hbm, halo_ref, out_ref, *scratch):
        held, tile_ref, inv_ref, feat_ref, sems = scratch

        def copies(group):
            here = group * team
            return [
                pltpu.make_async_copy(
                    tile_hbm.at[pl.ds(low + here, team)],
                    tile_ref.at[pl.ds(here, team)],
                    sems.at[0, group],
                ),
                pltpu.make_async_copy(
                    inv_hbm.at[pl.ds(low + here, team)],
                    inv_ref.at[pl.ds(here, team)],
                    sems.at[1, group],
                ),
                pltpu.make_async_copy(
                    feat_hbm.at[pl.ds(pl.multiple_of((low + here) * SLOT, SLOT), team * SLOT)],
                    feat_ref.at[pl.ds(pl.multiple_of(here * SLOT, SLOT), team * SLOT)],
                    sems.at[2, group],
                ),
            ]

        def begin(group, carry):
            for copy in copies(group):
                copy.start()
            return carry

        lax.fori_loop(0, groups, begin, 0)
        row = lax.broadcasted_iota(i32, (SLOT, SLOT), 0)
        column = lax.broadcasted_iota(i32, (SLOT, SLOT), 1)
        unit = jnp.where(row == column, 1.0, 0.0).astype(bf16)

        def step(group, carry):
            for copy in copies(group):
                copy.wait()

            @pl.when(off_ref[low + group * team] < first + rows)
            def _():
                for member in range(team):
                    here = group * team + member
                    tile = dot(unit, tile_ref[here], 1, 1).astype(bf16)
                    source = pl.ds(pl.multiple_of(here * SLOT, SLOT), SLOT)
                    total = dot(tile[:, :SLOT], feat_ref[source, :])
                    total += dot(tile[:, SLOT:], halo_ref[...])
                    scale = column_of(inv_ref, here)
                    start = jnp.clip(off_ref[low + here] - first + SLOT, 0, rows + SLOT)
                    for q in range(quarter):
                        held[q, pl.ds(start, SLOT), :] = (
                            total[:, q * LANE : (q + 1) * LANE] * scale
                        )

            return carry

        lax.fori_loop(0, groups, step, 0)
        total_rows = off_ref[slots] - first

        def finish(part, carry):
            begin_row = pl.multiple_of(part * sub, 16)
            live = lax.broadcasted_iota(i32, (sub, LANE), 0) + begin_row < total_rows
            for q in range(quarter):
                out_ref[pl.ds(begin_row, sub), q * LANE : (q + 1) * LANE] = jnp.where(
                    live, held[q, pl.ds(begin_row + SLOT, sub), :], 0.0
                ).astype(bf16)
            return carry

        lax.fori_loop(0, rows // sub, finish, 0)

    anywhere = pl.BlockSpec(memory_space=pl.ANY)
    return pl.pallas_call(
        kernel,
        out_shape=jax.ShapeDtypeStruct((rows, width), bf16),
        in_specs=[smem(), smem(), anywhere, anywhere, anywhere, whole()],
        out_specs=whole(),
        scratch_shapes=[
            pltpu.VMEM((quarter, rows + 2 * SLOT, LANE), f32),
            pltpu.VMEM((groups * team, 3 * SLOT, SLOT), bf16),
            pltpu.VMEM((groups * team, 8, SLOT), f32),
            pltpu.VMEM((groups * team * SLOT, width), bf16),
            pltpu.SemaphoreType.DMA((3, groups)),
        ],
        compiler_params=params(),
        cost_estimate=cost(2 * rows * 3 * SLOT * width, 4 * rows * width),
        name="aggregate",
    )(offsets, counts, tiles, inv, features, halo)


def partial_product(own, sib, weight, core, block, width):
    rows, depth = own.shape
    tile = rows // 2 if rows > 1600 else rows

    def kernel(core_ref, a_ref, b_ref, w_ref, out_ref):
        core = core_ref[0]
        first = w_ref[pl.ds(pl.multiple_of(core * depth, depth), depth), :]
        second = w_ref[pl.ds(pl.multiple_of((1 - core) * depth, depth), depth), :]
        out_ref[...] = (dot(a_ref[...], first) + dot(b_ref[...], second)).astype(bf16)

    return pl.pallas_call(
        kernel,
        grid=(rows // tile,),
        out_shape=jax.ShapeDtypeStruct((rows, width), bf16),
        in_specs=[smem()]
        + [pl.BlockSpec((tile, depth), lambda i: (i, 0))] * 2
        + [pl.BlockSpec((2 * depth, width), lambda i: (0, block))],
        out_specs=pl.BlockSpec((tile, width), lambda i: (i, 0)),
        compiler_params=params(),
        cost_estimate=cost(4 * rows * depth * width, 4 * rows * depth + 2 * rows * width),
        name="partial_product",
    )(core, own, sib, weight)


def linear_stats(own, sib, weight, core, received, offsets, slots, block, width):
    rows, depth = own.shape
    tile = rows // 2
    sub = rows // 8
    parts = width // LANE
    others = len(received)

    def kernel(off_ref, core_ref, a_ref, b_ref, w_ref, *rest):
        recv_refs, (lin_ref, stat_ref) = rest[:others], rest[others:]
        step = pl.program_id(0)
        core = core_ref[0]
        first = w_ref[pl.ds(pl.multiple_of(core * depth, depth), depth), :]
        second = w_ref[pl.ds(pl.multiple_of((1 - core) * depth, depth), depth), :]
        total = off_ref[slots]

        @pl.when(step == 0)
        def _():
            stat_ref[...] = jnp.zeros_like(stat_ref)
            stat_ref[2:3, :] = jnp.full((1, width), total.astype(f32), f32)

        for piece in range(tile // sub):
            here_rows = slice(piece * sub, (piece + 1) * sub)
            value = dot(a_ref[here_rows, :], first) + dot(b_ref[here_rows, :], second)
            for ref in recv_refs:
                value += ref[here_rows, :].astype(f32)
            for part in range(parts):
                lin_ref[part, here_rows, :] = value[:, part * LANE : (part + 1) * LANE]
            begin = step * tile + piece * sub
            before = jnp.minimum(begin, total)
            here = jnp.minimum(begin + sub, total) - before
            seen, new = before.astype(f32), here.astype(f32)
            both = jnp.full((1, width), jnp.maximum(seen + new, 1.0), f32)
            live = lax.broadcasted_iota(i32, (sub, width), 0) < here
            mean_here = jnp.sum(jnp.where(live, value, 0.0), 0, keepdims=True) / jnp.full(
                (1, width), jnp.maximum(new, 1.0), f32
            )
            centred = jnp.where(live, value - mean_here, 0.0)
            squares = jnp.sum(centred * centred, 0, keepdims=True)
            mean, held = stat_ref[0:1, :], stat_ref[1:2, :]
            gap = mean_here - mean
            ratio = new / both
            stat_ref[0:1, :] = mean + gap * ratio
            stat_ref[1:2, :] = held + squares + gap * gap * (seen * ratio)

    return pl.pallas_call(
        kernel,
        grid=(rows // tile,),
        out_shape=[
            jax.ShapeDtypeStruct((parts, rows + SLOT, LANE), f32),
            jax.ShapeDtypeStruct((8, width), f32),
        ],
        in_specs=[smem(), smem()]
        + [pl.BlockSpec((tile, depth), lambda i: (i, 0))] * 2
        + [pl.BlockSpec((2 * depth, width), lambda i: (0, block))]
        + [pl.BlockSpec((tile, width), lambda i: (i, 0))] * others,
        out_specs=[
            pl.BlockSpec((parts, tile, LANE), lambda i: (0, i, 0)),
            pl.BlockSpec((8, width), lambda i: (0, 0)),
        ],
        compiler_params=params(),
        cost_estimate=cost(4 * rows * depth * width, 4 * rows * depth + 6 * rows * width),
        name="linear_stats",
    )(offsets, core, own, sib, weight, *received)


def exchange(block, nodes, number=1):
    def kernel(in_ref, out_ref, held, send_sem, recv_sem):
        me = lax.axis_index("node")
        barrier = pltpu.get_barrier_semaphore()
        for step in range(1, nodes):
            pl.semaphore_signal(
                barrier,
                inc=1,
                device_id={"node": lax.rem(me + step, nodes)},
                device_id_type=MESH,
            )
        pl.semaphore_wait(barrier, nodes - 1)
        copies = []
        for step in range(1, nodes):
            copy = pltpu.make_async_remote_copy(
                src_ref=in_ref,
                dst_ref=held.at[step],
                send_sem=send_sem.at[step],
                recv_sem=recv_sem.at[step],
                device_id={"node": lax.rem(me + step, nodes)},
                device_id_type=MESH,
            )
            copy.start()
            copies.append(copy)
        out_ref[0] = in_ref[...]
        for copy in copies:
            copy.wait()
        for step in range(1, nodes):
            out_ref[step] = held[step]

    return pl.pallas_call(
        kernel,
        out_shape=jax.ShapeDtypeStruct((nodes,) + block.shape, f32),
        in_specs=[whole()],
        out_specs=whole(),
        scratch_shapes=[
            pltpu.VMEM((nodes,) + block.shape, f32),
            pltpu.SemaphoreType.DMA((nodes,)),
            pltpu.SemaphoreType.DMA((nodes,)),
        ],
        compiler_params=params(collective_id=number, has_side_effects=True),
        cost_estimate=cost(0, nodes * block.size * 4),
        name="exchange",
    )(block)


def merge_stats(stat_ref, width):
    nodes = stat_ref.shape[0]
    total = stat_ref[0, 2:3, :width]
    for node in range(1, nodes):
        total += stat_ref[node, 2:3, :width]
    mean = stat_ref[0, 2:3, :width] * stat_ref[0, 0:1, :width]
    for node in range(1, nodes):
        mean += stat_ref[node, 2:3, :width] * stat_ref[node, 0:1, :width]
    mean = mean / total
    spread = jnp.zeros_like(mean)
    for node in range(nodes):
        gap = stat_ref[node, 0:1, :width] - mean
        spread += stat_ref[node, 1:2, :width] + stat_ref[node, 2:3, :width] * gap * gap
    return total, mean, lax.rsqrt(spread / total + epsilon)


def activate(
    linear, stats, scale, shift, cotangent, offsets, counts, held, block, width, rows, feat_width
):
    nodes = stats.shape[0]
    slots = rows // SLOT
    parts = width // LANE
    compact = linear.shape[1]
    slope = 0.7978845608028654
    cubic = 0.044715
    half_slot = SLOT // 2

    def kernel(off_ref, counts_ref, lin_ref, stat_ref, scale_ref, shift_ref, cot_ref, *rest):
        act_ref, grad_ref, sum_ref, norm, sums = rest[-5:]
        step = pl.program_id(0)

        @pl.when(step == 0)
        def _():
            _, mean, rstd = merge_stats(stat_ref, width)
            norm[0:1, :] = mean
            norm[1:2, :] = rstd
            sums[...] = jnp.zeros_like(sums)

        place = lax.broadcasted_iota(i32, (half_slot, LANE), 0)

        def one(member, carry):
            slot = step * GROUP + member
            start = off_ref[slot]
            for side in range(2):
                live = place < counts_ref[slot] - side * half_slot
                here = pl.ds(pl.multiple_of(member * SLOT + side * half_slot, 16), half_slot)
                from_row = pl.ds(start + side * half_slot, half_slot)
                for part in range(parts):
                    lanes = slice(part * LANE, (part + 1) * LANE)
                    mean, rstd = norm[0:1, lanes], norm[1:2, lanes]
                    value = jnp.where(live, lin_ref[part, from_row, :], 0.0)
                    normed = (value - mean) * rstd
                    z = scale_ref[:, lanes] * normed + shift_ref[:, lanes]
                    square = z * z
                    bent = jnp.tanh(z * (slope + (slope * cubic) * square))
                    half = 0.5 + 0.5 * bent
                    act_ref[here, lanes] = jnp.where(live, z * half, 0.0)
                    back = half + z * (1.0 - bent * bent) * (
                        0.5 * slope + (1.5 * slope * cubic) * square
                    )
                    grad = jnp.where(live, cot_ref[here, lanes].astype(f32) * back, 0.0)
                    grad_ref[part, from_row, :] = grad
                    tall = (half_slot // 8, 8, LANE)
                    sums[0, :, lanes] += jnp.sum((grad * normed).reshape(tall), 0)
                    sums[1, :, lanes] += jnp.sum(grad.reshape(tall), 0)
            return carry

        lax.fori_loop(0, GROUP, one, 0)

        @pl.when(step == slots // GROUP - 1)
        def _():
            sum_ref[...] = jnp.zeros_like(sum_ref)
            sum_ref[0:1, :] = jnp.sum(sums[0], 0, keepdims=True)
            sum_ref[1:2, :] = jnp.sum(sums[1], 0, keepdims=True)

    given = [] if held is None else [held]
    return pl.pallas_call(
        kernel,
        grid=(slots // GROUP,),
        out_shape=[
            jax.ShapeDtypeStruct((rows, feat_width), f32),
            jax.ShapeDtypeStruct((parts, compact, LANE), f32),
            jax.ShapeDtypeStruct((8, width), f32),
        ],
        in_specs=[
            smem(),
            smem(),
            fixed((parts, compact, LANE)),
            fixed(stats.shape),
            pl.BlockSpec((1, width), lambda i: (0, block)),
            pl.BlockSpec((1, width), lambda i: (0, block)),
            pl.BlockSpec((GROUP * SLOT, width), lambda i: (i, block)),
        ]
        + [pl.BlockSpec(memory_space=pl.ANY)] * len(given),
        out_specs=[
            pl.BlockSpec((GROUP * SLOT, width), lambda i: (i, block)),
            fixed((parts, compact, LANE)),
            fixed((8, width)),
        ],
        scratch_shapes=[pltpu.VMEM((8, width), f32), pltpu.VMEM((2, 8, width), f32)],
        input_output_aliases={7: 0} if given else {},
        compiler_params=params(),
        cost_estimate=cost(60 * rows * width, 14 * rows * width, rows * width),
        name="activate",
    )(offsets, counts, linear, stats, scale, shift, cotangent, *given)


def linear_grad(linear, grad, stats, sums, scale, offsets, slots, block, width, pieces):
    parts, padded, _ = linear.shape
    rows = padded - SLOT
    tile = rows // 2
    sub = rows // 16
    nodes = stats.shape[0]
    share = width // pieces

    def kernel(off_ref, lin_ref, grad_ref, stat_ref, sums_ref, scale_ref, *rest):
        out_refs, (total_ref, norm) = rest[:pieces], rest[pieces:]
        step = pl.program_id(0)

        @pl.when(step == 0)
        def _():
            total, mean, rstd = merge_stats(stat_ref, width)
            by_gain = sums_ref[0, 0:1, :width]
            by_bias = sums_ref[0, 1:2, :width]
            for node in range(1, nodes):
                by_gain += sums_ref[node, 0:1, :width]
                by_bias += sums_ref[node, 1:2, :width]
            norm[0:1, :] = mean
            norm[1:2, :] = rstd
            norm[2:3, :] = by_gain / total
            norm[3:4, :] = by_bias / total
            norm[4:5, :] = rstd * scale_ref[...]
            total_ref[...] = jnp.zeros_like(total_ref)
            total_ref[0:1, :] = by_gain
            total_ref[1:2, :] = by_bias

        def one(piece, carry):
            begin = pl.multiple_of(piece * sub, 16)
            here = pl.ds(begin, sub)
            live = (
                lax.broadcasted_iota(i32, (sub, LANE), 0) + (step * tile + begin) < off_ref[slots]
            )
            for part in range(parts):
                lanes = slice(part * LANE, (part + 1) * LANE)
                normed = (lin_ref[part, here, :] - norm[0:1, lanes]) * norm[1:2, lanes]
                value = norm[4:5, lanes] * (
                    grad_ref[part, here, :] - norm[3:4, lanes] - normed * norm[2:3, lanes]
                )
                into, at = divmod(part * LANE, share)
                out_refs[into][here, at : at + LANE] = jnp.where(live, value, 0.0).astype(bf16)
            return carry

        lax.fori_loop(0, tile // sub, one, 0)

    return pl.pallas_call(
        kernel,
        grid=(rows // tile,),
        out_shape=[jax.ShapeDtypeStruct((rows, share), bf16)] * pieces
        + [jax.ShapeDtypeStruct((8, width), f32)],
        in_specs=[
            smem(),
            pl.BlockSpec((parts, tile, LANE), lambda i: (0, i, 0)),
            pl.BlockSpec((parts, tile, LANE), lambda i: (0, i, 0)),
            fixed(stats.shape),
            fixed(sums.shape),
            pl.BlockSpec((1, width), lambda i: (0, block)),
        ],
        out_specs=[pl.BlockSpec((tile, share), lambda i: (i, 0))] * pieces
        + [pl.BlockSpec((8, width), lambda i: (0, 0))],
        scratch_shapes=[pltpu.VMEM((8, width), f32)],
        compiler_params=params(),
        cost_estimate=cost(10 * rows * width, 10 * rows * width),
        name="linear_grad",
    )(offsets, linear, grad, stats, sums, scale)


def grad_products(grads, weights, places):
    rows = grads[0].shape[0]
    feat_width = weights[0].shape[0]
    parts = feat_width // LANE
    tile = rows // 4
    sub = tile // 2
    count = len(grads)
    depth = sum(g.shape[1] for g in grads)

    def kernel(*refs):
        out_ref = refs[-1]
        right = jnp.concatenate([ref[...] for ref in refs[count : 2 * count]], 1)
        for piece in range(tile // sub):
            here = slice(piece * sub, (piece + 1) * sub)
            left = jnp.concatenate([ref[here, :] for ref in refs[:count]], 1)
            value = dot(left, right, 1, 1)
            for part in range(parts):
                out_ref[part, here, :] = value[:, part * LANE : (part + 1) * LANE]

    def column(place, width):
        return pl.BlockSpec((feat_width, width), lambda i: (0, place))

    return pl.pallas_call(
        kernel,
        grid=(rows // tile,),
        out_shape=jax.ShapeDtypeStruct((parts, rows, LANE), f32),
        in_specs=[pl.BlockSpec((tile, g.shape[1]), lambda i: (i, 0)) for g in grads]
        + [column(p // g.shape[1], g.shape[1]) for p, g in zip(places, grads, strict=True)],
        out_specs=pl.BlockSpec((parts, tile, LANE), lambda i: (0, i, 0)),
        compiler_params=params(),
        cost_estimate=cost(2 * rows * feat_width * depth, rows * (4 * feat_width + 2 * depth)),
        name="grad_products",
    )(*grads, *weights)


def slot_grads(held, grads, weights, place, tiles, inv, offsets, counts):
    slots = tiles.shape[0]
    parts, rows, _ = held.shape
    width = parts * LANE
    count = len(grads)
    share = grads[0].shape[1]
    blocks = 8
    sub = rows // blocks
    team = 4

    def kernel(off_ref, counts_ref, held_ref, *refs):
        grad_refs, weight_refs = refs[:count], refs[count : 2 * count]
        tile_ref, inv_ref, out_ref, halo_ref, total, link_total, sems = refs[2 * count :]

        def copy(block):
            here = pl.ds(pl.multiple_of(block * sub, 16), sub)
            return pltpu.make_async_copy(
                held_ref.at[:, here, :], total.at[:, here, :], sems.at[block]
            )

        for block in range(blocks):
            copy(block).start()
        right = jnp.concatenate([ref[...] for ref in weight_refs], 1)
        link_total[...] = jnp.zeros_like(link_total)

        def add(block, carry):
            here = pl.ds(pl.multiple_of(block * sub, 16), sub)
            value = dot(jnp.concatenate([ref[here, :] for ref in grad_refs], 1), right, 1, 1)
            copy(block).wait()
            for part in range(parts):
                total[part, here, :] += value[:, part * LANE : (part + 1) * LANE]
            return carry

        lax.fori_loop(0, blocks, add, 0)
        place_row = lax.broadcasted_iota(i32, (SLOT, LANE), 0)

        def one(step, carry):
            pieces = []
            for member in range(team):
                slot = step * team + member
                start = off_ref[slot]
                live = place_row < counts_ref[slot]
                scale = column_of(inv_ref, slot)
                row = []
                for part in range(parts):
                    value = total[part, pl.ds(start, SLOT), :].astype(bf16).astype(f32)
                    row.append(jnp.where(live, value * scale, 0.0).astype(bf16))
                piece = jnp.concatenate(row, 1)
                out_ref[pl.ds(pl.multiple_of(slot * SLOT, SLOT), SLOT), :] = piece
                pieces.append(piece)
            link = jnp.concatenate(
                [tile_ref[step * team + member, SLOT:, :] for member in range(team)], 1
            )
            link_total[...] += dot(link, jnp.concatenate(pieces, 0))
            return carry

        lax.fori_loop(0, slots // team, one, 0)
        halo_ref[...] = link_total[...].astype(bf16)

    return pl.pallas_call(
        kernel,
        grid=(1,),
        out_shape=[
            jax.ShapeDtypeStruct((slots * SLOT, width), bf16),
            jax.ShapeDtypeStruct((2 * SLOT, width), bf16),
        ],
        in_specs=[smem(), smem(), pl.BlockSpec(memory_space=pl.ANY)]
        + [fixed((rows, share))] * count
        + [
            pl.BlockSpec(
                (width, share), lambda i: (0, place // share), pipeline_mode=pl.Buffered(1)
            )
        ]
        * count
        + [fixed(tiles.shape), fixed(inv.shape)],
        out_specs=[fixed((slots * SLOT, width)), fixed((2 * SLOT, width))],
        scratch_shapes=[
            pltpu.VMEM((parts, rows + SLOT, LANE), f32),
            pltpu.VMEM((2 * SLOT, width), f32),
            pltpu.SemaphoreType.DMA((blocks,)),
        ],
        compiler_params=params(),
        cost_estimate=cost(4 * slots * SLOT * SLOT * width, 6 * slots * SLOT * width),
        name="slot_grads",
    )(offsets, counts, held, *grads, *weights, tiles, inv)


def input_grads(slot_grad, tiles, returned, send_row, counts):
    rows, width = slot_grad.shape
    sends = send_row.shape[1]

    def kernel(counts_ref, grad_ref, tile_ref, back_ref, send_ref, out_ref):
        step = pl.program_id(0)

        def pair(turn, carry):
            for side in range(2):
                member = turn * 2 + side
                slot = step * GROUP + member
                here = pl.ds(pl.multiple_of(member * SLOT, SLOT), SLOT)
                hot = chosen(send_ref, slot * SLOT, SLOT, counts_ref[slot])
                value = dot(tile_ref[member], grad_ref[here, :])
                out_ref[here, :] = value + dot(hot, back_ref[...])
            return carry

        lax.fori_loop(0, GROUP // 2, pair, 0)

    return pl.pallas_call(
        kernel,
        grid=(rows // (GROUP * SLOT),),
        out_shape=jax.ShapeDtypeStruct((rows, width), f32),
        in_specs=[
            smem(),
            pl.BlockSpec((GROUP * SLOT, width), lambda i: (i, 0)),
            pl.BlockSpec((GROUP, SLOT, SLOT), lambda i: (i, 0, 0)),
            fixed((sends, width)),
            fixed((1, sends)),
        ],
        out_specs=pl.BlockSpec((GROUP * SLOT, width), lambda i: (i, 0)),
        compiler_params=params(),
        cost_estimate=cost(2 * rows * 3 * SLOT * width, 6 * rows * width),
        name="input_grads",
    )(counts, slot_grad, tiles, returned, send_row)


def last_pass(act, slot_grad, returned, shares, tiles, send_pairs, counts):
    rows, width = slot_grad.shape
    sends = 2 * send_pairs.shape[1]
    nodes = shares.shape[0]
    group = rows // SLOT // nodes

    def kernel(counts_ref, act_ref, grad_ref, tile_ref, back_ref, send_ref, share_ref, *outs):
        act_out, grad_out, weight_out = outs
        step = pl.program_id(0)
        wanted = jnp.concatenate([send_ref[1:2, :], send_ref[0:1, :]], 1)
        act_out[...] = act_ref[...]
        weight_out[...] = share_ref[...].astype(f32).reshape(weight_out.shape)

        def pair(turn, carry):
            for side in range(2):
                member = turn * 2 + side
                slot = step * group + member
                here = pl.ds(pl.multiple_of(member * SLOT, SLOT), SLOT)
                hot = chosen(wanted, slot * SLOT, SLOT, counts_ref[slot])
                value = dot(tile_ref[member], grad_ref[here, :])
                grad_out[here, :] = value + dot(hot, back_ref[...])
            return carry

        lax.fori_loop(0, group // 2, pair, 0)

    return pl.pallas_call(
        kernel,
        grid=(nodes,),
        out_shape=[
            jax.ShapeDtypeStruct((rows, width), f32),
            jax.ShapeDtypeStruct((rows, width), f32),
            jax.ShapeDtypeStruct((2, nodes, LANE, width), f32),
        ],
        in_specs=[
            smem(),
            pl.BlockSpec((group * SLOT, width), lambda i: (i, 0)),
            pl.BlockSpec((group * SLOT, width), lambda i: (i, 0)),
            pl.BlockSpec((group, SLOT, SLOT), lambda i: (i, 0, 0)),
            fixed((sends, width)),
            fixed(send_pairs.shape),
            pl.BlockSpec((1, 2, LANE, width), lambda i: (i, 0, 0, 0)),
        ],
        out_specs=[
            pl.BlockSpec((group * SLOT, width), lambda i: (i, 0)),
            pl.BlockSpec((group * SLOT, width), lambda i: (i, 0)),
            pl.BlockSpec((2, 1, LANE, width), lambda i: (0, i, 0, 0)),
        ],
        compiler_params=params(),
        cost_estimate=cost(0, 0),
        name="last_pass",
    )(counts, act, slot_grad, tiles, returned, send_pairs, shares)


def node_shift(block, distance):
    nodes = range(lax.axis_size("node"))
    return lax.ppermute(
        block, "node", [(i - distance, i) for i in nodes if i - distance in nodes]
    )


def to_sibling(block):
    return lax.ppermute(block, "mp", [(i, i ^ 1) for i in range(lax.axis_size("mp"))])


def to_chip(block, distance):
    size = lax.axis_size("mp")
    return lax.ppermute(block, "mp", [(i, (i + 2 * distance) % size) for i in range(size)])


def node_flip(block, bit):
    return lax.ppermute(block, "node", [(i, i ^ bit) for i in range(lax.axis_size("node"))])


def scatter_sum(value, axis):
    me, bit = lax.axis_index("node"), 1
    while bit < lax.axis_size("node"):
        mine = lax.rem(me // bit, 2)
        half = value.shape[axis] // 2
        keep = lax.dynamic_slice_in_dim(value, mine * half, half, axis)
        give = lax.dynamic_slice_in_dim(value, (1 - mine) * half, half, axis)
        value = keep + node_flip(give, bit)
        bit *= 2
    return value


def gather_shares(value, axis):
    me, bit = lax.axis_index("node"), lax.axis_size("node") // 2
    while bit >= 1:
        mine = lax.rem(me // bit, 2)
        other = node_flip(value, bit)
        low = jnp.where(mine == 0, value, other)
        high = jnp.where(mine == 0, other, value)
        value = jnp.concatenate([low, high], axis)
        bit //= 2
    return value


def core(
    features, weight, cotangent, near, links, send_pairs, scale, shift, lists, nodes, compact
):
    rows, fw = features.shape
    entries, link_entries = near.shape[0], links.shape[0]
    gain, bias = (v.reshape(fw // LANE, 1, LANE) for v in (scale, shift))
    slots = rows // SLOT
    quarter = fw // LANE
    tile = 3 * SLOT
    turns = compact // tile
    padded = rows + 2 * SLOT
    wide = fw // 2
    team = 4
    groups = slots // team
    ranges = [(0, 5), (5, 10), (10, turns)]
    early = 2
    slope, cubic = 0.7978845608028654, 0.044715
    sizes = {0: 2, 1: 1, 2: 1}
    firsts = {0: 0, 1: 2, 2: 3}

    def kernel(*refs):
        off_ref, cnt_ref, first_ref, feat_hbm, w_hbm, cot_hbm = refs[:6]
        near_ref, link_ref, send_ref, gain_ref, bias_ref = refs[6:11]
        act_hbm, slot_hbm, back_ref, wag_hbm, tot_ref, tile_hbm = refs[11:17]
        own, sib, stage, recv, glp, gls, big, wacc = refs[17:25]
        stg_a, stg_b, rs_a, rs_b, ag_a, ag_b, hop_a, hop_b = refs[25:33]
        fbuf, tbuf, cbuf, abuf, gbuf, sbuf, ebuf, st, sums, norm, link_total, hbuf, hback = refs[33:46]
        fsem, tsem, csem, asem, gsem = refs[46:51]
        d1s, d1r, x1s, x1r, x2s, x2r, d2s, d2r, f2s, f2r = refs[51:61]
        e_s, e_r, r_s, r_r, a_s, a_r, b_s, b_r, lsem, credit = refs[61:71]
        ws_ref, w_s, w_r, wc_ref, wp_ref, wsem, v_s, v_r, halo_ref, inv_ref = refs[71:81]
        u_s, u_r, h_s, h_r = refs[81:85]

        me = lax.axis_index("node")
        place = lax.axis_index("mp")
        chip, side = place // 2, place % 2
        peer_id = {"mp": (1 - chip) * 2 + side}
        sib_id = {"mp": chip * 2 + 1 - side}
        total = off_ref[slots]

        def node_id(step):
            return {"node": (me + step) % nodes}

        def across_id(step):
            return {"node": (me + step) % nodes, "mp": (1 - chip) * 2 + side}

        def weight_copy(mine, q):
            chosen_rows = chip if mine else 1 - chip
            return pltpu.make_async_copy(
                w_hbm.at[
                    pl.ds(pl.multiple_of(chosen_rows * 2 * fw, SLOT), 2 * fw),
                    pl.ds(q * LANE, LANE),
                ],
                big.at[q, pl.ds(mine * 2 * fw, 2 * fw)],
                wsem.at[mine * quarter + q],
            )

        for mine in range(2):
            for q in range(quarter):
                weight_copy(mine, q).start()
        barrier = pltpu.get_barrier_semaphore()
        targets = [sib_id] + [node_id(step) for step in range(1, nodes)]
        for target in targets + [across_id(step) for step in range(nodes)]:
            pl.semaphore_signal(barrier, inc=1, device_id=target, device_id_type=MESH)

        def remote(src, dst, send, arrive, target):
            return pltpu.make_async_remote_copy(
                src_ref=src,
                dst_ref=dst,
                send_sem=send,
                recv_sem=arrive,
                device_id=target,
                device_id_type=MESH,
            )

        def at(turn):
            return pl.ds(pl.multiple_of(turn * tile, SLOT), tile)

        def own_half(ref, columns):
            return ref[pl.ds(pl.multiple_of(side * fw, SLOT), fw), columns]

        def sib_half(ref, columns):
            return ref[pl.ds(pl.multiple_of((1 - side) * fw, SLOT), fw), columns]

        def loop(low, high, body):
            def step(index, carry):
                body(index)
                return carry

            lax.fori_loop(low, high, step, 0)

        def span(low, high):
            return pl.ds(pl.multiple_of(low * tile, SLOT), (high - low) * tile)

        every = span(0, turns)

        def send_own(t, rows_of=None):
            here = at(t) if rows_of is None else rows_of
            return remote(
                own.at[here], sib.at[here], d1s.at[0], d1r.at[0 if rows_of else t], sib_id
            )

        def send_partial(b, part, here):
            two = pl.ds(2 * b, 2)
            return remote(
                stage.at[two, here], recv.at[two, here], x1s.at[b], x1r.at[3 * b + part], peer_id
            )

        def send_grad(p, part, here):
            some = pl.ds(firsts[p], sizes[p])
            return remote(
                stage.at[some, here], glp.at[some, here], x2s.at[p], x2r.at[3 * p + part], peer_id
            )

        def give_grad(b, here):
            two = pl.ds(2 * b, 2)
            return remote(stage.at[two, here], gls.at[two, here], d2s.at[b], d2r.at[b], sib_id)

        def forward_grad(p, part, here):
            some = pl.ds(firsts[p], sizes[p])
            return remote(
                glp.at[some, here], recv.at[some, here], f2s.at[p], f2r.at[p + part], sib_id
            )

        def picked_rows(block):
            slot = first_ref[block]
            base = block * SLOT
            starts = []
            for step in range(3):
                here = jnp.minimum(slot + step, slots - 1)
                starts.append(
                    jnp.clip(here * SLOT + base - off_ref[here] + SLOT, 0, padded - SLOT)
                )
            place_row = lax.broadcasted_iota(i32, (SLOT, LANE), 0)
            one = place_row < off_ref[jnp.minimum(slot + 1, slots)] - base
            two = place_row < off_ref[jnp.minimum(slot + 2, slots)] - base
            live = place_row < total - base

            def pick(q):
                value = jnp.where(two, big[q, pl.ds(starts[1], SLOT), :], big[q, pl.ds(starts[2], SLOT), :])
                value = jnp.where(one, big[q, pl.ds(starts[0], SLOT), :], value)
                return jnp.where(live, value, 0.0)

            return pick

        def send_weights(which):
            src = wp_ref if which else wc_ref
            return remote(
                src.at[pl.ds(pl.multiple_of((1 - side) * fw, SLOT), fw)],
                ws_ref.at[pl.ds(which * fw, fw)],
                w_s.at[which],
                w_r.at[which],
                sib_id,
            )

        first_half, second_half = slice(0, wide), slice(wide, fw)

        def send_upper_weights():
            columns = pl.ds(0, wide)
            return remote(
                gbuf.at[0, :, columns], wp_ref.at[pl.ds(0, fw), columns], v_s.at[2], v_r.at[2], peer_id
            )

        per_half = nodes // 2

        def share_of_weights(which):
            if which == 0:
                start = pl.multiple_of(me * (LANE // 2), LANE // 2)
                source = gbuf.at[1, pl.ds(start, LANE // 2), pl.ds(0, wide)]
                return source, wp_ref.at[pl.ds(fw + start, LANE // 2), pl.ds(0, wide)]
            start = pl.multiple_of((me % per_half) * LANE, LANE)
            source = gbuf.at[me // per_half, pl.ds(start, LANE), pl.ds(wide, wide)]
            into = pl.ds(pl.multiple_of(me * LANE, LANE), LANE)
            return source, wp_ref.at[into, pl.ds(wide, wide)]

        def send_weight_share(which):
            source, into = share_of_weights(which)
            return remote(source, into, v_s.at[which], v_r.at[which], peer_id)

        def spread_weights(which):
            _, into = share_of_weights(which)
            for step in range(1, nodes):
                remote(into, into, u_s.at[which], u_r.at[which], node_id(step)).start()

        def spread_weights_end(which):
            count = (nodes - 1) * (LANE // 2 if which == 0 else LANE)
            some = wp_ref.at[pl.ds(0, count), pl.ds(which * wide, wide)]
            return remote(some, some, u_s.at[which], u_r.at[which], node_id(1))

        def loads(g):
            return pltpu.make_async_copy(
                feat_hbm.at[pl.ds(pl.multiple_of(g * team * SLOT, SLOT), team * SLOT)],
                fbuf.at[g % 3],
                fsem.at[g % 3],
            )

        for g in range(3):
            loads(g).start()
        for q in range(quarter):
            lanes = slice(q * LANE, (q + 1) * LANE)
            weight_copy(0, q).wait()
            for number in range(2):
                gbuf[number, :, lanes] = big[q, number * fw : (number + 1) * fw, :].astype(bf16)
        wanted = [
            jnp.transpose(
                jnp.broadcast_to(
                    send_ref[1 - part : 2 - part, :].astype(f32), (LANE, LANE)
                )
            )
            for part in range(2)
        ]
        wanted = jnp.concatenate(wanted, 0).astype(i32)
        lane = lax.broadcasted_iota(i32, (2 * SLOT, LANE), 1)
        link_total[...] = jnp.zeros_like(link_total)

        def pick_group(g):
            loads(g).wait()
            hot = []
            for member in range(team):
                slot = g * team + member
                hit = (wanted == lane + slot * SLOT) & (lane < cnt_ref[slot])
                hot.append(jnp.where(hit, 1.0, 0.0).astype(bf16))
            link_total[...] += dot(jnp.concatenate(hot, 1), fbuf[g % 3])

            @pl.when(g + 3 < groups)
            def _():
                loads(g + 3).start()

        loop(0, groups, pick_group)
        hbuf[...] = link_total[...].astype(bf16)
        half_rows = SLOT
        halo_in = [
            remote(
                hbuf.at[:half_rows], halo_ref.at[:half_rows], b_s.at[2], b_r.at[2], node_id(1)
            ),
            remote(
                hbuf.at[half_rows:],
                halo_ref.at[half_rows:],
                b_s.at[3],
                b_r.at[3],
                node_id(nodes - 1),
            ),
        ]
        pl.semaphore_wait(barrier, 2 * nodes)
        send_weight_share(0).start()
        send_upper_weights().start()
        send_weight_share(1).start()
        for copy in halo_in:
            copy.start()
        for q in range(quarter):
            weight_copy(1, q).wait()
            wc_ref[:, q * LANE : (q + 1) * LANE] = big[q, 2 * fw : 4 * fw, :].astype(bf16)
        for g in range(2):
            loads(g).start()

        row = lax.broadcasted_iota(i32, (SLOT, SLOT), 0)
        column = lax.broadcasted_iota(i32, (SLOT, SLOT), 1)
        link_row = lax.broadcasted_iota(i32, (2 * SLOT, SLOT), 0)
        unit = jnp.where(row == column, 1.0, 0.0).astype(bf16)

        def tile_copy(g):
            return pltpu.make_async_copy(
                tbuf.at[g % 3], tile_hbm.at[pl.ds(g * team, team)], tsem.at[g % 3]
            )

        def count_group(g):
            spot = g % 3

            def one(member):
                slot = g * team + member
                lanes = pl.ds(pl.multiple_of(slot * SLOT, SLOT), SLOT)
                near_here, link_here = near_ref[:, lanes], link_ref[:, lanes]
                counted = jnp.zeros((SLOT, SLOT), f32)
                for entry in range(entries):
                    counted += jnp.where(near_here[entry : entry + 1] == row, 1.0, 0.0)
                linked = jnp.zeros((2 * SLOT, SLOT), f32)
                for entry in range(link_entries):
                    linked += jnp.where(link_here[entry : entry + 1] == link_row, 1.0, 0.0)
                degree = (
                    1.0 + jnp.sum(counted, 0, keepdims=True) + jnp.sum(linked, 0, keepdims=True)
                )
                matrix = counted + jnp.where(row == column, counted + 2.0, 0.0)
                matrix = jnp.where(row < cnt_ref[slot], matrix, 0.0)
                tbuf[spot, member, :SLOT, :] = matrix.astype(bf16)
                tbuf[spot, member, SLOT:, :] = linked.astype(bf16)
                inv_ref[slot] = jnp.broadcast_to(1.0 / degree, (8, SLOT))

            loop(0, team, one)
            tile_copy(g).start()

        send_weight_share(0).wait_recv()
        spread_weights(0)
        count_group(0)
        count_group(1)
        for copy in halo_in:
            copy.wait()
        halo_ref[:half_rows, :] = jnp.where(
            me == 0, 0.0, halo_ref[:half_rows, :].astype(f32)
        ).astype(bf16)
        halo_ref[half_rows:, :] = jnp.where(
            me == nodes - 1, 0.0, halo_ref[half_rows:, :].astype(f32)
        ).astype(bf16)

        def partial(b, t):
            part = jnp.where(t < ranges[0][1], 0, jnp.where(t < ranges[1][1], 1, 2))
            columns = second_half if b else first_half
            value = dot(own[at(t), :], own_half(wp_ref, columns))
            value += dot(sib[at(t), :], sib_half(wp_ref, columns))
            for q in range(2):
                stage[2 * b + q, at(t), :] = value[:, q * LANE : (q + 1) * LANE].astype(bf16)
            send_partial(b, part, at(t)).start()

        def first_partial(t):
            send_own(t).wait_recv()
            partial(0, t)

        def compact_tile(t):
            for step in range(3):
                block = t * 3 + step
                pick = picked_rows(block)
                into = pl.ds(pl.multiple_of(block * SLOT, SLOT), SLOT)
                for q in range(quarter):
                    own[into, q * LANE : (q + 1) * LANE] = pick(q).astype(bf16)
            send_own(t).start()

            @pl.when(t > done_before[0])
            def _():
                first_partial(t - 1)

        done_before = [0]

        def ready(g):
            return jnp.where(g == groups - 1, turns, jnp.minimum((team * (g + 1)) // 6, turns))

        def gather_group(g):
            @pl.when(g + 2 < groups)
            def _():
                loads(g + 2).start()

                @pl.when(g >= 1)
                def _():
                    tile_copy(g - 1).wait()

                count_group(g + 2)

            done = jnp.where(g == 0, 0, jnp.minimum((team * g) // 6, turns))
            earlier = jnp.where(g <= 1, 0, jnp.minimum((team * (g - 1)) // 6, turns))

            @pl.when(g == 2)
            def _():
                send_weight_share(1).wait_recv()
                spread_weights(1)
                send_upper_weights().wait_recv()
                spread_weights_end(0).wait_recv()

            @pl.when(done > earlier)
            def _():
                first_partial(done - 1)

            loads(g).wait()
            spot = g % 3
            for member in range(team):
                slot = g * team + member
                matrix = dot(unit, tbuf[spot, member], 1, 1).astype(bf16)
                value = dot(matrix[:, :SLOT], fbuf[spot, member * SLOT : (member + 1) * SLOT, :])
                value += dot(matrix[:, SLOT:], halo_ref[...])
                scale = column_of(inv_ref, slot)
                into = pl.ds(pl.multiple_of((slot + 1) * SLOT, SLOT), SLOT)
                for q in range(quarter):
                    big[q, into, :] = value[:, q * LANE : (q + 1) * LANE] * scale
            done_before[0] = done
            loop(done, ready(g), compact_tile)

        loop(0, groups, gather_group)
        first_partial(turns - 1)
        spread_weights_end(1).wait_recv()
        loop(0, turns, lambda t: partial(1, t))
        send_weights(0).start()
        send_weights(1).start()
        send_upper_weights().wait_send()
        for which in range(2):
            send_weight_share(which).wait_send()
            spread_weights_end(which).wait_send()
        for g in range(groups - 3, groups):
            tile_copy(g).wait()

        def exchange_block(number):
            for step in range(1, nodes):
                remote(
                    sbuf.at[number],
                    ebuf.at[number, step],
                    e_s.at[number],
                    e_r.at[number],
                    node_id(step),
                ).start()
            ebuf[number, 0] = sbuf[number]
            others = ebuf.at[number, pl.ds(1, nodes - 1)]
            remote(others, others, e_s.at[number], e_r.at[number], node_id(1)).wait()

        def row_of(number, line):
            return [ebuf[number, node, line : line + 1, :] for node in range(nodes)]

        def norm_block(b):
            columns = second_half if b else first_half
            st[...] = jnp.zeros_like(st)

            def linear_tile(t):
                value = dot(own[at(t), :], own_half(wc_ref, columns))
                value += dot(sib[at(t), :], sib_half(wc_ref, columns))
                begin = t * tile
                before = jnp.minimum(begin, total)
                here = jnp.minimum(begin + tile, total) - before
                seen, new = before.astype(f32), here.astype(f32)
                for part in range(2):
                    lanes = slice(part * LANE, (part + 1) * LANE)
                    piece = value[:, lanes] + recv[2 * b + part, at(t), :].astype(f32)
                    big[part, at(t), :] = piece
                    both = jnp.full((1, LANE), jnp.maximum(seen + new, 1.0), f32)
                    live = lax.broadcasted_iota(i32, (tile, LANE), 0) < here
                    mean_here = jnp.sum(jnp.where(live, piece, 0.0), 0, keepdims=True) / jnp.full(
                        (1, LANE), jnp.maximum(new, 1.0), f32
                    )
                    centred = jnp.where(live, piece - mean_here, 0.0)
                    squares = jnp.sum(centred * centred, 0, keepdims=True)
                    mean, held = st[0:1, lanes], st[1:2, lanes]
                    gap = mean_here - mean
                    ratio = new / both
                    st[0:1, lanes] = mean + gap * ratio
                    st[1:2, lanes] = held + squares + gap * gap * (seen * ratio)

            for part, (low, high) in enumerate(ranges):
                send_partial(b, part, span(low, high)).wait_recv()
                loop(low, high, linear_tile)
            if b == 1:
                pl.semaphore_signal(credit, inc=1, device_id=sib_id, device_id_type=MESH)
            st[2:3, :] = jnp.full((1, wide), total.astype(f32), f32)
            sbuf[2 * b] = st[...]

            def cot_copy(g):
                return pltpu.make_async_copy(
                    cot_hbm.at[
                        pl.ds(pl.multiple_of(g * team * SLOT, SLOT), team * SLOT),
                        pl.ds(b * wide, wide),
                    ],
                    cbuf.at[g % 2],
                    csem.at[g % 2],
                )

            def act_copy(g):
                return pltpu.make_async_copy(
                    abuf.at[g % 2],
                    act_hbm.at[
                        pl.ds(pl.multiple_of(g * team * SLOT, SLOT), team * SLOT),
                        pl.ds(b * wide, wide),
                    ],
                    asem.at[g % 2],
                )

            cot_copy(0).start()
            exchange_block(2 * b)
            numbers, means, squares = (row_of(2 * b, line) for line in (2, 0, 1))
            count = sum(numbers[1:], numbers[0])
            mean = sum([n * m for n, m in zip(numbers, means, strict=True)][1:], numbers[0] * means[0])
            mean = mean / count
            spread = jnp.zeros_like(mean)
            for n, m, s in zip(numbers, means, squares, strict=True):
                spread += s + n * (m - mean) * (m - mean)
            norm[0:1, :] = mean
            norm[1:2, :] = lax.rsqrt(spread / count + epsilon)
            sums[...] = jnp.zeros_like(sums)
            half_slot = SLOT // 2
            place_row = lax.broadcasted_iota(i32, (half_slot, LANE), 0)

            def act_group(g):
                @pl.when(g + 1 < groups)
                def _():
                    cot_copy(g + 1).start()

                cot_copy(g).wait()

                @pl.when(g >= 2)
                def _():
                    act_copy(g - 2).wait()

                spot = g % 2

                def one(member):
                    slot = g * team + member
                    for part in range(2):
                        lanes = slice(part * LANE, (part + 1) * LANE)
                        mean_here, rstd = norm[0:1, lanes], norm[1:2, lanes]
                        scale, shift = gain_ref[2 * b + part], bias_ref[2 * b + part]
                        for turn in range(2):
                            live = place_row < cnt_ref[slot] - turn * half_slot
                            here = pl.ds(
                                pl.multiple_of(member * SLOT + turn * half_slot, half_slot),
                                half_slot,
                            )
                            value = big[
                                part, pl.ds(off_ref[slot] + turn * half_slot, half_slot), :
                            ]
                            value = jnp.where(live, value, 0.0)
                            normed = (value - mean_here) * rstd
                            z = scale * normed + shift
                            square = z * z
                            bent = jnp.tanh(z * (slope + (slope * cubic) * square))
                            half = 0.5 + 0.5 * bent
                            abuf[spot, here, lanes] = jnp.where(live, z * half, 0.0)
                            back = half + z * (1.0 - bent * bent) * (
                                0.5 * slope + (1.5 * slope * cubic) * square
                            )
                            grad = jnp.where(live, cbuf[spot, here, lanes].astype(f32) * back, 0.0)
                            into = pl.ds(
                                pl.multiple_of((slot + 1) * SLOT + turn * half_slot, half_slot),
                                half_slot,
                            )
                            big[2 + part, into, :] = grad
                            tall = (half_slot // 8, 8, LANE)
                            sums[0, :, lanes] += jnp.sum((grad * normed).reshape(tall), 0)
                            sums[1, :, lanes] += jnp.sum(grad.reshape(tall), 0)

                loop(0, team, one)
                act_copy(g).start()

            loop(0, groups, act_group)
            sbuf[2 * b + 1] = jnp.zeros((8, wide), f32)
            sbuf[2 * b + 1, 0:1, :] = jnp.sum(sums[0], 0, keepdims=True)
            sbuf[2 * b + 1, 1:2, :] = jnp.sum(sums[1], 0, keepdims=True)
            exchange_block(2 * b + 1)
            by_gain, by_bias = (row_of(2 * b + 1, line) for line in (0, 1))
            by_gain = sum(by_gain[1:], by_gain[0])
            by_bias = sum(by_bias[1:], by_bias[0])
            fullest = numbers[0]
            for number in numbers[1:]:
                fullest = jnp.maximum(fullest, number)
            tot_ref[2:3, columns] = fullest
            tot_ref[0:1, columns] = by_gain
            tot_ref[1:2, columns] = by_bias
            norm[2:3, :] = by_gain / count
            norm[3:4, :] = by_bias / count
            act_copy(groups - 2).wait()
            act_copy(groups - 1).wait()

            def grad_tile(t):
                for step in range(3):
                    block = t * 3 + step
                    pick = picked_rows(block)
                    here = pl.ds(pl.multiple_of(block * SLOT, SLOT), SLOT)
                    live = lax.broadcasted_iota(i32, (SLOT, LANE), 0) < total - block * SLOT
                    for part in range(2):
                        lanes = slice(part * LANE, (part + 1) * LANE)
                        rstd = norm[1:2, lanes]
                        normed = (big[part, here, :] - norm[0:1, lanes]) * rstd
                        value = (rstd * gain_ref[2 * b + part]) * (
                            pick(2 + part) - norm[3:4, lanes] - normed * norm[2:3, lanes]
                        )
                        stage[2 * b + part, here, :] = jnp.where(live, value, 0.0).astype(bf16)
                give_grad(b, at(t)).start()
                send_grad(b, part_number[0], at(t)).start()

            send_partial(b, 0, every).wait_send()
            for part, (low, high) in enumerate(ranges):
                part_number = [part]
                loop(low, high, grad_tile)
            if b == 1:
                loop(0, early, lambda t: send_grad(2, t, at(t)).start())

        def weight_part(source, qs, low, high, fresh):
            some = pl.ds(low * tile, (high - low) * tile)
            left = jnp.concatenate([source[q, some, :] for q in qs], 1)
            width = LANE * len(qs)
            for number, half in enumerate((own, sib)):
                into = slice(number * fw, (number + 1) * fw)
                value = dot(left, half[some, :], 0, 0)
                if fresh:
                    wacc[:width, into] = value
                else:
                    wacc[:width, into] += value

        def share_of(p, kind):
            return (stg_a, rs_a, ag_a, kind) if p == 0 else (stg_b, rs_b, ag_b, 2 * p - 2 + kind)

        def store_shares(p, kind, line):
            stg, _, _, k = share_of(p, kind)
            width = sizes[p] * LANE
            per = fw // LANE
            for number in range(2):
                base = (side if number == 0 else 1 - side) * per
                for step in range(per):
                    lanes = slice(number * fw + step * LANE, number * fw + (step + 1) * LANE)
                    stg[k, base + step] = wacc[line : line + width, lanes].astype(bf16)

        def crosses(p, kind):
            return kind == 1 and p == 2

        def scatter(p, kind):
            stg, rs, _, k = share_of(p, kind)
            index = 2 * p + kind
            return [
                remote(
                    stg.at[k, (me + step) % nodes],
                    rs.at[k, step],
                    r_s.at[index],
                    r_r.at[index],
                    across_id(step) if crosses(p, kind) else node_id(step),
                )
                for step in range(0 if crosses(p, kind) else 1, nodes)
            ]

        def scattered(p, kind):
            _, rs, _, k = share_of(p, kind)
            first = 0 if crosses(p, kind) else 1
            shares = rs.at[k, pl.ds(first, nodes - first)]
            index = 2 * p + kind
            return remote(shares, shares, r_s.at[index], r_r.at[index], peer_id)

        def begin(copies):
            for copy in copies:
                copy.start()

        def finish(copies):
            for copy in copies:
                copy.wait()

        def hop(p):
            _, _, ag, k = share_of(p, 1)
            return remote(hop_b if p else hop_a, ag.at[k], h_s.at[p], h_r.at[p], peer_id)

        def spread_share(p, kind):
            _, _, ag, k = share_of(p, kind)
            src = ag.at[k]
            index = 2 * p + kind
            which = chip if kind == 0 else 1 - chip
            dst = wag_hbm.at[me, which, :, pl.ds(firsts[p] * LANE, sizes[p] * LANE)]
            copies = [
                remote(src, dst, a_s.at[index], a_r.at[index], node_id(step))
                for step in range(1, nodes)
            ]
            return copies, pltpu.make_async_copy(src, dst, lsem.at[2 * p + kind])

        def begin_spread(p, kind):
            copies, here = spread_share(p, kind)
            begin(copies)
            here.start()

        def finish_spread(p, kind):
            _, here = spread_share(p, kind)
            index = 2 * p + kind
            shares = wag_hbm.at[
                pl.ds(0, nodes - 1), 0, :, pl.ds(firsts[p] * LANE, sizes[p] * LANE)
            ]
            remote(shares, shares, a_s.at[index], a_r.at[index], node_id(1)).wait()
            here.wait()

        def sum_shares(p, kind):
            scattered(p, kind).wait()
            stg, rs, ag, k = share_of(p, kind)
            value = (rs[k, 0] if crosses(p, kind) else stg[k, me]).astype(f32)
            for step in range(1, nodes):
                value += rs[k, step].astype(f32)
            value = jnp.transpose(value).astype(bf16)
            if kind == 1 and not crosses(p, kind):
                (hop_b if p else hop_a)[...] = value
                hop(p).start()
            else:
                ag[k] = value
                begin_spread(p, kind)

        def end_hop(p):
            hop(p).wait()
            begin_spread(p, 1)

        def product(p, t, fresh):
            qs = range(firsts[p], firsts[p] + sizes[p])
            columns = slice(firsts[p] * LANE, (firsts[p] + sizes[p]) * LANE)
            left = jnp.concatenate([ref[q, at(t), :] for ref in (stage, glp, gls, recv) for q in qs], 1)
            right = jnp.concatenate(
                [
                    own_half(wc_ref, columns),
                    own_half(wp_ref, columns),
                    ws_ref[:fw, columns],
                    ws_ref[fw:, columns],
                ],
                1,
            )
            value = dot(left, right, 1, 1)
            for q in range(quarter):
                piece = value[:, q * LANE : (q + 1) * LANE]
                if fresh:
                    big[q, at(t), :] = piece
                else:
                    big[q, at(t), :] += piece

        norm_block(0)
        send_weights(0).wait()
        send_weights(1).wait()
        for low, high in ranges:
            weight_part(stage, (0, 1), low, high, low == 0)
        store_shares(0, 0, 0)
        begin(scatter(0, 0))
        sum_shares(0, 0)
        norm_block(1)
        for low, high in ranges:
            weight_part(stage, (2, 3), low, high, low == 0)
        store_shares(1, 0, 0)
        store_shares(2, 0, LANE)
        begin(scatter(1, 0))
        begin(scatter(2, 0))
        pl.semaphore_wait(credit, 1)

        def pass_range(p, part, low, high):
            send_grad(p, part, span(low, high)).wait_recv()
            forward_grad(p, 0, span(low, high)).start()

        for part, (low, high) in enumerate(ranges):
            pass_range(0, part, low, high)
            weight_part(glp, (0, 1), low, high, low == 0)
        store_shares(0, 1, 0)
        begin(scatter(0, 1))
        sum_shares(1, 0)
        sum_shares(2, 0)

        for b in range(2):
            give_grad(b, every).wait_recv()
        forward_grad(0, 0, every).wait_recv()
        loop(0, turns, lambda t: product(0, t, True))
        sum_shares(0, 1)
        loop(early, turns, lambda t: send_grad(2, t, at(t)).start())
        for part, (low, high) in enumerate(ranges):
            pass_range(1, part, low, high)
            weight_part(glp, (2,), low, high, low == 0)
        store_shares(1, 1, 0)
        begin(scatter(1, 1))
        forward_grad(1, 0, every).wait_recv()
        loop(0, turns, lambda t: product(1, t, False))
        end_hop(0)

        def link_copy(g):
            return pltpu.make_async_copy(
                tile_hbm.at[pl.ds(g * team, team), pl.ds(SLOT, 2 * SLOT)],
                tbuf.at[g % 3, :, pl.ds(SLOT, 2 * SLOT)],
                tsem.at[g % 3],
            )

        def slot_copy(g):
            return pltpu.make_async_copy(
                gbuf.at[g % 2],
                slot_hbm.at[pl.ds(pl.multiple_of(g * team * SLOT, SLOT), team * SLOT)],
                gsem.at[g % 2],
            )

        link_copy(0).start()
        link_copy(1).start()
        link_total[...] = jnp.zeros_like(link_total)
        place_row = lax.broadcasted_iota(i32, (SLOT, LANE), 0)

        def slot_group(g):
            @pl.when(g + 2 < groups)
            def _():
                link_copy(g + 2).start()

            link_copy(g).wait()

            @pl.when(g >= 2)
            def _():
                slot_copy(g - 2).wait()

            for member in range(team):
                slot = g * team + member
                live = place_row < cnt_ref[slot]
                scale = column_of(inv_ref, slot)
                for q in range(quarter):
                    value = big[q, pl.ds(off_ref[slot], SLOT), :].astype(bf16).astype(f32)
                    gbuf[g % 2, member * SLOT : (member + 1) * SLOT, q * LANE : (q + 1) * LANE] = (
                        jnp.where(live, value * scale, 0.0).astype(bf16)
                    )
            link = jnp.concatenate([tbuf[g % 3, member, SLOT:, :] for member in range(team)], 1)
            link_total[...] += dot(link, gbuf[g % 2])
            slot_copy(g).start()

        def slots_done(t):
            return (3 * t) // 4

        def last_turn(t):
            @pl.when(t >= 1)
            def _():
                forward_grad(2, t - 1, at(t - 1)).wait_recv()
                product(2, t - 1, False)
                loop(slots_done(t - 1), slots_done(t), slot_group)

            send_grad(2, t, at(t)).wait_recv()
            forward_grad(2, t, at(t)).start()

        for low, high in ranges:
            loop(low, high, last_turn)
            weight_part(glp, (3,), low, high, low == 0)
            if low == 5:
                sum_shares(1, 1)
        store_shares(2, 1, 0)
        begin(scatter(2, 1))
        end_hop(1)
        forward_grad(2, turns - 1, at(turns - 1)).wait_recv()
        product(2, turns - 1, False)
        loop(slots_done(turns - 1), groups, slot_group)
        hbuf[...] = link_total[...].astype(bf16)
        half = hbuf.shape[0] // 2
        returns = [
            remote(hbuf.at[:half], hback.at[:half], b_s.at[0], b_r.at[0], node_id(nodes - 1)),
            remote(hbuf.at[half:], hback.at[half:], b_s.at[1], b_r.at[1], node_id(1)),
        ]
        begin(returns)
        sum_shares(2, 1)
        slot_copy(groups - 2).wait()
        slot_copy(groups - 1).wait()
        finish(returns)
        back_ref[:half, :] = jnp.where(me == nodes - 1, 0.0, hback[:half, :].astype(f32)).astype(bf16)
        back_ref[half:, :] = jnp.where(me == 0, 0.0, hback[half:, :].astype(f32)).astype(bf16)

        send_own(0, every).wait_send()
        for b in range(2):
            give_grad(b, every).wait_send()
        for p in range(3):
            send_grad(p, 0, every).wait_send()
            forward_grad(p, 0, every).wait_send()
        for p in range(3):
            for kind in range(2):
                finish_spread(p, kind)

    anywhere = pl.BlockSpec(memory_space=pl.ANY)
    dma = pltpu.SemaphoreType.DMA
    lane_rows = (quarter, compact, LANE)
    outs = [
        jax.ShapeDtypeStruct((rows, fw), f32),
        jax.ShapeDtypeStruct((rows, fw), bf16),
        jax.ShapeDtypeStruct((2 * SLOT, fw), bf16),
        jax.ShapeDtypeStruct((nodes, 2, LANE, fw), bf16),
        jax.ShapeDtypeStruct((8, fw), f32),
        jax.ShapeDtypeStruct((slots, 3 * SLOT, SLOT), bf16),
    ]
    scratch = [
        pltpu.VMEM((compact, fw), bf16),
        pltpu.VMEM((compact, fw), bf16),
        pltpu.VMEM(lane_rows, bf16),
        pltpu.VMEM(lane_rows, bf16),
        pltpu.VMEM(lane_rows, bf16),
        pltpu.VMEM(lane_rows, bf16),
        pltpu.VMEM((quarter, padded, LANE), f32),
        pltpu.VMEM((wide, 2 * fw), f32),
        pltpu.VMEM((2, nodes, wide, LANE), bf16),
        pltpu.VMEM((4, nodes, LANE, LANE), bf16),
        pltpu.VMEM((2, nodes, wide, LANE), bf16),
        pltpu.VMEM((4, nodes, LANE, LANE), bf16),
        pltpu.VMEM((2, LANE, wide), bf16),
        pltpu.VMEM((4, LANE, LANE), bf16),
        pltpu.VMEM((LANE, wide), bf16),
        pltpu.VMEM((LANE, LANE), bf16),
        pltpu.VMEM((3, team * SLOT, fw), bf16),
        pltpu.VMEM((3, team, 3 * SLOT, SLOT), bf16),
        pltpu.VMEM((2, team * SLOT, wide), bf16),
        pltpu.VMEM((2, team * SLOT, wide), f32),
        pltpu.VMEM((2, team * SLOT, fw), bf16),
        pltpu.VMEM((4, 8, wide), f32),
        pltpu.VMEM((4, nodes, 8, wide), f32),
        pltpu.VMEM((8, wide), f32),
        pltpu.VMEM((2, 8, wide), f32),
        pltpu.VMEM((8, wide), f32),
        pltpu.VMEM((2 * SLOT, fw), f32),
        pltpu.VMEM((2 * SLOT, fw), bf16),
        pltpu.VMEM((2 * SLOT, fw), bf16),
        dma((3,)),
        dma((3,)),
        dma((2,)),
        dma((2,)),
        dma((2,)),
        dma((1,)),
        dma((turns,)),
        dma((2,)),
        dma((6,)),
        dma((3,)),
        dma((6 + turns,)),
        dma((2,)),
        dma((2,)),
        dma((3,)),
        dma((2 + turns,)),
        dma((4,)),
        dma((4,)),
        dma((6,)),
        dma((6,)),
        dma((6,)),
        dma((6,)),
        dma((4,)),
        dma((4,)),
        dma((6,)),
        pltpu.SemaphoreType.REGULAR,
        pltpu.VMEM((2 * fw, fw), bf16),
        dma((2,)),
        dma((2,)),
        pltpu.VMEM((2 * fw, fw), bf16),
        pltpu.VMEM((2 * fw, fw), bf16),
        dma((2 * quarter,)),
        dma((3,)),
        dma((3,)),
        pltpu.VMEM((2 * SLOT, fw), bf16),
        pltpu.VMEM((slots, 8, SLOT), f32),
        dma((2,)),
        dma((2,)),
        dma((2,)),
        dma((2,)),
    ]
    return pl.pallas_call(
        kernel,
        out_shape=outs,
        in_specs=[smem()] * 3 + [anywhere] * 3 + [whole()] * 5,
        out_specs=[anywhere, anywhere, whole(), anywhere, whole(), anywhere],
        scratch_shapes=scratch,
        compiler_params=pltpu.CompilerParams(
            vmem_limit_bytes=CORE_BYTES, collective_id=2, has_side_effects=True
        ),
        cost_estimate=cost(0, 0),
        name="core",
    )(*lists, features, weight, cotangent, near, links, send_pairs, gain, bias)


def every_row(
    features, weight, cotangent, near, links, send_pairs, valid_rows, scale, shift, lists, nodes, chips
):
    offsets, counts = lists[:2]
    rows, fw = features.shape
    slots = rows // SLOT
    chip, core_side = lax.axis_index("mp") // 2, lax.rem(lax.axis_index("mp"), 2)
    core_word = core_side.astype(i32)[None]
    half = send_pairs.shape[1]
    send_list = jnp.concatenate([send_pairs[1], send_pairs[0]], 0)
    valid_row = valid_rows[None, :].astype(i32)
    others = range(1, chips)
    wide = fw // 2

    def chip_rows(which):
        return lax.dynamic_slice_in_dim(weight, which * 2 * fw, 2 * fw, 0).astype(bf16)

    w_peer = [to_chip(chip_rows(lax.rem(chip + d, chips)), d) for d in others]
    w_chip = chip_rows(chip)
    picked = pick_rows(features, send_list[:, None], valid_row)
    halo = jnp.concatenate([node_shift(picked[:half], 1), node_shift(picked[half:], -1)], 0)
    tiles, inv = count_tiles(near, links, counts)

    def half_of(block, which):
        return lax.dynamic_slice_in_dim(block, which * fw, fw, 0)

    w_all = [w_chip] + w_peer
    got = to_sibling(jnp.concatenate([half_of(w, 1 - core_side) for w in w_all], 0))
    wb = [half_of(w, core_side) for w in w_all] + [got[i * fw : (i + 1) * fw] for i in range(chips)]
    own = aggregate(tiles, inv, features, halo, offsets, counts, 0, rows)
    sib = to_sibling(own)
    received = []
    for b in range(2):
        parts = [partial_product(own, sib, w, core_word, b, wide) for w in w_peer]
        received.append([to_chip(p, -d) for p, d in zip(parts, others, strict=True)])
    gain, bias = scale[None, :], shift[None, :]
    act, grads, totals, weight_grads = None, [], [], []
    for b in range(2):
        lin, stat = linear_stats(
            own, sib, w_chip, core_word, received[b], offsets, slots, b, wide
        )
        stats = exchange(stat, nodes)
        act, grad_pre, sums = activate(
            lin, stats, gain, bias, cotangent, offsets, counts, act, b, wide, rows, fw
        )
        sums = exchange(sums, nodes)
        grad_lin, summed = linear_grad(
            lin, grad_pre, stats, sums, gain, offsets, slots, b, wide, 1
        )
        totals.append(summed)
        mine = [grad_lin] + [to_chip(grad_lin, d) for d in others]
        grads.append(mine + [to_sibling(g) for g in mine])
        sets = []
        for g in mine:
            left = jnp.einsum("rf,rc->fc", own, g, preferred_element_type=f32)
            right = jnp.einsum("rf,rc->fc", sib, g, preferred_element_type=f32)
            sets.append(
                jnp.concatenate(
                    [
                        jnp.where(core_side == 1, right, left),
                        jnp.where(core_side == 1, left, right),
                    ],
                    0,
                )
            )
        share = scatter_sum(jnp.stack(sets), 1)
        shares = [share[0]] + [to_chip(share[d], -d) for d in others]
        full = gather_shares(jnp.stack(shares), 1)
        placed = jnp.zeros((chips,) + full.shape[1:], f32)
        for d in range(chips):
            placed = lax.dynamic_update_slice(
                placed, full[d : d + 1], (lax.rem(chip + d, chips), 0, 0)
            )
        weight_grads.append(placed.reshape(chips * 2 * fw, wide))
    grad_agg = grad_products(grads[0], wb, [0] * len(wb))
    slot_grad, halo_grad = slot_grads(grad_agg, grads[1], wb, wide, tiles, inv, offsets, counts)
    returned = jnp.concatenate(
        [node_shift(halo_grad[:half], -1), node_shift(halo_grad[half:], 1)], 0
    )
    input_grad = input_grads(slot_grad, tiles, returned, send_list[None, :], counts)
    totals = jnp.concatenate(totals, 1)
    return act, input_grad, jnp.concatenate(weight_grads, 1), totals[0], totals[1]


def local(features, weight, scale, shift, cotangent, neighbours, halo_links, valid_rows, send_rows):
    rows, fw = features.shape
    slots = rows // SLOT
    nodes, mp = lax.axis_size("node"), lax.axis_size("mp")
    chips = mp // 2

    counts = jnp.sum(valid_rows.reshape(slots, SLOT), 1).astype(i32)
    order = jnp.arange(slots + 1, dtype=i32)
    offsets = jnp.sum(jnp.where(order[None, :slots] < order[:, None], counts[None, :], 0), 1)
    compact = rows * 13 // 16 // (3 * SLOT) * (3 * SLOT)
    blocks = jnp.arange(compact // SLOT, dtype=i32) * SLOT
    first = jnp.minimum(
        jnp.sum((offsets[None, 1:] <= blocks[:, None]).astype(i32), 1), slots - 1
    ).astype(i32)
    lists = (offsets, counts, first)
    near, links = neighbours.T, halo_links.T
    send_pairs = send_rows.T

    def all_rows(*args):
        return every_row(*args, lists, nodes, chips)

    given = (features, weight, cotangent, near, links, send_pairs, valid_rows, scale, shift)
    if not (chips == 2 and fw == 4 * LANE and 2 * fw == nodes * LANE and slots % nodes == 0):
        return all_rows(*given)
    *made, totals, tiles = core(
        features, weight, cotangent, near, links, send_pairs, scale, shift, lists, nodes, compact
    )

    def few_rows(*args):
        act, input_grad, weight_grad = last_pass(*made, tiles, send_pairs, counts)
        return act, input_grad, weight_grad.reshape(mp * fw, fw), totals[0], totals[1]

    return lax.cond(totals[2, 0] <= compact, few_rows, all_rows, *given)


def solution(mesh):
    in_specs = (
        P("node", "mp"),
        P(None, "mp"),
        P("mp"),
        P("mp"),
        P("node", "mp"),
        P("node", None),
        P("node", None),
        P("node"),
        P("node", None),
    )
    out_specs = (P("node", "mp"), P("node", "mp"), P(None, "mp"), P("mp"), P("mp"))
    return jax.shard_map(local, mesh=mesh, in_specs=in_specs, out_specs=out_specs, check_vma=False)
```
